32 devices in a mesh: fsdp: 8 (over y, x, core), tp: 4 (over z).
Axes of the slice: x: 2, y: 2, z: 4, core: 2. Of those that a mesh axis runs over, the one named last changes fastest.
Arguments:
- tokens: bfloat16 [16, 1024, 1024], P('fsdp', 'tp'), may hold values from -6 to 6
- lengths: int32 [16], replicated, may hold values from 1 to 1024, 10240 in all
- perm: int32 [16], replicated, may hold values from 0 to 15, as said below
- cotangent: bfloat16 [16, 1024, 1024], P('fsdp', 'tp'), may hold values from -6 to 6
- norm1_gain: float32 [1024], replicated, may hold values from 0.5 to 1.5
- input_weight: bfloat16 [1024, 8, 771], P('fsdp', 'tp'), may hold values from -0.1875 to 0.1875
- conv_w: float32 [8, 640, 4], replicated, may hold values from -3 to 3
- decay_log: float32 [8], replicated, may hold values from -7 to -2
- decay_bias: float32 [8], replicated, may hold values from -1 to 1
- out_gain: float32 [128], replicated, may hold values from 0.5 to 1.5
- w_out: bfloat16 [1024, 1024], P('tp', 'fsdp'), may hold values from -0.1875 to 0.1875
- norm2_gain: float32 [1024], replicated, may hold values from 0.5 to 1.5
- gate_up_weight: bfloat16 [1024, 2, 2816], P('fsdp', None, 'tp'), may hold values from -0.1875 to 0.1875
- down_weight: bfloat16 [2816, 1024], P('tp', 'fsdp'), may hold values from -0.109375 to 0.109375
Outputs:
- output: bfloat16 [16, 1024, 1024], P('fsdp', 'tp')
- input_grad: bfloat16 [16, 1024, 1024], P('fsdp', 'tp')
- grad_norm1_gain: float32 [1024], replicated
- grad_w_in: float32 [1024, 8, 771], P('fsdp', 'tp')
- grad_conv_w: float32 [8, 640, 4], replicated
- grad_decay_log: float32 [8], replicated
- grad_decay_bias: float32 [8], replicated
- grad_out_gain: float32 [128], replicated
- grad_w_out: float32 [1024, 1024], P('tp', 'fsdp')
- grad_norm2_gain: float32 [1024], replicated
- grad_w_gate_up: float32 [1024, 2, 2816], P('fsdp', None, 'tp')
- grad_w_down: float32 [2816, 1024], P('tp', 'fsdp')
The draws below stay inside these ranges and needn't reach their ends.
Inputs may be any that keep to these rules, and one draw needn't show every extreme that they name: lengths[i] is the number of live tokens of sequence i; one sequence has exactly 1024. perm is a permutation; slot d belongs to index d // 2 of fsdp. The sequences of one index of fsdp (given order) go to 2 different indices, and each index receives at most one sequence from each index.
All inputs are finite; a program needn't handle non-finite values.
Results may differ from the reference program's by a relative error of at most 0.03.
Values may be sent and summed in bfloat16 or wider, within the bound.
No kernel may reach another device: no remote copies, remote signals or barrier semaphores. Data moves between devices by JAX's collectives and lax.ppermute only.
A program may use at most 320 MiB of HBM per device.

```python
import math
import jax
import jax.numpy as jnp
import numpy as np
from jax import lax

D = 1024
H = 8
HEAD_DIM = 128
NH = 2
CONV = 4
FF = 2816
SPAN = 64
LMAX = 1024
SPG = 2
SEQS = 16
TOTAL_LEN = 10240
CONV_CH = 640
E_COLS = 771
N_TP = 4


def draw_perm(key, part):
    group_count = SEQS // SPG
    offset_key = jax.random.fold_in(key, 11)
    local_key = jax.random.fold_in(key, 23)
    offsets = jax.random.permutation(offset_key, group_count)[:SPG].astype(jnp.int32)
    local_keys = jax.random.split(local_key, group_count)
    local_order = jax.vmap(lambda single_key: jax.random.permutation(single_key, SPG))(local_keys).astype(jnp.int32)
    dest_ids = jnp.arange(group_count, dtype=jnp.int32)
    source_group = (dest_ids[:, None] + offsets[None, :]) % group_count
    slot_ids = jnp.arange(SPG, dtype=jnp.int32)
    source_local = local_order[source_group, slot_ids[None, :]]
    return (source_group * SPG + source_local).reshape(SEQS).astype(jnp.int32)


def level_of(key, shape, cuts, least, top_value):
    level = 1.0
    for dim, parts in cuts:
        draws = jax.random.uniform(jax.random.fold_in(jax.random.fold_in(key, 6), dim), (parts,), jnp.float32, least / len(cuts), top_value / len(cuts))
        level = level * jnp.repeat(jnp.exp(draws), shape[dim] // parts).reshape((-1,) + (1,) * (len(shape) - 1 - dim))
    return level


def split_up(number_of, total, reach, lean):
    weights = [(1 << 20) // math.isqrt(standing ** lean) + 1 for standing in range(2, number_of + 1)]
    surplus, holding = total - reach - (number_of - 1), [1] * (number_of - 1)
    while surplus > 0:
        movable = [i for i in range(number_of - 1) if holding[i] < reach]
        pool, left = sum([weights[i] for i in movable]), surplus
        for i in movable:
            addition = min(reach - holding[i], max(1, left * weights[i] // pool), surplus)
            holding[i] = holding[i] + addition
            surplus = surplus - addition
    return np.array([reach] + holding)


def uneven(stream_key, amount, total, bound, slope):
    if amount == 2:
        one = jax.random.randint(stream_key, (), max(1, total - bound), min(bound, total - 1) + 1)
        return jnp.stack([one, total - one])
    tallies = jnp.asarray(split_up(amount, total, bound, slope), jnp.int32)
    pairs = (amount - 1) // 2
    donor, receiver = tallies[1:1 + 2 * pairs:2], tallies[2:2 + 2 * pairs:2]
    room = jnp.minimum(donor - 1, bound - receiver)
    moved = jax.random.randint(jax.random.fold_in(stream_key, 1), (pairs,), 0, 1 << 20) % (room + 1)
    tallies = tallies.at[1:1 + 2 * pairs:2].set(donor - moved).at[2:2 + 2 * pairs:2].set(receiver + moved)
    return tallies[jax.random.permutation(jax.random.fold_in(stream_key, 2), amount)]


def centred(stream_key, dims, spread, most, cuts=(), kind=jnp.bfloat16):
    level = level_of(stream_key, dims, cuts, -0.22, 0.18) if cuts else 1.0
    drawn = jax.random.normal(stream_key, dims, jnp.float32) * spread * level
    return jnp.minimum(jnp.maximum(drawn, -most), most).astype(kind)


def setup_inputs(seed: int = 0) -> dict:
    seeds = jax.random.split(jax.random.key(seed), 15)
    return {
        "tokens": centred(seeds[0], (SEQS, LMAX, D), 1.0, 6.0, ((0, 8), (1, 4))),
        "lengths": uneven(seeds[1], SEQS, TOTAL_LEN, LMAX, 2).astype(jnp.int32),
        "perm": draw_perm(jax.random.fold_in(seeds[14], 71), 0),
        "cotangent": centred(seeds[3], (SEQS, LMAX, D), 1.0, 6.0, ((0, 8), (1, 4))),
        "norm1_gain": jnp.clip(1.0 + 0.1 * jax.random.normal(seeds[4], (D,), jnp.float32), 0.5, 1.5),
        "input_weight": centred(seeds[5], (D, H, E_COLS), D ** -0.5, 0.1875, ((0, 8), (1, 4))),
        "conv_w": centred(seeds[6], (H, CONV_CH, CONV), CONV ** -0.5, 3.0, (), jnp.float32),
        "decay_log": jnp.clip(jax.random.uniform(seeds[7], (H,), jnp.float32, -7.0, -2.0), -7.0, -2.0),
        "decay_bias": jnp.clip(jax.random.uniform(seeds[8], (H,), jnp.float32, -1.0, 1.0), -1.0, 1.0),
        "out_gain": jnp.clip(1.0 + 0.1 * jax.random.normal(seeds[9], (HEAD_DIM,), jnp.float32), 0.5, 1.5),
        "w_out": centred(seeds[10], (H * HEAD_DIM, D), (H * HEAD_DIM) ** -0.5, 0.1875, ((0, 4), (1, 8))),
        "norm2_gain": jnp.clip(1.0 + 0.1 * jax.random.normal(seeds[11], (D,), jnp.float32), 0.5, 1.5),
        "gate_up_weight": centred(seeds[12], (D, 2, FF), D ** -0.5, 0.1875, ((0, 8), (2, 4))),
        "down_weight": centred(seeds[13], (FF, D), FF ** -0.5, 0.109375, ((0, 4), (1, 8))),
    }


EPS_NORM = 1e-05
EPS_UNIT = 1e-06
PRECISION_MAX = lax.Precision.HIGHEST

@jax.custom_vjp
def reduced_value(v):
    return lax.optimization_barrier(v.astype(jnp.bfloat16)).astype(jnp.float32)

@jax.custom_vjp
def reduced_gradient(v):
    return v

def low_keep(v):
    return (reduced_value(v), None)

def low_pass(kept, grad):
    return (grad,)

def back_keep(v):
    return (v, None)

def back_low(kept, grad):
    return (reduced_value(grad),)
reduced_value.defvjp(low_keep, low_pass)
reduced_gradient.defvjp(back_keep, back_low)

def rms_scale(value, gain):
    return value * lax.rsqrt(lax.optimization_barrier(jnp.mean(value * value, axis=-1, keepdims=True)) + EPS_NORM) * gain

def unit_norm(value):
    return value * lax.rsqrt(lax.optimization_barrier(jnp.sum(value * value, axis=-1, keepdims=True)) + EPS_UNIT)

def causal_conv(raw_values, kernel):
    kernel_len = kernel.shape[-1]
    seq_len = raw_values.shape[1]
    padded = jnp.pad(raw_values, ((0, 0), (kernel_len - 1, 0), (0, 0), (0, 0)))
    summed = jnp.zeros_like(raw_values)
    for offset in range(kernel_len):
        summed = summed + padded[:, offset:offset + seq_len] * kernel[:, :, offset]
    return summed

def carry_step(state, pieces):
    weighted_block, value_block, key_block, decay_block = pieces
    updates = value_block - jnp.einsum('shid,shdv->shiv', key_block, state, precision=PRECISION_MAX)
    carried = decay_block * state + jnp.einsum('shjd,shjv->shdv', weighted_block, updates, precision=PRECISION_MAX)
    return (carried, (state, updates))

def delta_product(queries, key_rows, values, beta_rows, log_decay):
    batch_seqs, seq_len, head_count, head_dim = queries.shape
    value_dim = values.shape[-1]
    blocks = seq_len // SPAN
    sub_decay = jnp.concatenate([log_decay[..., None], jnp.zeros_like(beta_rows[..., 1:])], axis=-1)

    def split_steps(value):
        tail_dims = value.shape[4:]
        shaped = value.reshape((batch_seqs, blocks, SPAN, head_count, NH) + tail_dims)
        axes_order = (1, 0, 3, 2, 4) + tuple(range(5, 5 + len(tail_dims)))
        return shaped.transpose(axes_order).reshape((blocks, batch_seqs, head_count, SPAN * NH) + tail_dims)
    block_queries = queries.reshape(batch_seqs, blocks, SPAN, head_count, head_dim).transpose(1, 0, 3, 2, 4)
    block_keys = split_steps(key_rows)
    block_values = split_steps(values)
    block_betas = split_steps(beta_rows)
    cumulative = jnp.cumsum(split_steps(sub_decay), axis=-1)
    steps_in = SPAN * NH
    row_ids = lax.broadcasted_iota(jnp.int32, (steps_in, steps_in), 0)
    col_ids = lax.broadcasted_iota(jnp.int32, (steps_in, steps_in), 1)
    strictly = col_ids < row_ids
    key_inner = jnp.einsum('nshid,nshjd->nshij', block_keys, block_keys, precision=PRECISION_MAX)
    spread_log = cumulative[..., :, None] - cumulative[..., None, :]
    fading = jnp.where(strictly, jnp.exp(jnp.where(strictly, spread_log, 0.0)), 0.0)
    lower_mat = key_inner * fading * block_betas[..., :, None]
    right_sides = jnp.concatenate([block_betas[..., None] * block_values, (block_betas * jnp.exp(cumulative))[..., None] * block_keys], axis=-1)
    solved = jax.scipy.linalg.solve_triangular(lower_mat, right_sides, lower=True, unit_diagonal=True)
    value_part = solved[..., :value_dim]
    key_part = solved[..., value_dim:]
    last_log = cumulative[..., -1:]
    weighted = block_keys * jnp.exp(last_log - cumulative)[..., None]
    block_decay = jnp.exp(last_log)[..., None]
    first_state = jnp.zeros((batch_seqs, head_count, head_dim, value_dim), jnp.float32)
    last_state, (entering, updates) = lax.scan(carry_step, first_state, (weighted, value_part, key_part, block_decay))
    read_log = cumulative[..., NH - 1::NH]
    out_rows = lax.broadcasted_iota(jnp.int32, (SPAN, steps_in), 0)
    out_cols = lax.broadcasted_iota(jnp.int32, (SPAN, steps_in), 1)
    visible = out_cols <= out_rows * NH + NH - 1
    query_key = jnp.einsum('nshid,nshjd->nshij', block_queries, block_keys, precision=PRECISION_MAX)
    read_spread = read_log[..., :, None] - cumulative[..., None, :]
    read_fade = jnp.where(visible, jnp.exp(jnp.where(visible, read_spread, 0.0)), 0.0)
    from_state = jnp.einsum('nshid,nshdv->nshiv', block_queries, entering, precision=PRECISION_MAX)
    outputs = jnp.exp(read_log)[..., None] * from_state + jnp.einsum('nshij,nshjv->nshiv', query_key * read_fade, updates, precision=PRECISION_MAX)
    return outputs.transpose(1, 0, 3, 2, 4).reshape(batch_seqs, seq_len, head_count, value_dim)

def mixer(normalized_rows, input_weight, w_out, conv_w, decay_log, decay_bias, out_gain):
    batch_seqs, seq_len, model_dim = normalized_rows.shape
    head_count = input_weight.shape[1]
    conv_ch = conv_w.shape[1]
    heads_per_group = head_count // N_TP
    segment_list = []
    for head_group in range(N_TP):
        segment_list.append(jnp.einsum('mzk,kin->mzin', reduced_gradient(normalized_rows), input_weight[:, head_group * heads_per_group:(head_group + 1) * heads_per_group], precision=PRECISION_MAX))
    projected_rows = jnp.concatenate(segment_list, axis=2)
    conv_out = jax.nn.silu(causal_conv(projected_rows[..., :conv_ch], conv_w))
    queries = unit_norm(conv_out[..., :HEAD_DIM])
    key_rows = unit_norm(conv_out[..., HEAD_DIM:HEAD_DIM * (1 + NH)].reshape(batch_seqs, seq_len, head_count, NH, HEAD_DIM))
    values = conv_out[..., HEAD_DIM * (1 + NH):].reshape(batch_seqs, seq_len, head_count, NH, HEAD_DIM)
    out_gate = projected_rows[..., conv_ch:conv_ch + HEAD_DIM]
    beta_rows = jax.nn.sigmoid(projected_rows[..., conv_ch + HEAD_DIM:conv_ch + HEAD_DIM + NH])
    log_decay = -jnp.exp(decay_log) * jax.nn.softplus(projected_rows[..., conv_ch + HEAD_DIM + NH] + decay_bias)
    result = delta_product(queries, key_rows, values, beta_rows, log_decay)
    gated_result = reduced_value(rms_scale(result, out_gain) * jax.nn.silu(out_gate))
    output_matrix = w_out.reshape(head_count, HEAD_DIM, model_dim)
    grand_total = jnp.zeros((batch_seqs, seq_len, model_dim), jnp.float32)
    for head_group in range(N_TP):
        partial_total = jnp.einsum('gtpo,poz->gtz', gated_result[:, :, head_group * heads_per_group:(head_group + 1) * heads_per_group], output_matrix[head_group * heads_per_group:(head_group + 1) * heads_per_group], precision=PRECISION_MAX)
        grand_total = grand_total + reduced_value(partial_total)
    return grand_total

def feed_forward(normalized_rows, gate_up_weight, down_weight):
    group_units = down_weight.shape[0] // N_TP
    grand_total = jnp.zeros(normalized_rows.shape, jnp.float32)
    for head_group in range(N_TP):
        unit_count = slice(head_group * group_units, (head_group + 1) * group_units)
        gate_up_result = jnp.einsum('tux,xeg->tueg', reduced_gradient(normalized_rows), gate_up_weight[:, :, unit_count], precision=PRECISION_MAX)
        hidden_state = reduced_value(jax.nn.silu(gate_up_result[..., 0, :]) * gate_up_result[..., 1, :])
        grand_total = grand_total + reduced_value(jnp.einsum('wqh,hv->wqv', hidden_state, down_weight[unit_count], precision=PRECISION_MAX))
    return grand_total

def block(tokens, norm1_gain, input_weight, conv_w, decay_log, decay_bias, out_gain, w_out, norm2_gain, gate_up_weight, down_weight, live_mask):
    normalized_rows = reduced_value(rms_scale(tokens, norm1_gain))
    middle = tokens + reduced_gradient(mixer(normalized_rows, input_weight, w_out, conv_w, decay_log, decay_bias, out_gain))
    normed_two = reduced_value(rms_scale(middle, norm2_gain))
    return live_mask * (middle + reduced_gradient(feed_forward(normed_two, gate_up_weight, down_weight)))

def reference(tokens, lengths, perm, cotangent, norm1_gain, input_weight, conv_w, decay_log, decay_bias, out_gain, w_out, norm2_gain, gate_up_weight, down_weight):
    weights = (norm1_gain, input_weight.astype(jnp.float32), conv_w, decay_log, decay_bias, out_gain, w_out.astype(jnp.float32), norm2_gain, gate_up_weight.astype(jnp.float32), down_weight.astype(jnp.float32))
    given_cot = jnp.zeros_like(cotangent).at[perm].set(cotangent)
    positions = jnp.arange(LMAX, dtype=jnp.int32)
    live_mask = (positions[None, :] < lengths[:, None]).astype(jnp.float32)[..., None]
    batch_size = math.gcd(SEQS, max(1, 4096 // LMAX))
    batches = SEQS // batch_size
    tok_batches = tokens.reshape(batches, batch_size, LMAX, D)
    cot_batches = given_cot.reshape(batches, batch_size, LMAX, D)
    mask_batches = live_mask.reshape(batches, batch_size, LMAX, 1)

    def one_batch(totals, segment_list):
        tok_piece, cot_piece, mask_piece = segment_list

        def forward(tok_in, *weight_list):
            return block(tok_in, *weight_list, mask_piece)
        block_out, pullback = jax.vjp(forward, tok_piece.astype(jnp.float32), *weights)
        gradients = pullback(cot_piece.astype(jnp.float32))
        new_totals = tuple((grand_total + grad_part for grand_total, grad_part in zip(totals, gradients[1:])))
        return (new_totals, (block_out.astype(jnp.bfloat16), gradients[0].astype(jnp.bfloat16)))
    initial = tuple((jnp.zeros_like(weight) for weight in weights))
    totals, (outputs, input_grads) = lax.scan(one_batch, initial, (tok_batches, cot_batches, mask_batches))
    return (outputs.reshape(SEQS, LMAX, D), input_grads.reshape(SEQS, LMAX, D), totals[0], totals[1], totals[2], totals[3], totals[4], totals[5], totals[6], totals[7], totals[8], totals[9])
```

```python
import functools

import jax
import jax.numpy as jnp
from jax import lax
from jax.experimental import pallas as pl
from jax.experimental.pallas import tpu as pltpu
from jax.sharding import PartitionSpec as P

HD = 128
NH = 2
SPAN = 64
SUB = SPAN * NH
TAPS = 4
SMALL = 16
UNITS = 6 * HD + SMALL
EPS_NORM = 1e-05
EPS_UNIT = 1e-06
F32 = jnp.float32
BF16 = jnp.bfloat16
FAR = -1e30
VMEM_BYTES = 56 * 1024 * 1024
EXACT = lax.Precision.HIGHEST


def params(**kw):
    return pltpu.CompilerParams(vmem_limit_bytes=VMEM_BYTES, **kw)


def cost(flops, nbytes, trans=0):
    return pl.CostEstimate(flops=int(flops), bytes_accessed=int(nbytes), transcendentals=int(trans))


def nn(a, b):
    return lax.dot_general(a, b, (((1,), (0,)), ((), ())), preferred_element_type=F32)


def nt(a, b):
    return lax.dot_general(a, b, (((1,), (1,)), ((), ())), preferred_element_type=F32)


def tn(a, b):
    return lax.dot_general(a, b, (((0,), (0,)), ((), ())), preferred_element_type=F32)


def exact_nn(a, b):
    return lax.dot_general(a, b, (((1,), (0,)), ((), ())), precision=EXACT, preferred_element_type=F32)


def sigmoid(v):
    return 1.0 / (1.0 + jnp.exp(-v))


def sides(pieces, bit):
    return [p for p in range(pieces) if not p & bit], [p for p in range(pieces) if p & bit]


def stacks(pieces, shape):
    return [jax.ShapeDtypeStruct((pieces // 2,) + shape, BF16)] * 2


def add_kernel(count, *refs):
    ins, outs = refs[: 2 * count], refs[2 * count :]
    for i in range(count):
        for j in range(2):
            outs[2 * i + j][...] = (ins[2 * i][j].astype(F32) + ins[2 * i + 1][j].astype(F32)).astype(BF16)


def add_stacks(pairs):
    flat = [v for pair in pairs for v in pair]
    steps = 3
    blocks = [pl.BlockSpec((2, v.shape[1] // steps, v.shape[2]), lambda i: (0, i, 0)) for v in flat]
    single = [pl.BlockSpec((v.shape[1] // steps, v.shape[2]), lambda i: (i, 0)) for v in flat]
    res = pl.pallas_call(
        functools.partial(add_kernel, len(pairs)),
        out_shape=[jax.ShapeDtypeStruct(v.shape[1:], BF16) for v in flat],
        grid=(steps,),
        in_specs=blocks,
        out_specs=single,
        compiler_params=params(),
        cost_estimate=cost(1e6, 1e6),
        name="add_stacks",
    )(*flat)
    return [res[2 * i : 2 * i + 2] for i in range(len(pairs))]


def lane_sum(value):
    return jnp.sum(value, axis=-1, keepdims=True)


def conv_shifts(ref, start, rows, lanes):
    window = ref[start : start + rows + 8, lanes]
    views = [pltpu.roll(window, TAPS - 1 - j, 0)[8 : 8 + rows] for j in range(TAPS - 1)]
    return views + [window[8 : 8 + rows]]


def conv_shifts_back(ref, start, rows, lanes):
    window = ref[start : start + rows + 8, lanes]
    views = [pltpu.roll(window, rows + 8 - (TAPS - 1 - j), 0)[:rows] for j in range(TAPS - 1)]
    return views + [window[:rows]]


def iota(shape, dim):
    return lax.broadcasted_iota(jnp.int32, shape, dim)


def project_kernel(pieces, h, scal_ref, a_ref, cw_ref, *refs):
    parts = refs[:pieces]
    raw_ref, gate_ref, q_ref, k_ref, v_ref, rows_ref, raw_s, mix_s, aux_s = refs[pieces:]
    tile = a_ref.shape[0]
    depth = parts[0].shape[1]
    head = 8

    @pl.when(pl.program_id(0) == 0)
    def _():
        raw_s[0:head, :] = jnp.zeros_like(raw_s[0:head, :])

    @pl.when(pl.program_id(0) > 0)
    def _():
        raw_s[0:head, :] = raw_s[tile : tile + head, :]

    acc = jnp.zeros((tile, UNITS), F32)
    for p in range(pieces):
        acc += nt(a_ref[:, p * depth : (p + 1) * depth], parts[p][HD:])
    raw_s[head : tile + head, :] = acc[:, : 5 * HD]
    raw_ref[...] = acc[:, : 5 * HD].astype(BF16)
    gate_ref[...] = acc[:, 5 * HD : 6 * HD].astype(BF16)

    small = acc[:, 6 * HD :]
    rate, bias = scal_ref[h, 0], scal_ref[h, 1]
    arg = small[:, 2:3] + bias
    soft = jnp.maximum(arg, 0.0) + jnp.log(1.0 + jnp.exp(-jnp.abs(arg)))
    beta = sigmoid(small[:, 0:2])
    lane = iota((tile, HD), 1)
    aux_s[pl.ds(0, tile, 2), :] = jnp.where(
        lane == 0, beta[:, 0:1], jnp.where(lane == 1, -rate * soft, jnp.where(lane == 2, arg, 0.0))
    )
    aux_s[pl.ds(1, tile, 2), :] = jnp.where(lane == 0, beta[:, 1:2], 0.0)
    upper = jnp.where(iota((SUB, SUB), 0) <= iota((SUB, SUB), 1), 1.0, 0.0)
    for b in range(tile // SPAN):
        rows = jnp.transpose(aux_s[b * SUB : (b + 1) * SUB, :])[:8]
        cum = exact_nn(rows, upper)
        rows_ref[b] = jnp.where(iota((8, SUB), 0) == 3, cum[1:2], rows)

    chunk = 64
    for g in range(5):
        taps = cw_ref[0, :, g * HD : (g + 1) * HD]
        for i in range(tile // chunk):
            start = i * chunk
            views = conv_shifts(raw_s, start, chunk, slice(g * HD, (g + 1) * HD))
            pre = views[0] * taps[0:1]
            for j in range(1, TAPS):
                pre += views[j] * taps[j : j + 1]
            act = pre * sigmoid(pre)
            if g < 3:
                act = act * lax.rsqrt(lane_sum(act * act) + EPS_UNIT)
            if g == 0:
                q_ref[start : start + chunk, :] = act.astype(BF16)
            else:
                mix_s[pl.ds(2 * start + (g + 1) % 2, chunk, 2), :] = act
        if g in (2, 4):
            (k_ref if g == 2 else v_ref)[...] = mix_s[...].astype(BF16)


def project(h, normed, parts, conv_t, scal):
    seq, dim = normed.shape
    pieces = len(parts)
    tile = min(256, seq)
    fix = lambda i: (0, 0)
    along = lambda i: (i, 0)
    outs = [((seq, 5 * HD), BF16, 1), ((seq, HD), BF16, 1), ((seq, HD), BF16, 1), ((NH * seq, HD), BF16, NH), ((NH * seq, HD), BF16, NH)]
    return pl.pallas_call(
        functools.partial(project_kernel, pieces, h),
        out_shape=[jax.ShapeDtypeStruct(s, d) for s, d, _ in outs] + [jax.ShapeDtypeStruct((seq // SPAN, 8, SUB), F32)],
        grid=(seq // tile,),
        in_specs=[
            pl.BlockSpec(memory_space=pltpu.SMEM),
            pl.BlockSpec((tile, dim), along),
            pl.BlockSpec((1,) + conv_t.shape[1:], lambda i: (h, 0, 0)),
        ]
        + [pl.BlockSpec(w.shape, fix) for w in parts],
        out_specs=[pl.BlockSpec((tile * n, s[1]), along) for s, _, n in outs]
        + [pl.BlockSpec((tile // SPAN, 8, SUB), lambda i: (i, 0, 0))],
        scratch_shapes=[
            pltpu.VMEM((tile + 8, 5 * HD), F32),
            pltpu.VMEM((NH * tile, HD), F32),
            pltpu.VMEM((NH * tile, HD), F32),
        ],
        compiler_params=params(),
        cost_estimate=cost(2 * seq * dim * UNITS, 8e6),
        name="project",
    )(scal, normed, conv_t, *parts)


BASE = 16


def unit_lower_inverses(lowers):
    n, groups = SUB, SUB // BASE
    lane = iota((BASE, n), 1)
    group = lane // BASE
    packed = []
    for low in lowers:
        p = jnp.where(group == 0, low[:BASE], 0.0)
        for b in range(1, groups):
            p = jnp.where(group == b, low[b * BASE : (b + 1) * BASE], p)
        packed.append(p)
    eye = jnp.where(lane % BASE == iota((BASE, n), 0), 1.0, 0.0)
    invs = [eye] * len(lowers)
    first = group * BASE
    for j in range(BASE - 1):
        coefs = [jnp.take_along_axis(p, first + j, axis=1) for p in packed]
        invs = [x - c * x[j : j + 1] for x, c in zip(invs, coefs)]
    fulls = [
        jnp.concatenate([jnp.where(group == b, x, 0.0).astype(BF16) for b in range(groups)], axis=0) for x in invs
    ]
    row, col = iota((n, n), 0), iota((n, n), 1)
    size = BASE
    while size < n:
        odd = range(1, n // size, 2)
        mask = jnp.logical_and(row // size == col // size + 1, row // (2 * size) == col // (2 * size))
        crosses = [jnp.where(mask, low, 0.0).astype(BF16) for low in lowers]
        picks = [jnp.concatenate([f[b * size : (b + 1) * size] for b in odd], axis=0) for f in fulls]
        halves = [nn(p, c).astype(BF16) for p, c in zip(picks, crosses)]
        belows = [(p.astype(F32) - nn(h, f)).astype(BF16) for p, h, f in zip(picks, halves, fulls)]
        fulls = [
            jnp.concatenate(
                [
                    below[(b // 2) * size : (b // 2 + 1) * size] if b % 2 else f[b * size : (b + 1) * size]
                    for b in range(n // size)
                ],
                axis=0,
            )
            for f, below in zip(fulls, belows)
        ]
        size *= 2
    return fulls


def turned(value, eye):
    return nt(eye, value)


def decay_terms(rows_ref, cums, items):
    out = []
    pick_row = iota((8, SUB), 0)
    for i, (b, h) in enumerate(items):
        rows = rows_ref[h][b]
        g = rows[3:4, :]
        g_last = g[:, SUB - 1 :]
        e = jnp.exp(g)
        wide = jnp.where(pick_row == 1, e, jnp.where(pick_row == 2, jnp.exp(g_last - g), rows))
        wide = jnp.where(pick_row == 4, rows[0:1, :] * e, wide)
        cols = jnp.transpose(jnp.concatenate([wide] * (SUB // 8), axis=0))
        cums[i] = cols
        c_col = cums[i, pl.ds(1, SPAN, 2), :][:, 3:4]
        out.append((cols[:, 0:1], cols[:, 1:2], cols[:, 2:3], cols[:, 3:4], cols[:, 4:5], g, c_col, g_last))
    return out


PER_STEP = 2


def recur_kernel(heads, more, gain_ref, start_ref, *refs):
    q_r, k_r, v_r, g_r, rows_r = (refs[i * heads : (i + 1) * heads] for i in range(5))
    refs = refs[: 5 * heads] + refs[5 * heads + more :]
    z_ref, end_ref = refs[5 * heads : 5 * heads + 2]
    o_r = refs[5 * heads + 2 : 6 * heads + 2]
    u_r = refs[6 * heads + 2 : 7 * heads + 2]
    s_ref, t_ref, cums = refs[7 * heads + 2 :]

    @pl.when(pl.program_id(0) == 0)
    def _():
        end_ref[...] = start_ref[...]

    row, col = iota((SUB, SUB), 0), iota((SUB, SUB), 1)
    strict = col < row
    vis = iota((SPAN, SUB), 1) // NH <= iota((SPAN, SUB), 0)
    items = [(b, h) for b in range(PER_STEP) for h in range(heads)]
    tok = [pl.ds(b * SPAN, SPAN) for b, _ in items]
    sub = [pl.ds(b * SUB, SUB) for b, _ in items]
    eye = jnp.where(row == col, 1.0, 0.0).astype(BF16)
    terms = decay_terms(rows_r, cums, items)
    ks = [k_r[h][sub[i]] for i, (b, h) in enumerate(items)]
    qs = [q_r[h][tok[i]] for i, (b, h) in enumerate(items)]
    prods = [nt(jnp.concatenate([k, q], axis=0), k) for k, q in zip(ks, qs)]
    lowers = [
        t[0] * jnp.exp(jnp.where(strict, t[3] - t[5], FAR)) * p[:SUB] for p, t in zip(prods, terms)
    ]
    inner = [(jnp.exp(jnp.where(vis, t[6] - t[5], FAR)) * p[SUB:]).astype(BF16) for p, t in zip(prods, terms)]
    inverses = unit_lower_inverses(lowers)
    for (b, h), inv in zip(items, inverses):
        t_ref[b, h] = inv
    solved, backs = [], []
    for i, (b, h) in enumerate(items):
        t = terms[i]
        k = ks[i].astype(F32)
        right = jnp.concatenate([t[0] * v_r[h][sub[i]].astype(F32), t[4] * k], axis=1)
        solved.append(nn(inverses[i], right.astype(BF16)))
        weighted = turned((t[2] * k).astype(BF16), eye).astype(BF16)
        backs.append(jnp.concatenate([weighted, inner[i]], axis=0))
    gain = gain_ref[...]
    for b in range(PER_STEP):
        mine = [i for i, it in enumerate(items) if it[0] == b]
        olds = [end_ref[items[i][1]] for i in mine]
        old_bs = [o.astype(BF16) for o in olds]
        reads = [
            nn(jnp.concatenate([solved[i][:, HD:].astype(BF16), qs[i]], axis=0), ob) for i, ob in zip(mine, old_bs)
        ]
        ubs = [(solved[i][:, :HD] - r[:SUB]).astype(BF16) for i, r in zip(mine, reads)]
        adds = [nn(backs[i], ub) for i, ub in zip(mine, ubs)]
        for i, old, ob, r, ub, add in zip(mine, olds, old_bs, reads, ubs, adds):
            h = items[i][1]
            c_col, g_last = terms[i][6:]
            end_ref[h] = jnp.exp(g_last) * old + add[:HD]
            s_ref[b, h] = ob
            u_r[h][sub[i], :] = ub
            o = jnp.exp(c_col) * r[SUB:] + add[HD:]
            o_r[h][tok[i], :] = o.astype(BF16)
            scaled = o * lax.rsqrt(jnp.mean(o * o, axis=-1, keepdims=True) + EPS_NORM) * gain
            gate = g_r[h][tok[i]].astype(F32)
            z_ref[tok[i], h * HD : (h + 1) * HD] = (scaled * gate * sigmoid(gate)).astype(BF16)


def recur_specs(heads, at):
    tok = pl.BlockSpec((PER_STEP * SPAN, HD), lambda i: (at(i), 0))
    sub = pl.BlockSpec((PER_STEP * SUB, HD), lambda i: (at(i), 0))
    rows = pl.BlockSpec((PER_STEP, 8, SUB), lambda i: (at(i), 0, 0))
    wide = pl.BlockSpec((PER_STEP * SPAN, heads * HD), lambda i: (at(i), 0))
    mat = pl.BlockSpec((PER_STEP, heads, HD, HD), lambda i: (at(i), 0, 0, 0))
    one = pl.BlockSpec((1, HD), lambda i: (0, 0))
    state = pl.BlockSpec((heads, HD, HD), lambda i: (0, 0, 0))
    return tok, sub, rows, wide, mat, one, state


def recur(gain, start, q, k, v, gate, rows, first, steps, z=None):
    heads = len(q)
    tok, sub, row, wide, mat, one, state = recur_specs(heads, lambda i: i + first)
    o_tok, o_sub, _, _, o_mat, _, _ = recur_specs(heads, lambda i: i)
    n = steps * PER_STEP
    more = [] if z is None else [z]

    def shape(s, d):
        return jax.ShapeDtypeStruct(s, d)

    res = pl.pallas_call(
        functools.partial(recur_kernel, heads, len(more)),
        out_shape=[shape((q[0].shape[0], heads * HD), BF16), shape((heads, HD, HD), F32)]
        + [shape((n * SPAN, HD), BF16)] * heads
        + [shape((n * SUB, HD), BF16)] * heads
        + [shape((n, heads, HD, HD), BF16)] * 2,
        grid=(steps,),
        in_specs=[one, state]
        + [tok] * heads
        + [sub] * (2 * heads)
        + [tok] * heads
        + [row] * heads
        + [pl.BlockSpec(memory_space=pl.ANY)] * len(more),
        out_specs=[wide, state] + [o_tok] * heads + [o_sub] * heads + [o_mat] * 2,
        scratch_shapes=[pltpu.VMEM((PER_STEP * heads, SUB, SUB), F32)],
        compiler_params=params(),
        input_output_aliases={2 + 5 * heads: 0} if more else {},
        cost_estimate=cost(heads * n * 20 * 4.2e6, 1e6),
        name="recur",
    )(gain, start, *q, *k, *v, *gate, *rows, *more)
    return res[0], res[1], res[2 : 2 + heads], res[2 + heads : 2 + 2 * heads], res[2 + 2 * heads], res[3 + 2 * heads]


def recur_back_kernel(heads, more, gain_ref, start_ref, dz_ref, *refs):
    q_r, k_r, v_r, g_r, rows_r, o_r, u_r = (refs[i * heads : (i + 1) * heads] for i in range(7))
    s_ref, t_ref = refs[7 * heads : 7 * heads + 2]
    refs = refs[: 7 * heads + 2] + refs[7 * heads + 2 + more :]
    d_r = refs[7 * heads + 2 : 8 * heads + 2]
    drows_r = refs[8 * heads + 2 : 9 * heads + 2]
    dgain_ref, end_ref, cums, mixed = refs[9 * heads + 2 :]

    @pl.when(pl.program_id(0) == 0)
    def _():
        end_ref[...] = start_ref[...]
        dgain_ref[...] = jnp.zeros_like(dgain_ref)

    row, col = iota((SUB, SUB), 0), iota((SUB, SUB), 1)
    strict = col < row
    later = jnp.where(row >= col, 1.0, 0.0)
    vis = iota((SPAN, SUB), 1) // NH <= iota((SPAN, SUB), 0)
    gain = gain_ref[...]
    items = [(b, h) for b in reversed(range(PER_STEP)) for h in range(heads)]
    every = range(len(items))
    tok = [pl.ds(b * SPAN, SPAN) for b, _ in items]
    sub = [pl.ds(b * SUB, SUB) for b, _ in items]
    terms = decay_terms(rows_r, cums, items)
    ks = [k_r[h][sub[i]] for i, (b, h) in enumerate(items)]
    qs = [q_r[h][tok[i]] for i, (b, h) in enumerate(items)]
    us = [u_r[h][sub[i]] for i, (b, h) in enumerate(items)]
    ss = [s_ref[b, h] for b, h in items]
    prods = [nt(jnp.concatenate([k, q], axis=0), k) for k, q in zip(ks, qs)]

    dos = []
    dgain = jnp.zeros((1, HD), F32)
    for i, (b, h) in enumerate(items):
        dz = dz_ref[tok[i], h * HD : (h + 1) * HD].astype(F32)
        o = o_r[h][tok[i]].astype(F32)
        gate = g_r[h][tok[i]].astype(F32)
        inv_rms = lax.rsqrt(jnp.mean(o * o, axis=-1, keepdims=True) + EPS_NORM)
        n = o * inv_rms
        sg = sigmoid(gate)
        dy = dz * gate * sg
        d_r[h][tok[i], 5 * HD :] = (dz * n * gain * sg * (1.0 + gate * (1.0 - sg))).astype(BF16)
        dgain += jnp.sum(dy * n, axis=0, keepdims=True)
        dn = dy * gain
        dos.append((inv_rms * (dn - n * jnp.mean(dn * n, axis=-1, keepdims=True))).astype(BF16))
    dgain_ref[...] += dgain

    eye = jnp.where(row == col, 1.0, 0.0).astype(BF16)
    reads = [jnp.exp(jnp.where(vis, t[6] - t[5], FAR)) for t in terms]
    ecs = [jnp.exp(t[6]) for t in terms]
    kfs = [k.astype(F32) for k in ks]
    qfs = [q.astype(F32) for q in qs]
    lefts = [
        jnp.concatenate([turned((p[SUB:] * r).astype(BF16), eye).astype(BF16), (t[2] * k).astype(BF16)], axis=1)
        for p, r, t, k in zip(prods, reads, terms, kfs)
    ]
    downs = [
        turned(jnp.concatenate([(ec * q).astype(BF16), (-t[4] * k).astype(BF16)], axis=0), eye).astype(BF16)
        for ec, q, t, k in zip(ecs, qfs, terms, kfs)
    ]
    solves = [turned(t_ref[b, h], eye).astype(BF16) for b, h in items]

    drs, dsbs, dots = [None] * len(items), [None] * len(items), [None] * len(items)
    for b in reversed(range(PER_STEP)):
        mine = [i for i, it in enumerate(items) if it[0] == b]
        dss = {i: end_ref[items[i][1]] for i in mine}
        for i in mine:
            dsbs[i] = dss[i].astype(BF16)
            dots[i] = jnp.sum(dss[i] * ss[i].astype(F32), axis=0, keepdims=True)
        dus = {i: nn(lefts[i], jnp.concatenate([dos[i], dsbs[i]], axis=0)).astype(BF16) for i in mine}
        for i in mine:
            drs[i] = nn(solves[i], dus[i])
        for i in mine:
            add = nn(downs[i], jnp.concatenate([dos[i], drs[i].astype(BF16)], axis=0))
            end_ref[items[i][1]] = jnp.exp(terms[i][7]) * dss[i] + add

    drbs = [d.astype(BF16) for d in drs]
    from_s = [nt(jnp.concatenate([a, c], axis=0), s) for a, c, s in zip(drbs, dos, ss)]
    from_u = [nt(jnp.concatenate([a, c], axis=0), u) for a, c, u in zip(drbs, dos, us)]
    ks0 = [nn(k, s) for k, s in zip(ks, ss)]
    dws = [nt(u, d) for u, d in zip(us, dsbs)]
    dgs, dbs, dks, minus, dcs, syms = [], [], [], [], [], []
    nms = []
    for i, (b, h) in enumerate(items):
        beta, e_col, e_rest, g_col, beta_e, g_row, c_col, g_last = terms[i]
        k, q = kfs[i], qfs[i]
        mixed[i] = beta * drs[i]
        d_r[h][tok[i], 3 * HD : 4 * HD] = mixed[i, pl.ds(0, SPAN, 2), :].astype(BF16)
        d_r[h][tok[i], 4 * HD : 5 * HD] = mixed[i, pl.ds(1, SPAN, 2), :].astype(BF16)
        t1 = beta_e * from_s[i][:SUB]
        t3 = e_rest * dws[i]
        fade = jnp.exp(jnp.where(strict, g_col - g_row, FAR))
        y = -from_u[i][:SUB] * fade
        le = y * prods[i][:SUB]
        hh = beta * le
        kt3 = k * t3
        dbs.append(lane_sum(drs[i] * (v_r[h][sub[i]].astype(F32) - e_col * ks0[i]) + le))
        dg = lane_sum(hh - k * t1 - kt3)
        d_last = lane_sum(jnp.sum(kt3, axis=0, keepdims=True) + jnp.exp(g_last) * dots[i])
        dgs.append(dg + jnp.where(row[:, :1] == SUB - 1, d_last, 0.0))
        dks.append(t3 - t1)
        dkk = beta * y
        syms.append(dkk + turned(dkk.astype(BF16), eye))
        nm = from_u[i][SUB:] * reads[i]
        hm = nm * prods[i][SUB:]
        t2 = ecs[i] * from_s[i][SUB:]
        nms.append((nm.astype(BF16), t2))
        dcs.append(lane_sum(hm + q * t2))
        minus.append(jnp.sum(hh, axis=0, keepdims=True) + jnp.sum(hm, axis=0, keepdims=True))
    tops = [
        nn(jnp.concatenate([s.astype(BF16), nm], axis=0), k) for s, (nm, _), k in zip(syms, nms, ks)
    ]
    turns = [nn(turned(nm, eye).astype(BF16), q) for (nm, _), q in zip(nms, qs)]
    for i, (b, h) in enumerate(items):
        d_r[h][tok[i], :HD] = (tops[i][SUB:] + nms[i][1]).astype(BF16)
        mixed[i] = dks[i] + tops[i][:SUB] + turns[i]
        d_r[h][tok[i], HD : 2 * HD] = mixed[i, pl.ds(0, SPAN, 2), :].astype(BF16)
        d_r[h][tok[i], 2 * HD : 3 * HD] = mixed[i, pl.ds(1, SPAN, 2), :].astype(BF16)
        cums[i] = jnp.where(col == 0, dbs[i], jnp.where(col == 1, dgs[i], 0.0))
        odd = pl.ds(1, SPAN, 2)
        cums[i, odd, :] = cums[i, odd, :] + jnp.where(col[:SPAN] == 1, dcs[i], 0.0)
        rows = jnp.transpose(cums[i])[:8]
        first = iota((8, SUB), 0)
        summed = exact_nn(rows - jnp.where(first == 1, minus[i], 0.0), later)
        drows_r[h][b] = jnp.where(first == 0, rows, summed)


def recur_back(gain, start, dz, q, k, v, gate, rows, o, u, s, t, first, steps, done=()):
    heads = len(q)
    tok, sub, row, wide, mat, one, state = recur_specs(heads, lambda i: first + steps - 1 - i)
    o_tok, o_sub, _, _, o_mat, _, _ = recur_specs(heads, lambda i: steps - 1 - i)
    n = steps * PER_STEP
    seq = q[0].shape[0]
    d_spec = pl.BlockSpec((PER_STEP * SPAN, 6 * HD), lambda i: (first + steps - 1 - i, 0))

    def shape(s, d):
        return jax.ShapeDtypeStruct(s, d)

    res = pl.pallas_call(
        functools.partial(recur_back_kernel, heads, len(done)),
        out_shape=[shape((seq, 6 * HD), BF16)] * heads
        + [shape((seq // SPAN, 8, SUB), F32)] * heads
        + [shape((1, HD), F32), shape((heads, HD, HD), F32)],
        grid=(steps,),
        in_specs=[one, state, wide]
        + [tok] * heads
        + [sub] * (2 * heads)
        + [tok] * heads
        + [row] * heads
        + [o_tok] * heads
        + [o_sub] * heads
        + [o_mat] * 2
        + [pl.BlockSpec(memory_space=pl.ANY)] * len(done),
        out_specs=[d_spec] * heads + [row] * heads + [one, state],
        scratch_shapes=[pltpu.VMEM((PER_STEP * heads, SUB, SUB), F32)] * 2,
        compiler_params=params(),
        input_output_aliases={5 + 7 * heads + i: i for i in range(len(done))},
        cost_estimate=cost(heads * n * 30 * 4.2e6, 1e6),
        name="recur_back",
    )(gain, start, dz, *q, *k, *v, *gate, *rows, *o, *u, s, t, *done)
    return res[:heads], res[heads : 2 * heads], res[2 * heads], res[2 * heads + 1]


def project_back_kernel(pieces, bit, h, scal_ref, a_ref, cw_ref, raw_ref, rows_ref, d_ref, drow_ref, *refs):
    outer, refs = refs[:pieces], refs[pieces:]
    dp_ref, dcw_ref, dsm_ref = refs[:3]
    stacked = refs[3:5]
    raw_s, ds_s, acc, aux_s = refs[5:]
    tile = a_ref.shape[0]
    depth = outer[0].shape[1]
    chunk = 64
    step, steps = pl.program_id(0), pl.num_programs(0)
    base = pl.multiple_of((steps - 1 - step) * tile, tile)

    @pl.when(step == 0)
    def _():
        ds_s[tile : tile + 8, :] = jnp.zeros_like(ds_s[tile : tile + 8, :])
        dcw_ref[...] = jnp.zeros_like(dcw_ref)
        dsm_ref[...] = jnp.zeros_like(dsm_ref)

    @pl.when(step > 0)
    def _():
        ds_s[tile : tile + 8, :] = ds_s[0:8, :]

    @pl.when(step == steps - 1)
    def _():
        raw_s[0:8, :] = jnp.zeros_like(raw_s[0:8, :])

    @pl.when(step < steps - 1)
    def _():
        before = raw_ref[pl.ds(pl.multiple_of(base - 16, 16), 16), :].astype(F32)
        raw_s[0:8, :] = before[8:]

    raw_s[8 : tile + 8, :] = raw_ref[pl.ds(base, tile), :].astype(F32)
    for g in range(5):
        lanes = slice(g * HD, (g + 1) * HD)
        taps = cw_ref[0, :, lanes]
        sums = [jnp.zeros((8, HD), F32)] * TAPS
        for i in range(tile // chunk):
            start = i * chunk
            shifted = conv_shifts(raw_s, start, chunk, lanes)
            pre = shifted[0] * taps[0:1]
            for j in range(1, TAPS):
                pre = pre + shifted[j] * taps[j : j + 1]
            sg = sigmoid(pre)
            act = pre * sg
            d = d_ref[start : start + chunk, lanes].astype(F32)
            if g < 3:
                inv = lax.rsqrt(lane_sum(act * act) + EPS_UNIT)
                unit = act * inv
                d = inv * (d - unit * lane_sum(d * unit))
            d = d * (sg + act * (1.0 - sg))
            ds_s[start : start + chunk, lanes] = d
            sums = [s + jnp.sum((d * x).reshape(chunk // 8, 8, HD), axis=0) for s, x in zip(sums, shifted)]
        for j in range(TAPS):
            dcw_ref[j : j + 1, lanes] += jnp.sum(sums[j], axis=0, keepdims=True)
        for i in range(tile // chunk):
            start = i * chunk
            views = conv_shifts_back(ds_s, start, chunk, lanes)
            total = views[0] * taps[0:1]
            for j in range(1, TAPS):
                total = total + views[j] * taps[j : j + 1]
            dp_ref[start : start + chunk, lanes] = total.astype(BF16)

    rate = scal_ref[h, 0]
    lane = iota((SPAN, HD), 1)
    total = jnp.zeros((8, HD), F32)
    for b in range(tile // SPAN):
        both = jnp.concatenate([rows_ref[b], drow_ref[b]] + [jnp.zeros((8, SUB), F32)] * (SUB // 8 - 2), axis=0)
        aux_s[b] = jnp.transpose(both)
        even, odd = aux_s[b, pl.ds(0, SPAN, 2), :], aux_s[b, pl.ds(1, SPAN, 2), :]
        b1, b2, dg = even[:, 0:1], odd[:, 0:1], even[:, 9:10]
        darg = -rate * dg * sigmoid(even[:, 2:3])
        d1 = even[:, 8:9] * b1 * (1.0 - b1)
        d2 = odd[:, 8:9] * b2 * (1.0 - b2)
        vals = jnp.where(lane == 0, d1, jnp.where(lane == 1, d2, jnp.where(lane == 2, darg, 0.0)))
        here = pl.ds(b * SPAN, SPAN)
        dp_ref[here, 6 * HD :] = vals[:, :SMALL].astype(BF16)
        dp_ref[here, 5 * HD : 6 * HD] = d_ref[here, 5 * HD :]
        extra = jnp.where(lane == 0, dg * even[:, 1:2], jnp.where(lane == 1, darg, 0.0))
        total += jnp.sum(extra.reshape(SPAN // 8, 8, HD), axis=0)
    dsm_ref[...] += total

    term = tn(dp_ref[...], a_ref[...])

    @pl.when(step == 0)
    def _():
        acc[...] = term

    @pl.when(step > 0)
    def _():
        acc[...] += term

    @pl.when(step == steps - 1)
    def _():
        for stack, group in zip(stacked, sides(pieces, bit)):
            for i, p in enumerate(group):
                stack[i, :HD] = outer[p][...]
                stack[i, HD:] = acc[:, p * depth : (p + 1) * depth].astype(BF16)


def project_back(h, normed, conv_t, scal, raw, rows, d, drows, outer, bit):
    seq, dim = normed.shape
    pieces = len(outer)
    depth = outer[0].shape[1]
    tile = min(512, seq)
    end = seq // tile - 1
    along = lambda i: (end - i, 0)
    deep = pl.BlockSpec((tile // SPAN, 8, SUB), lambda i: (end - i, 0, 0))
    fix = lambda i: (0, 0)
    outs = [((seq, UNITS), BF16), ((8, 5 * HD), F32), ((8, HD), F32)]
    shapes = [jax.ShapeDtypeStruct(s, t) for s, t in outs] + stacks(pieces, (HD + UNITS, depth))
    res = pl.pallas_call(
        functools.partial(project_back_kernel, pieces, bit, h),
        out_shape=shapes,
        grid=(seq // tile,),
        in_specs=[
            pl.BlockSpec(memory_space=pltpu.SMEM),
            pl.BlockSpec((tile, dim), along),
            pl.BlockSpec((1,) + conv_t.shape[1:], lambda i: (h, 0, 0)),
            pl.BlockSpec(raw.shape, fix),
            deep,
            pl.BlockSpec((tile, 6 * HD), along),
            deep,
        ]
        + [pl.BlockSpec(g.shape, fix) for g in outer],
        out_specs=[pl.BlockSpec((tile, UNITS), along)]
        + [pl.BlockSpec(s, fix) for s, _ in outs[1:]]
        + [pl.BlockSpec(v.shape, lambda i: (0, 0, 0)) for v in shapes[3:]],
        scratch_shapes=[
            pltpu.VMEM((tile + 8, 5 * HD), F32),
            pltpu.VMEM((tile + 8, 5 * HD), F32),
            pltpu.VMEM((UNITS, dim), F32),
            pltpu.VMEM((tile // SPAN, SUB, SUB), F32),
        ],
        compiler_params=params(),
        cost_estimate=cost(2 * seq * dim * UNITS, 1e6),
        name="project_back",
    )(scal, normed, conv_t, raw, rows, d, drows, *outer)
    return res[0], res[1], res[2], res[3:]


def input_back_kernel(heads, pieces, *refs):
    dps, parts = refs[:heads], refs[heads : heads + heads * pieces]
    x_ref, da_ref, dgain_ref = refs[heads + heads * pieces :]
    depth = parts[0].shape[1]
    x = x_ref[...].astype(F32)
    unit = x * lax.rsqrt(jnp.mean(x * x, axis=-1, keepdims=True) + EPS_NORM)
    shares = []
    for p in range(pieces):
        total = nn(
            jnp.concatenate([d[:, 6 * HD :] for d in dps], axis=1),
            jnp.concatenate([parts[h * pieces + p][7 * HD :] for h in range(heads)], axis=0),
        )
        for h in range(heads):
            total += nn(dps[h][:, : 6 * HD], parts[h * pieces + p][HD : 7 * HD])
        low = total.astype(BF16)
        lanes = slice(p * depth, (p + 1) * depth)
        da_ref[:, lanes] = low
        shares.append(jnp.sum(low.astype(F32) * unit[:, lanes], axis=0, keepdims=True))
    share = jnp.concatenate(shares, axis=1)

    @pl.when(pl.program_id(0) == 0)
    def _():
        dgain_ref[...] = share

    @pl.when(pl.program_id(0) > 0)
    def _():
        dgain_ref[...] += share


def input_back(dps, parts, x):
    seq = dps[0].shape[0]
    heads, pieces = len(parts), len(parts[0])
    flat = [w for head in parts for w in head]
    dim = pieces * flat[0].shape[1]
    tile = min(256, seq)
    along = lambda i: (i, 0)
    return pl.pallas_call(
        functools.partial(input_back_kernel, heads, pieces),
        out_shape=[jax.ShapeDtypeStruct((seq, dim), BF16), jax.ShapeDtypeStruct((1, dim), F32)],
        grid=(seq // tile,),
        in_specs=[pl.BlockSpec((tile, UNITS), along)] * heads
        + [pl.BlockSpec(w.shape, lambda i: (0, 0)) for w in flat]
        + [pl.BlockSpec((tile, dim), along)],
        out_specs=[pl.BlockSpec((tile, dim), along), pl.BlockSpec((1, dim), lambda i: (0, 0))],
        compiler_params=params(),
        cost_estimate=cost(2 * seq * dim * UNITS * heads, 1e6),
        name="input_back",
    )(*dps, *flat, x)


def mix_kernel(heads, pieces, z_ref, *refs):
    parts, out_ref = refs[:-1], refs[-1]
    depth = parts[0].shape[1]
    for p in range(pieces):
        right = jnp.concatenate([parts[h * pieces + p][...] for h in range(heads)], axis=0)
        out_ref[:, p * depth : (p + 1) * depth] = nn(z_ref[...], right).astype(BF16)


def outer_specs(parts):
    return [pl.BlockSpec((HD, w.shape[1]), lambda i: (0, 0)) for head in parts for w in head]


def mix_out(z, parts):
    seq = z.shape[0]
    heads, pieces = len(parts), len(parts[0])
    dim = pieces * parts[0][0].shape[1]
    tile = min(256, seq)
    along = lambda i: (i, 0)
    return pl.pallas_call(
        functools.partial(mix_kernel, heads, pieces),
        out_shape=jax.ShapeDtypeStruct((seq, dim), BF16),
        grid=(seq // tile,),
        in_specs=[pl.BlockSpec((tile, z.shape[1]), along)] + outer_specs(parts),
        out_specs=pl.BlockSpec((tile, dim), along),
        compiler_params=params(),
        cost_estimate=cost(2 * seq * dim * z.shape[1], 1e6),
        name="mix_out",
    )(z, *[w for head in parts for w in head])


def mix_back_kernel(heads, pieces, gain_ref, own_ref, other_ref, mid_ref, dy_ref, z_ref, *refs):
    parts, refs = refs[: heads * pieces], refs[heads * pieces :]
    dmix_ref, dz_ref, dgain_ref = refs[:3]
    grads, acc = refs[3:-1], refs[-1]
    depth = parts[0].shape[1]
    step, steps = pl.program_id(0), pl.num_programs(0)
    mid = mid_ref[...]
    dn = own_ref[...].astype(F32) + other_ref[...].astype(F32)
    inv = lax.rsqrt(jnp.mean(mid * mid, axis=-1, keepdims=True) + EPS_NORM)
    unit = mid * inv
    prod = dn * unit
    share = jnp.sum(prod, axis=0, keepdims=True)
    scaled = dn * gain_ref[...]
    back = inv * (scaled - unit * jnp.mean(prod * gain_ref[...], axis=-1, keepdims=True))
    dmix_ref[...] = (dy_ref[...].astype(F32) + back).astype(BF16)

    @pl.when(step == 0)
    def _():
        dgain_ref[...] = share
        acc[...] = jnp.zeros_like(acc)

    @pl.when(step > 0)
    def _():
        dgain_ref[...] += share

    dz = jnp.zeros((z_ref.shape[0], heads * HD), F32)
    for p in range(pieces):
        lanes = slice(p * depth, (p + 1) * depth)
        right = jnp.concatenate([parts[h * pieces + p][...] for h in range(heads)], axis=0)
        dz += nt(dmix_ref[:, lanes], right)
    acc[...] += tn(z_ref[...], dmix_ref[...])
    dz_ref[...] = dz.astype(BF16)

    @pl.when(step == steps - 1)
    def _():
        for h in range(heads):
            for p in range(pieces):
                grads[h * pieces + p][...] = acc[h * HD : (h + 1) * HD, p * depth : (p + 1) * depth].astype(BF16)


def mix_back(gain, own, other, mid, dy, z, parts):
    seq, dim = mid.shape
    heads, pieces = len(parts), len(parts[0])
    wide = z.shape[1]
    tile = min(256, seq)
    row = pl.BlockSpec((tile, dim), lambda i: (i, 0))
    one = pl.BlockSpec((1, dim), lambda i: (0, 0))
    zs = pl.BlockSpec((tile, wide), lambda i: (i, 0))
    res = pl.pallas_call(
        functools.partial(mix_back_kernel, heads, pieces),
        out_shape=[
            jax.ShapeDtypeStruct((seq, dim), BF16),
            jax.ShapeDtypeStruct((seq, wide), BF16),
            jax.ShapeDtypeStruct((1, dim), F32),
        ]
        + [jax.ShapeDtypeStruct((HD, dim // pieces), BF16)] * (heads * pieces),
        grid=(seq // tile,),
        in_specs=[one, row, row, row, row, zs] + outer_specs(parts),
        out_specs=[row, zs, one] + outer_specs(parts),
        scratch_shapes=[pltpu.VMEM((wide, dim), F32)],
        compiler_params=params(),
        cost_estimate=cost(4 * seq * dim * wide, 1e6),
        name="mix_back",
    )(gain, own, other, mid, dy, z, *[w for head in parts for w in head])
    return res[0], res[1], res[2], [res[3 + h * pieces : 3 + (h + 1) * pieces] for h in range(heads)]


def select_kernel(counts, apart, table_ref, *refs):
    j = pl.program_id(0)
    first = 0
    for g, n in enumerate(counts):
        width = refs[first].shape[2]
        value = refs[first][...]
        for i in range(1, n):
            value = jnp.where(table_ref[2 * g, j] == i, refs[first + i][...], value)
        if apart:
            refs[sum(counts) + g][...] = value
        else:
            refs[-1][:, :, g * width : (g + 1) * width] = value
        first += n


def select_blocks(groups, table, count, apart=False):
    specs, flat = [], []
    for g, sources in enumerate(groups):
        for i, value in enumerate(sources):

            def where(j, t, g=g, i=i):
                return (jnp.where(t[2 * g, j] == i, t[2 * g + 1, j], 0), 0, 0)

            specs.append(pl.BlockSpec((1,) + value.shape[1:], where))
            flat.append(value)
    piece, width = flat[0].shape[1:]
    total = width if apart else width * len(groups)
    outs = len(groups) if apart else 1
    res = pl.pallas_call(
        functools.partial(select_kernel, [len(g) for g in groups], apart),
        out_shape=[jax.ShapeDtypeStruct((count, piece, total), flat[0].dtype)] * outs,
        grid_spec=pltpu.PrefetchScalarGridSpec(
            num_scalar_prefetch=1,
            grid=(count,),
            in_specs=specs,
            out_specs=[pl.BlockSpec((1, piece, total), lambda j, t: (j, 0, 0))] * outs,
        ),
        compiler_params=params(),
        cost_estimate=cost(1e6, 1e6),
        name="select_blocks",
    )(table, *flat)
    return res if apart else res[0]


def ffn_kernel(pieces, chunks, bits, more, b_ref, dy_ref, *refs):
    weights = refs[: pieces * chunks]
    refs = refs[pieces * chunks :]
    sums_in, refs = (refs[:2], refs[2:]) if more else (None, refs)
    out_ref, db_ref = refs[:2]
    stacked = refs[2 : 2 + 2 * chunks]
    b_s, dy_s, hid_s, dg_s, du_s = refs[2 + 2 * chunks :]
    depth = weights[0].shape[1]
    units = weights[0].shape[0] // 3
    tile = b_ref.shape[0]
    step, steps = pl.program_id(0), pl.num_programs(0)

    def weight(p, i):
        return jnp.concatenate(
            [weights[c * pieces + p][i * units : (i + 1) * units] for c in range(chunks)], axis=0
        )

    rows = pl.ds(pl.multiple_of(step * tile, tile), tile)
    b_s[rows, :] = b_ref[...]
    dy_s[rows, :] = dy_ref[...]
    gate = jnp.zeros((tile, units * chunks), F32)
    up = jnp.zeros((tile, units * chunks), F32)
    dh = jnp.zeros((tile, units * chunks), F32)
    for p in range(pieces):
        lanes = slice(p * depth, (p + 1) * depth)
        block, dblock = b_ref[:, lanes], dy_ref[:, lanes]
        gate += nt(block, weight(p, 0))
        up += nt(block, weight(p, 1))
        dh += nt(dblock, weight(p, 2))
    sg = sigmoid(gate)
    act = gate * sg
    hid = (act * up).astype(BF16)
    du = (dh * act).astype(BF16)
    dg = (dh * up * (sg + act * (1.0 - sg))).astype(BF16)
    hid_s[rows, :] = hid
    dg_s[rows, :] = dg
    du_s[rows, :] = du
    for p in range(pieces):
        lanes = slice(p * depth, (p + 1) * depth)
        o = nn(hid, weight(p, 2))
        d = nn(dg, weight(p, 0)) + nn(du, weight(p, 1))
        if more:
            o += sums_in[0][:, lanes].astype(F32)
            d += sums_in[1][:, lanes].astype(F32)
        out_ref[:, lanes] = o.astype(out_ref.dtype)
        db_ref[:, lanes] = d.astype(db_ref.dtype)

    @pl.when(step == steps - 1)
    def _():
        for i, (left, right) in enumerate([(dg_s, b_s), (du_s, b_s), (hid_s, dy_s)]):
            g = tn(left[...], right[...]).astype(BF16)
            for c in range(chunks):
                for stack, group in zip(stacked[2 * c : 2 * c + 2], sides(pieces, bits[c])):
                    for n, p in enumerate(group):
                        stack[n, i * units : (i + 1) * units] = g[
                            c * units : (c + 1) * units, p * depth : (p + 1) * depth
                        ]


def ffn(normed, dy, parts, bits, sums=None, last=True):
    seq, dim = normed.shape
    chunks, pieces = len(parts), len(parts[0])
    flat = [w for chunk in parts for w in chunk]
    units = flat[0].shape[0] // 3
    tile = min(256, seq)
    row = pl.BlockSpec((tile, dim), lambda i: (i, 0))
    more = () if sums is None else tuple(sums)
    grads = stacks(pieces, flat[0].shape) * chunks
    res = pl.pallas_call(
        functools.partial(ffn_kernel, pieces, chunks, bits, bool(more)),
        out_shape=[jax.ShapeDtypeStruct((seq, dim), BF16 if last else F32)] * 2 + grads,
        grid=(seq // tile,),
        in_specs=[row, row] + [pl.BlockSpec(w.shape, lambda i: (0, 0)) for w in flat] + [row] * len(more),
        out_specs=[row, row] + [pl.BlockSpec(g.shape, lambda i: (0, 0, 0)) for g in grads],
        scratch_shapes=[pltpu.VMEM((seq, dim), BF16)] * 2 + [pltpu.VMEM((seq, units * chunks), BF16)] * 3,
        compiler_params=params(),
        cost_estimate=cost(18 * seq * dim * units * chunks, 1e6),
        name="ffn",
    )(normed, dy, *flat, *more)
    return res[0], res[1], [res[2 + 2 * c : 4 + 2 * c] for c in range(chunks)]


def sync(*trees):
    leaves, tree = jax.tree.flatten(trees)
    return jax.tree.unflatten(tree, lax.optimization_barrier(leaves))


def bits_of(n):
    return [1 << i for i in range(n.bit_length() - 1)]


class Place:
    def __init__(self):
        self.n_f = lax.axis_size("fsdp")
        self.n_t = lax.axis_size("tp")
        self.chips = self.n_f // 2
        f = lax.axis_index("fsdp")
        self.f = f
        self.core = f % 2
        self.k = f // 2
        self.t = lax.axis_index("tp")

    def swap(self, value):
        return lax.ppermute(value, "fsdp", [(i, i ^ 1) for i in range(self.n_f)])

    def move(self, value, bit):
        return lax.ppermute(value, "fsdp", [(i, i ^ (2 * bit)) for i in range(self.n_f)])

    def turn(self, value, r):
        return lax.ppermute(value, "tp", [(i, (i + r) % self.n_t) for i in range(self.n_t)])

    def in_order(self, mine, other, axis):
        first = jnp.where(self.core == 0, mine, other)
        second = jnp.where(self.core == 0, other, mine)
        return jnp.concatenate([first, second], axis=axis)

    def halves(self, value, axis):
        size = value.shape[axis] // 2
        return (
            lax.dynamic_slice_in_dim(value, self.core * size, size, axis),
            lax.dynamic_slice_in_dim(value, (1 - self.core) * size, size, axis),
        )

    def relative(self, value):
        width = value.shape[-1] // self.chips
        blocks = [
            lax.dynamic_slice_in_dim(value, (self.k ^ p) * width, width, value.ndim - 1) for p in range(self.chips)
        ]
        return jnp.concatenate(blocks, axis=-1)

    def spread_out(self, value):
        if value.shape[0] < self.n_t:
            value = jnp.pad(value, ((0, self.n_t - value.shape[0]),) + ((0, 0),) * (value.ndim - 1))
        return lax.all_to_all(value, "tp", split_axis=0, concat_axis=0, tiled=True)

    def chip_sum(self, value):
        for bit in [1] + [2 * b for b in bits_of(self.chips)]:
            value = value + lax.ppermute(value, "fsdp", [(i, i ^ bit) for i in range(self.n_f)])
        return value

    def line_sum(self, value):
        total = value
        for r in range(1, self.n_t):
            total = total + self.turn(value, r)
        return total


def rms_terms(value):
    return lax.rsqrt(jnp.mean(value * value, axis=-1, keepdims=True) + EPS_NORM)


def rms_back(value, gain, d_normed):
    inv = rms_terms(value)
    unit = value * inv
    dn = d_normed * gain
    return inv * (dn - unit * jnp.mean(dn * unit, axis=-1, keepdims=True))


class Gather:
    def __init__(self, at, shard):
        self.at = at
        self.parts = {(0, 0): shard}

    def turn(self, r, by=None):
        by = by or r
        self.parts[r, 0] = self.at.turn(self.parts[r - by, 0], by)

    def move(self, r, to, via):
        self.parts[r, to] = self.at.move(self.parts[r, to ^ via], via)

    def full(self, r):
        return [self.parts[r, p] for p in range(self.at.chips)]

    def rest(self):
        for r in range(1, self.at.n_t):
            self.turn(r)
        for r in range(self.at.n_t):
            for p in range(1, self.at.chips):
                self.move(r, p, p & -p)
        return [self.full(r) for r in range(self.at.n_t)]


def first_bit(at, r):
    return at.chips // 2 if r % 3 == 0 else 1


class Scatter:
    def __init__(self, at):
        self.at = at
        self.near, self.far, self.two, self.one, self.end = {}, {}, {}, {}, {}

    def put(self, r, stacked):
        self.near[r], self.far[r] = stacked

    def cross(self, *turns):
        for r in turns:
            self.far[r] = self.at.move(self.far[r], first_bit(self.at, r))

    def fold(self, *turns):
        sums = add_stacks([(self.near.pop(r), self.far.pop(r)) for r in turns])
        for r, (keep, give) in zip(turns, sums):
            self.two[r] = keep, self.at.move(give, 3 - first_bit(self.at, r))

    def close(self, *turns):
        for r in turns:
            keep, came = self.two.pop(r)
            self.one[r] = (keep.astype(F32) + came.astype(F32)).astype(BF16)

    def home(self, r):
        self.end[r] = self.at.turn(self.one.pop(r), self.at.n_t - r)

    def merge(self, r):
        self.end[r] = self.at.turn(self.one.pop(r), self.at.n_t - 1)

    def join(self, r):
        self.one[r - 1] = (self.one[r - 1].astype(F32) + self.end.pop(r).astype(F32)).astype(BF16)

    def total(self):
        return sum(v.astype(F32) for v in list(self.one.values()) + list(self.end.values()))

    def state(self):
        return self.near, self.far, self.two, self.one, self.end

    def take(self, state):
        self.near, self.far, self.two, self.one, self.end = state

    def rest(self):
        for r in range(self.at.n_t):
            have = {}
            for stack, group in zip((self.near.pop(r), self.far.pop(r)), sides(self.at.chips, first_bit(self.at, r))):
                have.update({p: stack[i] for i, p in enumerate(group)})
            for bit in bits_of(self.at.chips):
                for p in [p for p in have if p & bit]:
                    came = self.at.move(have.pop(p), bit)
                    have[p ^ bit] = (have[p ^ bit].astype(F32) + came.astype(F32)).astype(BF16)
            self.one[r] = have[0]
            if r:
                self.home(r)


class Routing:
    def __init__(self, at, value, order, source):
        self.at, self.order = at, order
        self.per_chip = value.shape[0]
        self.have, self.where = [value], [0]
        reach = [0]
        for bit in order[:-1]:
            reach += [w | bit for w in reach]
        tables = []
        for chip in (at.k ^ order[-1], at.k):
            ask = lax.dynamic_slice_in_dim(source, chip * self.per_chip, self.per_chip, 0)
            distance = (ask // self.per_chip) ^ at.k
            src = sum(jnp.where(distance == w, i, 0) for i, w in enumerate(reach))
            near = (distance & order[-1]) == 0
            slot = ask % self.per_chip
            if chip is not at.k:
                tables.append((src, slot))
            else:
                tables.append(
                    (
                        jnp.where(near, src, len(reach)),
                        jnp.where(near, slot, jnp.arange(self.per_chip, dtype=jnp.int32)),
                    )
                )
        self.ask, self.keep = (jnp.stack(t) for t in tables)

    def step(self):
        bit = self.order[len(self.where).bit_length() - 1]
        self.have = self.have + [self.at.move(v, bit) for v in self.have]
        self.where = self.where + [w | bit for w in self.where]

    def last(self, give):
        self.have = self.have + [self.at.move(give, self.order[-1])]


def local(
    tokens, lengths, perm, cotangent, norm1_gain, input_weight, conv_w, decay_log, decay_bias, out_gain, w_out,
    norm2_gain, gate_up_weight, down_weight
):
    at = Place()
    slots, piece, dim = tokens.shape
    n_f, n_t, chips = at.n_f, at.n_t, at.chips
    heads_all = conv_w.shape[0]
    heads = heads_all // 2
    local_heads = input_weight.shape[1]
    cols = input_weight.shape[2]
    by_turn = local_heads == 2
    laps = list(range(n_t))
    bits = bits_of(chips)
    fast = by_turn and chips == 4 and n_t == 4
    per_chip = 2 * slots
    seq = n_t * piece
    steps = seq // SPAN // PER_STEP // 2

    pad = SMALL - (cols - 6 * HD)
    if by_turn:
        packed = jnp.transpose(input_weight, (1, 2, 0))
        zeros = jnp.zeros((local_heads, pad, packed.shape[2]), BF16)
        packed = jnp.concatenate([w_out.reshape(local_heads, HD, -1), packed, zeros], axis=1)
        mine, give = at.halves(packed, 0)
        m_own = at.in_order(mine[0], at.swap(give[0]), 1)
        head_ids = ((at.t - jnp.arange(n_t, dtype=jnp.int32)) % n_t) * 2 + at.core
    else:
        m_own = None
        head_ids = at.core * heads + jnp.arange(heads, dtype=jnp.int32)
    m_own, tokens, gate_up_weight, down_weight, cotangent = sync(
        m_own, tokens, gate_up_weight, down_weight, cotangent
    )
    mine, give = at.halves(tokens, 2)
    both = at.in_order(mine, at.swap(give), 0)
    packed = jnp.concatenate([jnp.transpose(gate_up_weight, (1, 2, 0)), down_weight[None]], axis=0)
    mine, give = at.halves(packed, 1)
    f_own = at.in_order(mine, at.swap(give), 2)
    f_own = f_own.reshape(-1, f_own.shape[2])
    mine, give = at.halves(cotangent, 2)
    cot_both = at.in_order(mine, at.swap(give), 0)

    own = head_ids[:, None] == jnp.arange(heads_all, dtype=jnp.int32)[None, :]
    taps = jnp.pad(jnp.transpose(conv_w, (0, 2, 1)), ((0, 0), (0, 8 - TAPS), (0, 0)))
    conv_t = jnp.sum(jnp.where(own[:, :, None, None], taps[None], 0.0), axis=1)
    scal = jnp.stack(
        [
            jnp.sum(jnp.where(own, jnp.exp(decay_log)[None], 0.0), axis=1),
            jnp.sum(jnp.where(own, decay_bias[None], 0.0), axis=1),
        ],
        axis=1,
    )
    gain1 = at.relative(norm1_gain)
    gain2 = at.relative(norm2_gain)
    gain_o = out_gain[None]
    start_state = jnp.zeros((heads, HD, HD), F32)

    seq_id = jnp.minimum(at.k * per_chip + at.t, lengths.shape[0] - 1)
    length = jnp.where(at.t < per_chip, lax.dynamic_index_in_dim(lengths, seq_id, 0, keepdims=False), 0)
    live = (jnp.arange(seq, dtype=jnp.int32) < length).astype(BF16)[:, None]
    slot_ids = jnp.arange(perm.shape[0], dtype=jnp.int32)
    source = jnp.sum(jnp.where(perm[None, :] == slot_ids[:, None], slot_ids[None, :], 0), axis=1)
    quarter = dim // 4
    routes = [
        Routing(at, cot_both[:, :, :quarter], bits, source),
        Routing(at, cot_both[:, :, quarter:], bits[::-1], source),
    ]

    def route_state():
        return [r.have for r in routes]

    def set_routes(state):
        for r, v in zip(routes, state):
            r.have = v

    def routed():
        groups = [r.have for r in routes]
        return select_blocks(groups, jnp.concatenate([r.keep for r in routes], axis=0), per_chip)

    def sequence(half):
        half = half.reshape(seq, -1)
        return at.relative(at.in_order(half, at.swap(half), 1))

    def norm_first(x):
        return (x * rms_terms(x) * gain1).astype(BF16)

    f = Gather(at, f_own)
    proj = {}

    def asked():
        return select_blocks([r.have for r in routes], jnp.concatenate([r.ask for r in routes], axis=0), per_chip, True)

    if fast:
        m = Gather(at, m_own)

        def run(r):
            proj[r] = project(r, normed_one, m.full(r), conv_t, scal)

        def without(parts, *keys):
            return {k: v for k, v in parts.items() if k not in keys}

        for p in range(1, chips):
            m.move(0, p, p)
        m.turn(1)
        m.turn(3)
        m.parts, f.parts, both, cot_both, conv_t, scal, gain1, gain2, live, extra = sync(
            m.parts, f.parts, both, cot_both, conv_t, scal, gain1, gain2, live, [(r.ask, r.keep) for r in routes]
        )
        for r, (ask, keep), part in zip(routes, extra, (cot_both[:, :, :quarter], cot_both[:, :, quarter:])):
            r.ask, r.keep, r.have = ask, keep, [part]
        for r in (1, 3):
            m.move(r, 1, 1)
            m.move(r, 2, 2)
        came = at.spread_out(both)
        m.turn(2, 1)
        m.parts, f.parts, came = sync(m.parts, f.parts, came)
        m.move(1, 3, 1)
        m.move(3, 3, 2)
        m.move(2, 1, 1)
        m.move(2, 2, 2)
        x = sequence(came)
        normed_one = norm_first(x.astype(F32))
        run(0)
        early = without(m.parts, (2, 1), (2, 2))
        early, f.parts, proj[0], normed_one, x = sync(early, f.parts, proj[0], normed_one, x)
        m.parts.update(early)
        m.move(2, 3, 3)
        f.turn(1)
        f.turn(3)
        run(1)
        run(3)
        state = route_state()
        m.parts, proj, normed_one, f.parts, state = sync(m.parts, proj, normed_one, f.parts, state)
        set_routes(state)
        for r in routes:
            r.step()
        f.move(0, 1, 1)
        f.move(0, 2, 2)
        run(2)
        early = without(f.parts, (0, 1), (0, 2))
        state = route_state()
        proj, early, state = sync(proj, early, state)
        f.parts.update(early)
        set_routes(state)
        give = asked()
        m_parts = [m.full(r) for r in laps]
    else:
        x = sequence(at.spread_out(both))
        normed_one = norm_first(x.astype(F32))
        if by_turn:
            m_parts = Gather(at, m_own).rest()
        else:
            full = lax.all_gather(lax.all_gather(input_weight, "tp", axis=1, tiled=True), "fsdp", axis=0, tiled=True)
            full = at.relative(jnp.transpose(full, (1, 2, 0)))
            full_out = lax.all_gather(lax.all_gather(w_out, "tp", axis=0, tiled=True), "fsdp", axis=1, tiled=True)
            full_out = at.relative(full_out).reshape(heads_all, HD, dim)
            zeros = jnp.zeros((heads_all, pad, dim), BF16)
            full = at.halves(jnp.concatenate([full_out, full, zeros], axis=1), 0)[0]
            m_parts = [jnp.split(full[h], chips, axis=1) for h in range(heads)]
        for h in range(heads):
            proj[h] = project(h, normed_one, m_parts[h], conv_t, scal)
        for r in routes:
            for _ in bits[1:]:
                r.step()
        give = asked()
        f_parts = f.rest()

    raw, gate, q, k, v, rows = (list(group) for group in zip(*[proj[h] for h in range(heads)]))
    for r, part in zip(routes, give):
        r.last(part)
    if fast:
        f.move(1, 1, 1)
        f.move(1, 2, 2)
    first = recur(gain_o, start_state, q, k, v, gate, rows, 0, steps)
    if fast:
        state = route_state()
        first, f.parts, state = sync(first, f.parts, state)
        set_routes(state)
    cot_came = at.spread_out(routed())
    if fast:
        f.move(0, 3, 2)
        f.move(1, 3, 1)
        f.move(3, 1, 1)
        f.turn(2, 1)
    second = recur(gain_o, first[1], q, k, v, gate, rows, steps, steps, first[0])
    if fast:
        second, f.parts, cot_came = sync(second, f.parts, cot_came)
        f.move(3, 2, 2)
        f.move(2, 1, 1)
    z = second[0]
    mix = mix_out(z, m_parts)
    mid = x.astype(F32) + (mix.astype(F32) + at.swap(mix).astype(F32))
    normed_two = (mid * rms_terms(mid) * gain2).astype(BF16)
    dy = live * sequence(cot_came)

    f_rs = Scatter(at)
    half = n_t // 2
    group_a, group_b = laps[:half], laps[half:][::-1]
    bits_a, bits_b = [first_bit(at, r) for r in group_a], [first_bit(at, r) for r in group_b]
    if fast:
        normed_two, dy, f.parts = sync(normed_two, dy, f.parts)
        f.move(3, 3, 2)
        f.move(2, 2, 2)
        f.move(2, 3, 2)
        f_parts = {r: f.full(r) for r in group_a}
    net, db, grads = ffn(normed_two, dy, [f_parts[r] for r in group_a], bits_a, last=False)
    if fast:
        net, db, grads, f.parts = sync(net, db, grads, f.parts)
        f_parts = {r: f.full(r) for r in group_b}
    for r, g in zip(group_a, grads):
        f_rs.put(r, g)
    if fast:
        f_rs.cross(0, 1)
    net, db, grads = ffn(normed_two, dy, [f_parts[r] for r in group_b], bits_b, (net, db))
    if fast:
        net, db, grads, state = sync(net, db, grads, f_rs.state())
        f_rs.take(state)
    for r, g in zip(group_b, grads):
        f_rs.put(r, g)

    db_other = at.swap(db)
    if fast:
        f_rs.fold(0, 1)
        f_rs.cross(3, 2)
    d_mix, dz, g_gain2, g_out = mix_back(gain2[None], db, db_other, mid, dy, z, m_parts)
    if fast:
        dz, d_mix, g_out, f_rs.two, net = sync(dz, d_mix, g_out, f_rs.two, net)
    net_other = at.swap(net)
    back = recur_back(gain_o, start_state, dz, q, k, v, gate, rows, *second[2:], steps, steps)
    if fast:
        back, state, net_other, dz = sync(back, f_rs.state(), net_other, dz)
        f_rs.take(state)
        f_rs.close(0, 1)
        f_rs.fold(3, 2)

    def give_back(value):
        mine = at.halves(at.relative(value.astype(BF16)), 1)[0]
        return mine.reshape(n_t, piece, dim // 2)

    def settle(came):
        mine, give = at.halves(came[:per_chip], 0)
        return at.in_order(mine, at.swap(give), 2)

    g_gain_o = back[2]
    out_home = give_back(live.astype(F32) * (mid + (net.astype(F32) + net_other.astype(F32))))
    out_came = lax.all_to_all(out_home, "tp", split_axis=0, concat_axis=0, tiled=True)
    back = recur_back(
        gain_o, back[3], dz, q, k, v, gate, rows, *first[2:], 0, steps, tuple(back[0]) + tuple(back[1])
    )
    g_gain_o = g_gain_o + back[2]
    ds, drows = back[:2]
    if fast:
        ds, drows, out_came, state = sync(ds, drows, out_came, f_rs.state())
        f_rs.take(state)
        f_rs.close(3, 2)
        f_rs.merge(2)
        f_rs.home(3)

    dps, g_conv, g_small = {}, {}, {}
    m_rs = Scatter(at)

    def run_back(h):
        dps[h], g_conv[h], g_small[h], grads = project_back(
            h, normed_one, conv_t, scal, raw[h], rows[h], ds[h], drows[h], g_out[h], first_bit(at, h)
        )
        m_rs.put(h, grads)

    if fast:
        run_back(2)
        dps, state, f_state, ds = sync(dps, m_rs.state(), f_rs.state(), ds)
        m_rs.take(state)
        f_rs.take(f_state)
        f_rs.join(2)
        f_rs.home(1)
        m_rs.cross(2)
        run_back(1)
        dps, state, ds = sync(dps, m_rs.state(), ds)
        m_rs.take(state)
        m_rs.fold(2)
        m_rs.cross(1)
        run_back(3)
        dps, state, ds, f_rs.end = sync(dps, m_rs.state(), ds, f_rs.end)
        m_rs.take(state)
        m_rs.close(2)
        m_rs.home(2)
        m_rs.fold(1)
        m_rs.cross(3)
        run_back(0)
        dps, m_rs.two, m_rs.near, far = sync(dps, m_rs.two, m_rs.near, {0: m_rs.far[0]})
        m_rs.far.update(far)
        m_rs.close(1)
        m_rs.home(1)
        m_rs.cross(0)
    else:
        for h in range(heads):
            run_back(h)
    output = settle(out_came)
    da, g_gain1 = input_back([dps[h] for h in range(heads)], m_parts, x)
    if fast:
        da, g_gain1, far, m_rs.near = sync(da, g_gain1, {3: m_rs.far[3]}, m_rs.near)
        m_rs.far.update(far)
        m_rs.fold(3)
    da_other = at.swap(da)
    d_x_norm = rms_back(x.astype(F32), gain1, da.astype(F32) + da_other.astype(F32))
    dx_home = give_back(d_mix.astype(F32) + d_x_norm)

    small = [jnp.sum(g_small[h], axis=0) for h in range(heads)]
    conv_all = sum(jnp.where(own[h][:, None, None], g_conv[h][None, :TAPS], 0.0) for h in range(heads)).reshape(-1, HD)
    decay_all = sum(jnp.where(own[h][:, None], small[h][None], 0.0) for h in range(heads))
    gains = jnp.concatenate([at.relative(g_gain1[0]), 0.5 * at.relative(g_gain2[0])]).reshape(-1, HD)
    sums = jnp.concatenate([conv_all, decay_all, gains, g_gain_o], axis=0)
    if fast:
        dx_home, sums, state = sync(dx_home, at.chip_sum(sums), m_rs.state())
        m_rs.take(state)
        m_rs.fold(0)
        m_rs.close(3)
        m_rs.home(3)
    else:
        sums = at.chip_sum(sums)
    sums = at.line_sum(sums)
    dx_came = lax.all_to_all(dx_home, "tp", split_axis=0, concat_axis=0, tiled=True)
    if fast:
        dx_came, sums, m_rs.two, m_rs.end = sync(dx_came, sums, m_rs.two, m_rs.end)
        m_rs.close(0)
    input_grad = settle(dx_came)
    n_conv = conv_all.shape[0]
    g_conv_all = jnp.transpose(sums[:n_conv].reshape(heads_all, TAPS, -1), (0, 2, 1))
    decay_sum = sums[n_conv : n_conv + heads_all]
    gain_sum = sums[n_conv + heads_all : -1].reshape(2, dim)

    def to_core(value, joined):
        mine, give = at.halves(value.astype(BF16), value.ndim - 1)
        return at.in_order(mine, at.swap(give), joined).astype(F32)

    if not fast:
        f_rs.rest()
    f_total = f_rs.total()
    g_ffn = to_core(f_total.reshape(3, -1, f_total.shape[1]), 1)
    grad_gate_up = jnp.transpose(g_ffn[:2], (2, 0, 1))
    grad_down = g_ffn[2]
    if by_turn:
        if not fast:
            m_rs.rest()
        joined = to_core(m_rs.total()[None], 0)
    else:
        joined = []
        for h in range(heads):
            have = {}
            for stack, group in zip((m_rs.near[h], m_rs.far[h]), sides(chips, first_bit(at, h))):
                have.update({p: stack[i] for i, p in enumerate(group)})
            joined.append(jnp.concatenate([have[p] for p in range(chips)], axis=1))
        joined = jnp.stack(joined)
        spread = jnp.zeros((heads_all,) + joined.shape[1:], BF16)
        spread = lax.dynamic_update_slice_in_dim(spread, at.relative(joined), at.core * heads, 0)
        spread = lax.psum_scatter(spread, "tp", scatter_dimension=0, tiled=True)
        joined = lax.psum_scatter(spread, "fsdp", scatter_dimension=2, tiled=True).astype(F32)
    grad_in = jnp.transpose(joined[:, HD : HD + cols], (2, 0, 1))
    grad_out = joined[:, :HD].reshape(local_heads * HD, -1)
    return (
        output, input_grad, gain_sum[0], grad_in, g_conv_all, decay_sum[:, 0], decay_sum[:, 1], sums[-1], grad_out,
        gain_sum[1], grad_gate_up, grad_down
    )


def solution(mesh):
    tokens = P("fsdp", "tp", None)
    rows = P("tp", "fsdp")
    split = P("fsdp", None, "tp")
    return jax.shard_map(
        local,
        mesh=mesh,
        in_specs=(tokens, P(), P(), tokens, P(), tokens, P(), P(), P(), P(), rows, P(), split, rows),
        out_specs=(tokens, tokens, P(), tokens, P(), P(), P(), P(), rows, P(), split, rows),
        check_vma=False,
    )
```

```python
import functools

import jax
import jax.numpy as jnp
from jax import lax
from jax.experimental import pallas as pl
from jax.experimental.pallas import tpu as pltpu
from jax.sharding import PartitionSpec as P

HD = 128
NH = 2
SPAN = 64
SUB = SPAN * NH
TAPS = 4
SMALL = 16
UNITS = 6 * HD + SMALL
EPS_NORM = 1e-05
EPS_UNIT = 1e-06
F32 = jnp.float32
BF16 = jnp.bfloat16
FAR = -1e30
VMEM_BYTES = 56 * 1024 * 1024
EXACT = lax.Precision.HIGHEST


def params(**kw):
    return pltpu.CompilerParams(vmem_limit_bytes=VMEM_BYTES, **kw)


def cost(flops, nbytes, trans=0):
    return pl.CostEstimate(flops=int(flops), bytes_accessed=int(nbytes), transcendentals=int(trans))


def nn(a, b):
    return lax.dot_general(a, b, (((1,), (0,)), ((), ())), preferred_element_type=F32)


def nt(a, b):
    return lax.dot_general(a, b, (((1,), (1,)), ((), ())), preferred_element_type=F32)


def tn(a, b):
    return lax.dot_general(a, b, (((0,), (0,)), ((), ())), preferred_element_type=F32)


def exact_nn(a, b):
    return lax.dot_general(a, b, (((1,), (0,)), ((), ())), precision=EXACT, preferred_element_type=F32)


def sigmoid(v):
    return 1.0 / (1.0 + jnp.exp(-v))


def sides(pieces, bit):
    return [p for p in range(pieces) if not p & bit], [p for p in range(pieces) if p & bit]


def stacks(pieces, shape):
    return [jax.ShapeDtypeStruct((pieces // 2,) + shape, BF16)] * 2


def add_kernel(count, *refs):
    ins, outs = refs[: 2 * count], refs[2 * count :]
    for i in range(count):
        for j in range(2):
            outs[2 * i + j][...] = (ins[2 * i][j].astype(F32) + ins[2 * i + 1][j].astype(F32)).astype(BF16)


def add_stacks(pairs):
    flat = [v for pair in pairs for v in pair]
    steps = 3
    blocks = [pl.BlockSpec((2, v.shape[1] // steps, v.shape[2]), lambda i: (0, i, 0)) for v in flat]
    single = [pl.BlockSpec((v.shape[1] // steps, v.shape[2]), lambda i: (i, 0)) for v in flat]
    res = pl.pallas_call(
        functools.partial(add_kernel, len(pairs)),
        out_shape=[jax.ShapeDtypeStruct(v.shape[1:], BF16) for v in flat],
        grid=(steps,),
        in_specs=blocks,
        out_specs=single,
        compiler_params=params(),
        cost_estimate=cost(1e6, 1e6),
        name="add_stacks",
    )(*flat)
    return [res[2 * i : 2 * i + 2] for i in range(len(pairs))]


def lane_sum(value):
    return jnp.sum(value, axis=-1, keepdims=True)


def conv_shifts(ref, start, rows, lanes):
    window = ref[start : start + rows + 8, lanes]
    views = [pltpu.roll(window, TAPS - 1 - j, 0)[8 : 8 + rows] for j in range(TAPS - 1)]
    return views + [window[8 : 8 + rows]]


def conv_shifts_back(ref, start, rows, lanes):
    window = ref[start : start + rows + 8, lanes]
    views = [pltpu.roll(window, rows + 8 - (TAPS - 1 - j), 0)[:rows] for j in range(TAPS - 1)]
    return views + [window[:rows]]


def iota(shape, dim):
    return lax.broadcasted_iota(jnp.int32, shape, dim)


def project_kernel(pieces, h, scal_ref, a_ref, cw_ref, *refs):
    parts = refs[:pieces]
    raw_ref, gate_ref, q_ref, k_ref, v_ref, rows_ref, raw_s, mix_s, aux_s = refs[pieces:]
    tile = a_ref.shape[0]
    depth = parts[0].shape[1]
    head = 8

    @pl.when(pl.program_id(0) == 0)
    def _():
        raw_s[0:head, :] = jnp.zeros_like(raw_s[0:head, :])

    @pl.when(pl.program_id(0) > 0)
    def _():
        raw_s[0:head, :] = raw_s[tile : tile + head, :]

    acc = jnp.zeros((tile, UNITS), F32)
    for p in range(pieces):
        acc += nt(a_ref[:, p * depth : (p + 1) * depth], parts[p][HD:])
    raw_s[head : tile + head, :] = acc[:, : 5 * HD]
    raw_ref[...] = acc[:, : 5 * HD].astype(BF16)
    gate_ref[...] = acc[:, 5 * HD : 6 * HD].astype(BF16)

    small = acc[:, 6 * HD :]
    rate, bias = scal_ref[h, 0], scal_ref[h, 1]
    arg = small[:, 2:3] + bias
    soft = jnp.maximum(arg, 0.0) + jnp.log(1.0 + jnp.exp(-jnp.abs(arg)))
    beta = sigmoid(small[:, 0:2])
    lane = iota((tile, HD), 1)
    aux_s[pl.ds(0, tile, 2), :] = jnp.where(
        lane == 0, beta[:, 0:1], jnp.where(lane == 1, -rate * soft, jnp.where(lane == 2, arg, 0.0))
    )
    aux_s[pl.ds(1, tile, 2), :] = jnp.where(lane == 0, beta[:, 1:2], 0.0)
    upper = jnp.where(iota((SUB, SUB), 0) <= iota((SUB, SUB), 1), 1.0, 0.0)
    for b in range(tile // SPAN):
        rows = jnp.transpose(aux_s[b * SUB : (b + 1) * SUB, :])[:8]
        cum = exact_nn(rows, upper)
        rows_ref[b] = jnp.where(iota((8, SUB), 0) == 3, cum[1:2], rows)

    chunk = 64
    for g in range(5):
        taps = cw_ref[0, :, g * HD : (g + 1) * HD]
        for i in range(tile // chunk):
            start = i * chunk
            views = conv_shifts(raw_s, start, chunk, slice(g * HD, (g + 1) * HD))
            pre = views[0] * taps[0:1]
            for j in range(1, TAPS):
                pre += views[j] * taps[j : j + 1]
            act = pre * sigmoid(pre)
            if g < 3:
                act = act * lax.rsqrt(lane_sum(act * act) + EPS_UNIT)
            if g == 0:
                q_ref[start : start + chunk, :] = act.astype(BF16)
            else:
                mix_s[pl.ds(2 * start + (g + 1) % 2, chunk, 2), :] = act
        if g in (2, 4):
            (k_ref if g == 2 else v_ref)[...] = mix_s[...].astype(BF16)


def project(h, normed, parts, conv_t, scal):
    seq, dim = normed.shape
    pieces = len(parts)
    tile = min(256, seq)
    fix = lambda i: (0, 0)
    along = lambda i: (i, 0)
    outs = [((seq, 5 * HD), BF16, 1), ((seq, HD), BF16, 1), ((seq, HD), BF16, 1), ((NH * seq, HD), BF16, NH), ((NH * seq, HD), BF16, NH)]
    return pl.pallas_call(
        functools.partial(project_kernel, pieces, h),
        out_shape=[jax.ShapeDtypeStruct(s, d) for s, d, _ in outs] + [jax.ShapeDtypeStruct((seq // SPAN, 8, SUB), F32)],
        grid=(seq // tile,),
        in_specs=[
            pl.BlockSpec(memory_space=pltpu.SMEM),
            pl.BlockSpec((tile, dim), along),
            pl.BlockSpec((1,) + conv_t.shape[1:], lambda i: (h, 0, 0)),
        ]
        + [pl.BlockSpec(w.shape, fix) for w in parts],
        out_specs=[pl.BlockSpec((tile * n, s[1]), along) for s, _, n in outs]
        + [pl.BlockSpec((tile // SPAN, 8, SUB), lambda i: (i, 0, 0))],
        scratch_shapes=[
            pltpu.VMEM((tile + 8, 5 * HD), F32),
            pltpu.VMEM((NH * tile, HD), F32),
            pltpu.VMEM((NH * tile, HD), F32),
        ],
        compiler_params=params(),
        cost_estimate=cost(2 * seq * dim * UNITS, 8e6),
        name="project",
    )(scal, normed, conv_t, *parts)


BASE = 16


def unit_lower_inverses(lowers):
    n, groups = SUB, SUB // BASE
    lane = iota((BASE, n), 1)
    group = lane // BASE
    packed = []
    for low in lowers:
        p = jnp.where(group == 0, low[:BASE], 0.0)
        for b in range(1, groups):
            p = jnp.where(group == b, low[b * BASE : (b + 1) * BASE], p)
        packed.append(p)
    eye = jnp.where(lane % BASE == iota((BASE, n), 0), 1.0, 0.0)
    invs = [eye] * len(lowers)
    first = group * BASE
    for j in range(BASE - 1):
        coefs = [jnp.take_along_axis(p, first + j, axis=1) for p in packed]
        invs = [x - c * x[j : j + 1] for x, c in zip(invs, coefs)]
    fulls = [
        jnp.concatenate([jnp.where(group == b, x, 0.0).astype(BF16) for b in range(groups)], axis=0) for x in invs
    ]
    row, col = iota((n, n), 0), iota((n, n), 1)
    size = BASE
    while size < n:
        odd = range(1, n // size, 2)
        mask = jnp.logical_and(row // size == col // size + 1, row // (2 * size) == col // (2 * size))
        crosses = [jnp.where(mask, low, 0.0).astype(BF16) for low in lowers]
        picks = [jnp.concatenate([f[b * size : (b + 1) * size] for b in odd], axis=0) for f in fulls]
        halves = [nn(p, c).astype(BF16) for p, c in zip(picks, crosses)]
        belows = [(p.astype(F32) - nn(h, f)).astype(BF16) for p, h, f in zip(picks, halves, fulls)]
        fulls = [
            jnp.concatenate(
                [
                    below[(b // 2) * size : (b // 2 + 1) * size] if b % 2 else f[b * size : (b + 1) * size]
                    for b in range(n // size)
                ],
                axis=0,
            )
            for f, below in zip(fulls, belows)
        ]
        size *= 2
    return fulls


def turned(value, eye):
    return nt(eye, value)


def decay_terms(rows_ref, cums, items):
    out = []
    pick_row = iota((8, SUB), 0)
    for i, (b, h) in enumerate(items):
        rows = rows_ref[h][b]
        g = rows[3:4, :]
        g_last = g[:, SUB - 1 :]
        e = jnp.exp(g)
        wide = jnp.where(pick_row == 1, e, jnp.where(pick_row == 2, jnp.exp(g_last - g), rows))
        wide = jnp.where(pick_row == 4, rows[0:1, :] * e, wide)
        cols = jnp.transpose(jnp.concatenate([wide] * (SUB // 8), axis=0))
        cums[i] = cols
        c_col = cums[i, pl.ds(1, SPAN, 2), :][:, 3:4]
        out.append((cols[:, 0:1], cols[:, 1:2], cols[:, 2:3], cols[:, 3:4], cols[:, 4:5], g, c_col, g_last))
    return out


PER_STEP = 2


def recur_kernel(heads, more, gain_ref, start_ref, *refs):
    q_r, k_r, v_r, g_r, rows_r = (refs[i * heads : (i + 1) * heads] for i in range(5))
    refs = refs[: 5 * heads] + refs[5 * heads + more :]
    z_ref, end_ref = refs[5 * heads : 5 * heads + 2]
    o_r = refs[5 * heads + 2 : 6 * heads + 2]
    u_r = refs[6 * heads + 2 : 7 * heads + 2]
    s_ref, t_ref, cums = refs[7 * heads + 2 :]

    @pl.when(pl.program_id(0) == 0)
    def _():
        end_ref[...] = start_ref[...]

    row, col = iota((SUB, SUB), 0), iota((SUB, SUB), 1)
    strict = col < row
    vis = iota((SPAN, SUB), 1) // NH <= iota((SPAN, SUB), 0)
    items = [(b, h) for b in range(PER_STEP) for h in range(heads)]
    tok = [pl.ds(b * SPAN, SPAN) for b, _ in items]
    sub = [pl.ds(b * SUB, SUB) for b, _ in items]
    eye = jnp.where(row == col, 1.0, 0.0).astype(BF16)
    terms = decay_terms(rows_r, cums, items)
    ks = [k_r[h][sub[i]] for i, (b, h) in enumerate(items)]
    qs = [q_r[h][tok[i]] for i, (b, h) in enumerate(items)]
    prods = [nt(jnp.concatenate([k, q], axis=0), k) for k, q in zip(ks, qs)]
    lowers = [
        t[0] * jnp.exp(jnp.where(strict, t[3] - t[5], FAR)) * p[:SUB] for p, t in zip(prods, terms)
    ]
    inner = [(jnp.exp(jnp.where(vis, t[6] - t[5], FAR)) * p[SUB:]).astype(BF16) for p, t in zip(prods, terms)]
    inverses = unit_lower_inverses(lowers)
    for (b, h), inv in zip(items, inverses):
        t_ref[b, h] = inv
    solved, backs = [], []
    for i, (b, h) in enumerate(items):
        t = terms[i]
        k = ks[i].astype(F32)
        right = jnp.concatenate([t[0] * v_r[h][sub[i]].astype(F32), t[4] * k], axis=1)
        solved.append(nn(inverses[i], right.astype(BF16)))
        weighted = turned((t[2] * k).astype(BF16), eye).astype(BF16)
        backs.append(jnp.concatenate([weighted, inner[i]], axis=0))
    gain = gain_ref[...]
    for b in range(PER_STEP):
        mine = [i for i, it in enumerate(items) if it[0] == b]
        olds = [end_ref[items[i][1]] for i in mine]
        old_bs = [o.astype(BF16) for o in olds]
        reads = [
            nn(jnp.concatenate([solved[i][:, HD:].astype(BF16), qs[i]], axis=0), ob) for i, ob in zip(mine, old_bs)
        ]
        ubs = [(solved[i][:, :HD] - r[:SUB]).astype(BF16) for i, r in zip(mine, reads)]
        adds = [nn(backs[i], ub) for i, ub in zip(mine, ubs)]
        for i, old, ob, r, ub, add in zip(mine, olds, old_bs, reads, ubs, adds):
            h = items[i][1]
            c_col, g_last = terms[i][6:]
            end_ref[h] = jnp.exp(g_last) * old + add[:HD]
            s_ref[b, h] = ob
            u_r[h][sub[i], :] = ub
            o = jnp.exp(c_col) * r[SUB:] + add[HD:]
            o_r[h][tok[i], :] = o.astype(BF16)
            scaled = o * lax.rsqrt(jnp.mean(o * o, axis=-1, keepdims=True) + EPS_NORM) * gain
            gate = g_r[h][tok[i]].astype(F32)
            z_ref[tok[i], h * HD : (h + 1) * HD] = (scaled * gate * sigmoid(gate)).astype(BF16)


def recur_specs(heads, at):
    tok = pl.BlockSpec((PER_STEP * SPAN, HD), lambda i: (at(i), 0))
    sub = pl.BlockSpec((PER_STEP * SUB, HD), lambda i: (at(i), 0))
    rows = pl.BlockSpec((PER_STEP, 8, SUB), lambda i: (at(i), 0, 0))
    wide = pl.BlockSpec((PER_STEP * SPAN, heads * HD), lambda i: (at(i), 0))
    mat = pl.BlockSpec((PER_STEP, heads, HD, HD), lambda i: (at(i), 0, 0, 0))
    one = pl.BlockSpec((1, HD), lambda i: (0, 0))
    state = pl.BlockSpec((heads, HD, HD), lambda i: (0, 0, 0))
    return tok, sub, rows, wide, mat, one, state


def recur(gain, start, q, k, v, gate, rows, first, steps, z=None):
    heads = len(q)
    tok, sub, row, wide, mat, one, state = recur_specs(heads, lambda i: i + first)
    o_tok, o_sub, _, _, o_mat, _, _ = recur_specs(heads, lambda i: i)
    n = steps * PER_STEP
    more = [] if z is None else [z]

    def shape(s, d):
        return jax.ShapeDtypeStruct(s, d)

    res = pl.pallas_call(
        functools.partial(recur_kernel, heads, len(more)),
        out_shape=[shape((q[0].shape[0], heads * HD), BF16), shape((heads, HD, HD), F32)]
        + [shape((n * SPAN, HD), BF16)] * heads
        + [shape((n * SUB, HD), BF16)] * heads
        + [shape((n, heads, HD, HD), BF16)] * 2,
        grid=(steps,),
        in_specs=[one, state]
        + [tok] * heads
        + [sub] * (2 * heads)
        + [tok] * heads
        + [row] * heads
        + [pl.BlockSpec(memory_space=pl.ANY)] * len(more),
        out_specs=[wide, state] + [o_tok] * heads + [o_sub] * heads + [o_mat] * 2,
        scratch_shapes=[pltpu.VMEM((PER_STEP * heads, SUB, SUB), F32)],
        compiler_params=params(),
        input_output_aliases={2 + 5 * heads: 0} if more else {},
        cost_estimate=cost(heads * n * 20 * 4.2e6, 1e6),
        name="recur",
    )(gain, start, *q, *k, *v, *gate, *rows, *more)
    return res[0], res[1], res[2 : 2 + heads], res[2 + heads : 2 + 2 * heads], res[2 + 2 * heads], res[3 + 2 * heads]


def recur_back_kernel(heads, more, gain_ref, start_ref, dz_ref, *refs):
    q_r, k_r, v_r, g_r, rows_r, o_r, u_r = (refs[i * heads : (i + 1) * heads] for i in range(7))
    s_ref, t_ref = refs[7 * heads : 7 * heads + 2]
    refs = refs[: 7 * heads + 2] + refs[7 * heads + 2 + more :]
    d_r = refs[7 * heads + 2 : 8 * heads + 2]
    drows_r = refs[8 * heads + 2 : 9 * heads + 2]
    dgain_ref, end_ref, cums, mixed = refs[9 * heads + 2 :]

    @pl.when(pl.program_id(0) == 0)
    def _():
        end_ref[...] = start_ref[...]
        dgain_ref[...] = jnp.zeros_like(dgain_ref)

    row, col = iota((SUB, SUB), 0), iota((SUB, SUB), 1)
    strict = col < row
    later = jnp.where(row >= col, 1.0, 0.0)
    vis = iota((SPAN, SUB), 1) // NH <= iota((SPAN, SUB), 0)
    gain = gain_ref[...]
    items = [(b, h) for b in reversed(range(PER_STEP)) for h in range(heads)]
    every = range(len(items))
    tok = [pl.ds(b * SPAN, SPAN) for b, _ in items]
    sub = [pl.ds(b * SUB, SUB) for b, _ in items]
    terms = decay_terms(rows_r, cums, items)
    ks = [k_r[h][sub[i]] for i, (b, h) in enumerate(items)]
    qs = [q_r[h][tok[i]] for i, (b, h) in enumerate(items)]
    us = [u_r[h][sub[i]] for i, (b, h) in enumerate(items)]
    ss = [s_ref[b, h] for b, h in items]
    prods = [nt(jnp.concatenate([k, q], axis=0), k) for k, q in zip(ks, qs)]

    dos = []
    dgain = jnp.zeros((1, HD), F32)
    for i, (b, h) in enumerate(items):
        dz = dz_ref[tok[i], h * HD : (h + 1) * HD].astype(F32)
        o = o_r[h][tok[i]].astype(F32)
        gate = g_r[h][tok[i]].astype(F32)
        inv_rms = lax.rsqrt(jnp.mean(o * o, axis=-1, keepdims=True) + EPS_NORM)
        n = o * inv_rms
        sg = sigmoid(gate)
        dy = dz * gate * sg
        d_r[h][tok[i], 5 * HD :] = (dz * n * gain * sg * (1.0 + gate * (1.0 - sg))).astype(BF16)
        dgain += jnp.sum(dy * n, axis=0, keepdims=True)
        dn = dy * gain
        dos.append((inv_rms * (dn - n * jnp.mean(dn * n, axis=-1, keepdims=True))).astype(BF16))
    dgain_ref[...] += dgain

    eye = jnp.where(row == col, 1.0, 0.0).astype(BF16)
    reads = [jnp.exp(jnp.where(vis, t[6] - t[5], FAR)) for t in terms]
    ecs = [jnp.exp(t[6]) for t in terms]
    kfs = [k.astype(F32) for k in ks]
    qfs = [q.astype(F32) for q in qs]
    lefts = [
        jnp.concatenate([turned((p[SUB:] * r).astype(BF16), eye).astype(BF16), (t[2] * k).astype(BF16)], axis=1)
        for p, r, t, k in zip(prods, reads, terms, kfs)
    ]
    downs = [
        turned(jnp.concatenate([(ec * q).astype(BF16), (-t[4] * k).astype(BF16)], axis=0), eye).astype(BF16)
        for ec, q, t, k in zip(ecs, qfs, terms, kfs)
    ]
    solves = [turned(t_ref[b, h], eye).astype(BF16) for b, h in items]

    drs, dsbs, dots = [None] * len(items), [None] * len(items), [None] * len(items)
    for b in reversed(range(PER_STEP)):
        mine = [i for i, it in enumerate(items) if it[0] == b]
        dss = {i: end_ref[items[i][1]] for i in mine}
        for i in mine:
            dsbs[i] = dss[i].astype(BF16)
            dots[i] = jnp.sum(dss[i] * ss[i].astype(F32), axis=0, keepdims=True)
        dus = {i: nn(lefts[i], jnp.concatenate([dos[i], dsbs[i]], axis=0)).astype(BF16) for i in mine}
        for i in mine:
            drs[i] = nn(solves[i], dus[i])
        for i in mine:
            add = nn(downs[i], jnp.concatenate([dos[i], drs[i].astype(BF16)], axis=0))
            end_ref[items[i][1]] = jnp.exp(terms[i][7]) * dss[i] + add

    drbs = [d.astype(BF16) for d in drs]
    from_s = [nt(jnp.concatenate([a, c], axis=0), s) for a, c, s in zip(drbs, dos, ss)]
    from_u = [nt(jnp.concatenate([a, c], axis=0), u) for a, c, u in zip(drbs, dos, us)]
    ks0 = [nn(k, s) for k, s in zip(ks, ss)]
    dws = [nt(u, d) for u, d in zip(us, dsbs)]
    dgs, dbs, dks, minus, dcs, syms = [], [], [], [], [], []
    nms = []
    for i, (b, h) in enumerate(items):
        beta, e_col, e_rest, g_col, beta_e, g_row, c_col, g_last = terms[i]
        k, q = kfs[i], qfs[i]
        mixed[i] = beta * drs[i]
        d_r[h][tok[i], 3 * HD : 4 * HD] = mixed[i, pl.ds(0, SPAN, 2), :].astype(BF16)
        d_r[h][tok[i], 4 * HD : 5 * HD] = mixed[i, pl.ds(1, SPAN, 2), :].astype(BF16)
        t1 = beta_e * from_s[i][:SUB]
        t3 = e_rest * dws[i]
        fade = jnp.exp(jnp.where(strict, g_col - g_row, FAR))
        y = -from_u[i][:SUB] * fade
        le = y * prods[i][:SUB]
        hh = beta * le
        kt3 = k * t3
        dbs.append(lane_sum(drs[i] * (v_r[h][sub[i]].astype(F32) - e_col * ks0[i]) + le))
        dg = lane_sum(hh - k * t1 - kt3)
        d_last = lane_sum(jnp.sum(kt3, axis=0, keepdims=True) + jnp.exp(g_last) * dots[i])
        dgs.append(dg + jnp.where(row[:, :1] == SUB - 1, d_last, 0.0))
        dks.append(t3 - t1)
        dkk = beta * y
        syms.append(dkk + turned(dkk.astype(BF16), eye))
        nm = from_u[i][SUB:] * reads[i]
        hm = nm * prods[i][SUB:]
        t2 = ecs[i] * from_s[i][SUB:]
        nms.append((nm.astype(BF16), t2))
        dcs.append(lane_sum(hm + q * t2))
        minus.append(jnp.sum(hh, axis=0, keepdims=True) + jnp.sum(hm, axis=0, keepdims=True))
    tops = [
        nn(jnp.concatenate([s.astype(BF16), nm], axis=0), k) for s, (nm, _), k in zip(syms, nms, ks)
    ]
    turns = [nn(turned(nm, eye).astype(BF16), q) for (nm, _), q in zip(nms, qs)]
    for i, (b, h) in enumerate(items):
        d_r[h][tok[i], :HD] = (tops[i][SUB:] + nms[i][1]).astype(BF16)
        mixed[i] = dks[i] + tops[i][:SUB] + turns[i]
        d_r[h][tok[i], HD : 2 * HD] = mixed[i, pl.ds(0, SPAN, 2), :].astype(BF16)
        d_r[h][tok[i], 2 * HD : 3 * HD] = mixed[i, pl.ds(1, SPAN, 2), :].astype(BF16)
        cums[i] = jnp.where(col == 0, dbs[i], jnp.where(col == 1, dgs[i], 0.0))
        odd = pl.ds(1, SPAN, 2)
        cums[i, odd, :] = cums[i, odd, :] + jnp.where(col[:SPAN] == 1, dcs[i], 0.0)
        rows = jnp.transpose(cums[i])[:8]
        first = iota((8, SUB), 0)
        summed = exact_nn(rows - jnp.where(first == 1, minus[i], 0.0), later)
        drows_r[h][b] = jnp.where(first == 0, rows, summed)


def recur_back(gain, start, dz, q, k, v, gate, rows, o, u, s, t, first, steps, done=()):
    heads = len(q)
    tok, sub, row, wide, mat, one, state = recur_specs(heads, lambda i: first + steps - 1 - i)
    o_tok, o_sub, _, _, o_mat, _, _ = recur_specs(heads, lambda i: steps - 1 - i)
    n = steps * PER_STEP
    seq = q[0].shape[0]
    d_spec = pl.BlockSpec((PER_STEP * SPAN, 6 * HD), lambda i: (first + steps - 1 - i, 0))

    def shape(s, d):
        return jax.ShapeDtypeStruct(s, d)

    res = pl.pallas_call(
        functools.partial(recur_back_kernel, heads, len(done)),
        out_shape=[shape((seq, 6 * HD), BF16)] * heads
        + [shape((seq // SPAN, 8, SUB), F32)] * heads
        + [shape((1, HD), F32), shape((heads, HD, HD), F32)],
        grid=(steps,),
        in_specs=[one, state, wide]
        + [tok] * heads
        + [sub] * (2 * heads)
        + [tok] * heads
        + [row] * heads
        + [o_tok] * heads
        + [o_sub] * heads
        + [o_mat] * 2
        + [pl.BlockSpec(memory_space=pl.ANY)] * len(done),
        out_specs=[d_spec] * heads + [row] * heads + [one, state],
        scratch_shapes=[pltpu.VMEM((PER_STEP * heads, SUB, SUB), F32)] * 2,
        compiler_params=params(),
        input_output_aliases={5 + 7 * heads + i: i for i in range(len(done))},
        cost_estimate=cost(heads * n * 30 * 4.2e6, 1e6),
        name="recur_back",
    )(gain, start, dz, *q, *k, *v, *gate, *rows, *o, *u, s, t, *done)
    return res[:heads], res[heads : 2 * heads], res[2 * heads], res[2 * heads + 1]


def project_back_kernel(pieces, bit, h, scal_ref, a_ref, cw_ref, raw_ref, rows_ref, d_ref, drow_ref, *refs):
    outer, refs = refs[:pieces], refs[pieces:]
    dp_ref, dcw_ref, dsm_ref = refs[:3]
    stacked = refs[3:5]
    raw_s, ds_s, acc, aux_s = refs[5:]
    tile = a_ref.shape[0]
    depth = outer[0].shape[1]
    chunk = 64
    step, steps = pl.program_id(0), pl.num_programs(0)
    base = pl.multiple_of((steps - 1 - step) * tile, tile)

    @pl.when(step == 0)
    def _():
        ds_s[tile : tile + 8, :] = jnp.zeros_like(ds_s[tile : tile + 8, :])
        dcw_ref[...] = jnp.zeros_like(dcw_ref)
        dsm_ref[...] = jnp.zeros_like(dsm_ref)

    @pl.when(step > 0)
    def _():
        ds_s[tile : tile + 8, :] = ds_s[0:8, :]

    @pl.when(step == steps - 1)
    def _():
        raw_s[0:8, :] = jnp.zeros_like(raw_s[0:8, :])

    @pl.when(step < steps - 1)
    def _():
        before = raw_ref[pl.ds(pl.multiple_of(base - 16, 16), 16), :].astype(F32)
        raw_s[0:8, :] = before[8:]

    raw_s[8 : tile + 8, :] = raw_ref[pl.ds(base, tile), :].astype(F32)
    for g in range(5):
        lanes = slice(g * HD, (g + 1) * HD)
        taps = cw_ref[0, :, lanes]
        sums = [jnp.zeros((8, HD), F32)] * TAPS
        for i in range(tile // chunk):
            start = i * chunk
            shifted = conv_shifts(raw_s, start, chunk, lanes)
            pre = shifted[0] * taps[0:1]
            for j in range(1, TAPS):
                pre = pre + shifted[j] * taps[j : j + 1]
            sg = sigmoid(pre)
            act = pre * sg
            d = d_ref[start : start + chunk, lanes].astype(F32)
            if g < 3:
                inv = lax.rsqrt(lane_sum(act * act) + EPS_UNIT)
                unit = act * inv
                d = inv * (d - unit * lane_sum(d * unit))
            d = d * (sg + act * (1.0 - sg))
            ds_s[start : start + chunk, lanes] = d
            sums = [s + jnp.sum((d * x).reshape(chunk // 8, 8, HD), axis=0) for s, x in zip(sums, shifted)]
        for j in range(TAPS):
            dcw_ref[j : j + 1, lanes] += jnp.sum(sums[j], axis=0, keepdims=True)
        for i in range(tile // chunk):
            start = i * chunk
            views = conv_shifts_back(ds_s, start, chunk, lanes)
            total = views[0] * taps[0:1]
            for j in range(1, TAPS):
                total = total + views[j] * taps[j : j + 1]
            dp_ref[start : start + chunk, lanes] = total.astype(BF16)

    rate = scal_ref[h, 0]
    lane = iota((SPAN, HD), 1)
    total = jnp.zeros((8, HD), F32)
    for b in range(tile // SPAN):
        both = jnp.concatenate([rows_ref[b], drow_ref[b]] + [jnp.zeros((8, SUB), F32)] * (SUB // 8 - 2), axis=0)
        aux_s[b] = jnp.transpose(both)
        even, odd = aux_s[b, pl.ds(0, SPAN, 2), :], aux_s[b, pl.ds(1, SPAN, 2), :]
        b1, b2, dg = even[:, 0:1], odd[:, 0:1], even[:, 9:10]
        darg = -rate * dg * sigmoid(even[:, 2:3])
        d1 = even[:, 8:9] * b1 * (1.0 - b1)
        d2 = odd[:, 8:9] * b2 * (1.0 - b2)
        vals = jnp.where(lane == 0, d1, jnp.where(lane == 1, d2, jnp.where(lane == 2, darg, 0.0)))
        here = pl.ds(b * SPAN, SPAN)
        dp_ref[here, 6 * HD :] = vals[:, :SMALL].astype(BF16)
        dp_ref[here, 5 * HD : 6 * HD] = d_ref[here, 5 * HD :]
        extra = jnp.where(lane == 0, dg * even[:, 1:2], jnp.where(lane == 1, darg, 0.0))
        total += jnp.sum(extra.reshape(SPAN // 8, 8, HD), axis=0)
    dsm_ref[...] += total

    term = tn(dp_ref[...], a_ref[...])

    @pl.when(step == 0)
    def _():
        acc[...] = term

    @pl.when(step > 0)
    def _():
        acc[...] += term

    @pl.when(step == steps - 1)
    def _():
        for stack, group in zip(stacked, sides(pieces, bit)):
            for i, p in enumerate(group):
                stack[i, :HD] = outer[p][...]
                stack[i, HD:] = acc[:, p * depth : (p + 1) * depth].astype(BF16)


def project_back(h, normed, conv_t, scal, raw, rows, d, drows, outer, bit):
    seq, dim = normed.shape
    pieces = len(outer)
    depth = outer[0].shape[1]
    tile = min(512, seq)
    end = seq // tile - 1
    along = lambda i: (end - i, 0)
    deep = pl.BlockSpec((tile // SPAN, 8, SUB), lambda i: (end - i, 0, 0))
    fix = lambda i: (0, 0)
    outs = [((seq, UNITS), BF16), ((8, 5 * HD), F32), ((8, HD), F32)]
    shapes = [jax.ShapeDtypeStruct(s, t) for s, t in outs] + stacks(pieces, (HD + UNITS, depth))
    res = pl.pallas_call(
        functools.partial(project_back_kernel, pieces, bit, h),
        out_shape=shapes,
        grid=(seq // tile,),
        in_specs=[
            pl.BlockSpec(memory_space=pltpu.SMEM),
            pl.BlockSpec((tile, dim), along),
            pl.BlockSpec((1,) + conv_t.shape[1:], lambda i: (h, 0, 0)),
            pl.BlockSpec(raw.shape, fix),
            deep,
            pl.BlockSpec((tile, 6 * HD), along),
            deep,
        ]
        + [pl.BlockSpec(g.shape, fix) for g in outer],
        out_specs=[pl.BlockSpec((tile, UNITS), along)]
        + [pl.BlockSpec(s, fix) for s, _ in outs[1:]]
        + [pl.BlockSpec(v.shape, lambda i: (0, 0, 0)) for v in shapes[3:]],
        scratch_shapes=[
            pltpu.VMEM((tile + 8, 5 * HD), F32),
            pltpu.VMEM((tile + 8, 5 * HD), F32),
            pltpu.VMEM((UNITS, dim), F32),
            pltpu.VMEM((tile // SPAN, SUB, SUB), F32),
        ],
        compiler_params=params(),
        cost_estimate=cost(2 * seq * dim * UNITS, 1e6),
        name="project_back",
    )(scal, normed, conv_t, raw, rows, d, drows, *outer)
    return res[0], res[1], res[2], res[3:]


def input_back_kernel(heads, pieces, *refs):
    dps, parts = refs[:heads], refs[heads : heads + heads * pieces]
    x_ref, da_ref, dgain_ref = refs[heads + heads * pieces :]
    depth = parts[0].shape[1]
    x = x_ref[...].astype(F32)
    unit = x * lax.rsqrt(jnp.mean(x * x, axis=-1, keepdims=True) + EPS_NORM)
    shares = []
    for p in range(pieces):
        total = nn(
            jnp.concatenate([d[:, 6 * HD :] for d in dps], axis=1),
            jnp.concatenate([parts[h * pieces + p][7 * HD :] for h in range(heads)], axis=0),
        )
        for h in range(heads):
            total += nn(dps[h][:, : 6 * HD], parts[h * pieces + p][HD : 7 * HD])
        low = total.astype(BF16)
        lanes = slice(p * depth, (p + 1) * depth)
        da_ref[:, lanes] = low
        shares.append(jnp.sum(low.astype(F32) * unit[:, lanes], axis=0, keepdims=True))
    share = jnp.concatenate(shares, axis=1)

    @pl.when(pl.program_id(0) == 0)
    def _():
        dgain_ref[...] = share

    @pl.when(pl.program_id(0) > 0)
    def _():
        dgain_ref[...] += share


def input_back(dps, parts, x):
    seq = dps[0].shape[0]
    heads, pieces = len(parts), len(parts[0])
    flat = [w for head in parts for w in head]
    dim = pieces * flat[0].shape[1]
    tile = min(256, seq)
    along = lambda i: (i, 0)
    return pl.pallas_call(
        functools.partial(input_back_kernel, heads, pieces),
        out_shape=[jax.ShapeDtypeStruct((seq, dim), BF16), jax.ShapeDtypeStruct((1, dim), F32)],
        grid=(seq // tile,),
        in_specs=[pl.BlockSpec((tile, UNITS), along)] * heads
        + [pl.BlockSpec(w.shape, lambda i: (0, 0)) for w in flat]
        + [pl.BlockSpec((tile, dim), along)],
        out_specs=[pl.BlockSpec((tile, dim), along), pl.BlockSpec((1, dim), lambda i: (0, 0))],
        compiler_params=params(),
        cost_estimate=cost(2 * seq * dim * UNITS * heads, 1e6),
        name="input_back",
    )(*dps, *flat, x)


def mix_kernel(heads, pieces, z_ref, *refs):
    parts, out_ref = refs[:-1], refs[-1]
    depth = parts[0].shape[1]
    for p in range(pieces):
        right = jnp.concatenate([parts[h * pieces + p][...] for h in range(heads)], axis=0)
        out_ref[:, p * depth : (p + 1) * depth] = nn(z_ref[...], right).astype(BF16)


def outer_specs(parts):
    return [pl.BlockSpec((HD, w.shape[1]), lambda i: (0, 0)) for head in parts for w in head]


def mix_out(z, parts):
    seq = z.shape[0]
    heads, pieces = len(parts), len(parts[0])
    dim = pieces * parts[0][0].shape[1]
    tile = min(256, seq)
    along = lambda i: (i, 0)
    return pl.pallas_call(
        functools.partial(mix_kernel, heads, pieces),
        out_shape=jax.ShapeDtypeStruct((seq, dim), BF16),
        grid=(seq // tile,),
        in_specs=[pl.BlockSpec((tile, z.shape[1]), along)] + outer_specs(parts),
        out_specs=pl.BlockSpec((tile, dim), along),
        compiler_params=params(),
        cost_estimate=cost(2 * seq * dim * z.shape[1], 1e6),
        name="mix_out",
    )(z, *[w for head in parts for w in head])


def mix_back_kernel(heads, pieces, gain_ref, own_ref, other_ref, mid_ref, dy_ref, z_ref, *refs):
    parts, refs = refs[: heads * pieces], refs[heads * pieces :]
    dmix_ref, dz_ref, dgain_ref = refs[:3]
    grads, acc = refs[3:-1], refs[-1]
    depth = parts[0].shape[1]
    step, steps = pl.program_id(0), pl.num_programs(0)
    mid = mid_ref[...]
    dn = own_ref[...].astype(F32) + other_ref[...].astype(F32)
    inv = lax.rsqrt(jnp.mean(mid * mid, axis=-1, keepdims=True) + EPS_NORM)
    unit = mid * inv
    prod = dn * unit
    share = jnp.sum(prod, axis=0, keepdims=True)
    scaled = dn * gain_ref[...]
    back = inv * (scaled - unit * jnp.mean(prod * gain_ref[...], axis=-1, keepdims=True))
    dmix_ref[...] = (dy_ref[...].astype(F32) + back).astype(BF16)

    @pl.when(step == 0)
    def _():
        dgain_ref[...] = share
        acc[...] = jnp.zeros_like(acc)

    @pl.when(step > 0)
    def _():
        dgain_ref[...] += share

    dz = jnp.zeros((z_ref.shape[0], heads * HD), F32)
    for p in range(pieces):
        lanes = slice(p * depth, (p + 1) * depth)
        right = jnp.concatenate([parts[h * pieces + p][...] for h in range(heads)], axis=0)
        dz += nt(dmix_ref[:, lanes], right)
    acc[...] += tn(z_ref[...], dmix_ref[...])
    dz_ref[...] = dz.astype(BF16)

    @pl.when(step == steps - 1)
    def _():
        for h in range(heads):
            for p in range(pieces):
                grads[h * pieces + p][...] = acc[h * HD : (h + 1) * HD, p * depth : (p + 1) * depth].astype(BF16)


def mix_back(gain, own, other, mid, dy, z, parts):
    seq, dim = mid.shape
    heads, pieces = len(parts), len(parts[0])
    wide = z.shape[1]
    tile = min(256, seq)
    row = pl.BlockSpec((tile, dim), lambda i: (i, 0))
    one = pl.BlockSpec((1, dim), lambda i: (0, 0))
    zs = pl.BlockSpec((tile, wide), lambda i: (i, 0))
    res = pl.pallas_call(
        functools.partial(mix_back_kernel, heads, pieces),
        out_shape=[
            jax.ShapeDtypeStruct((seq, dim), BF16),
            jax.ShapeDtypeStruct((seq, wide), BF16),
            jax.ShapeDtypeStruct((1, dim), F32),
        ]
        + [jax.ShapeDtypeStruct((HD, dim // pieces), BF16)] * (heads * pieces),
        grid=(seq // tile,),
        in_specs=[one, row, row, row, row, zs] + outer_specs(parts),
        out_specs=[row, zs, one] + outer_specs(parts),
        scratch_shapes=[pltpu.VMEM((wide, dim), F32)],
        compiler_params=params(),
        cost_estimate=cost(4 * seq * dim * wide, 1e6),
        name="mix_back",
    )(gain, own, other, mid, dy, z, *[w for head in parts for w in head])
    return res[0], res[1], res[2], [res[3 + h * pieces : 3 + (h + 1) * pieces] for h in range(heads)]


def select_kernel(counts, apart, table_ref, *refs):
    j = pl.program_id(0)
    first = 0
    for g, n in enumerate(counts):
        width = refs[first].shape[2]
        value = refs[first][...]
        for i in range(1, n):
            value = jnp.where(table_ref[2 * g, j] == i, refs[first + i][...], value)
        if apart:
            refs[sum(counts) + g][...] = value
        else:
            refs[-1][:, :, g * width : (g + 1) * width] = value
        first += n


def select_blocks(groups, table, count, apart=False):
    specs, flat = [], []
    for g, sources in enumerate(groups):
        for i, value in enumerate(sources):

            def where(j, t, g=g, i=i):
                return (jnp.where(t[2 * g, j] == i, t[2 * g + 1, j], 0), 0, 0)

            specs.append(pl.BlockSpec((1,) + value.shape[1:], where))
            flat.append(value)
    piece, width = flat[0].shape[1:]
    total = width if apart else width * len(groups)
    outs = len(groups) if apart else 1
    res = pl.pallas_call(
        functools.partial(select_kernel, [len(g) for g in groups], apart),
        out_shape=[jax.ShapeDtypeStruct((count, piece, total), flat[0].dtype)] * outs,
        grid_spec=pltpu.PrefetchScalarGridSpec(
            num_scalar_prefetch=1,
            grid=(count,),
            in_specs=specs,
            out_specs=[pl.BlockSpec((1, piece, total), lambda j, t: (j, 0, 0))] * outs,
        ),
        compiler_params=params(),
        cost_estimate=cost(1e6, 1e6),
        name="select_blocks",
    )(table, *flat)
    return res if apart else res[0]


def ffn_kernel(pieces, chunks, bits, more, b_ref, dy_ref, *refs):
    weights = refs[: pieces * chunks]
    refs = refs[pieces * chunks :]
    sums_in, refs = (refs[:2], refs[2:]) if more else (None, refs)
    out_ref, db_ref = refs[:2]
    stacked = refs[2 : 2 + 2 * chunks]
    b_s, dy_s, hid_s, dg_s, du_s = refs[2 + 2 * chunks :]
    depth = weights[0].shape[1]
    units = weights[0].shape[0] // 3
    tile = b_ref.shape[0]
    step, steps = pl.program_id(0), pl.num_programs(0)

    def weight(p, i):
        return jnp.concatenate(
            [weights[c * pieces + p][i * units : (i + 1) * units] for c in range(chunks)], axis=0
        )

    rows = pl.ds(pl.multiple_of(step * tile, tile), tile)
    b_s[rows, :] = b_ref[...]
    dy_s[rows, :] = dy_ref[...]
    gate = jnp.zeros((tile, units * chunks), F32)
    up = jnp.zeros((tile, units * chunks), F32)
    dh = jnp.zeros((tile, units * chunks), F32)
    for p in range(pieces):
        lanes = slice(p * depth, (p + 1) * depth)
        block, dblock = b_ref[:, lanes], dy_ref[:, lanes]
        gate += nt(block, weight(p, 0))
        up += nt(block, weight(p, 1))
        dh += nt(dblock, weight(p, 2))
    sg = sigmoid(gate)
    act = gate * sg
    hid = (act * up).astype(BF16)
    du = (dh * act).astype(BF16)
    dg = (dh * up * (sg + act * (1.0 - sg))).astype(BF16)
    hid_s[rows, :] = hid
    dg_s[rows, :] = dg
    du_s[rows, :] = du
    for p in range(pieces):
        lanes = slice(p * depth, (p + 1) * depth)
        o = nn(hid, weight(p, 2))
        d = nn(dg, weight(p, 0)) + nn(du, weight(p, 1))
        if more:
            o += sums_in[0][:, lanes].astype(F32)
            d += sums_in[1][:, lanes].astype(F32)
        out_ref[:, lanes] = o.astype(out_ref.dtype)
        db_ref[:, lanes] = d.astype(db_ref.dtype)

    @pl.when(step == steps - 1)
    def _():
        for i, (left, right) in enumerate([(dg_s, b_s), (du_s, b_s), (hid_s, dy_s)]):
            g = tn(left[...], right[...]).astype(BF16)
            for c in range(chunks):
                for stack, group in zip(stacked[2 * c : 2 * c + 2], sides(pieces, bits[c])):
                    for n, p in enumerate(group):
                        stack[n, i * units : (i + 1) * units] = g[
                            c * units : (c + 1) * units, p * depth : (p + 1) * depth
                        ]


def ffn(normed, dy, parts, bits, sums=None, last=True):
    seq, dim = normed.shape
    chunks, pieces = len(parts), len(parts[0])
    flat = [w for chunk in parts for w in chunk]
    units = flat[0].shape[0] // 3
    tile = min(256, seq)
    row = pl.BlockSpec((tile, dim), lambda i: (i, 0))
    more = () if sums is None else tuple(sums)
    grads = stacks(pieces, flat[0].shape) * chunks
    res = pl.pallas_call(
        functools.partial(ffn_kernel, pieces, chunks, bits, bool(more)),
        out_shape=[jax.ShapeDtypeStruct((seq, dim), BF16 if last else F32)] * 2 + grads,
        grid=(seq // tile,),
        in_specs=[row, row] + [pl.BlockSpec(w.shape, lambda i: (0, 0)) for w in flat] + [row] * len(more),
        out_specs=[row, row] + [pl.BlockSpec(g.shape, lambda i: (0, 0, 0)) for g in grads],
        scratch_shapes=[pltpu.VMEM((seq, dim), BF16)] * 2 + [pltpu.VMEM((seq, units * chunks), BF16)] * 3,
        compiler_params=params(),
        cost_estimate=cost(18 * seq * dim * units * chunks, 1e6),
        name="ffn",
    )(normed, dy, *flat, *more)
    return res[0], res[1], [res[2 + 2 * c : 4 + 2 * c] for c in range(chunks)]


def sync(*trees):
    leaves, tree = jax.tree.flatten(trees)
    return jax.tree.unflatten(tree, lax.optimization_barrier(leaves))


def bits_of(n):
    return [1 << i for i in range(n.bit_length() - 1)]


class Place:
    def __init__(self):
        self.n_f = lax.axis_size("fsdp")
        self.n_t = lax.axis_size("tp")
        self.chips = self.n_f // 2
        f = lax.axis_index("fsdp")
        self.f = f
        self.core = f % 2
        self.k = f // 2
        self.t = lax.axis_index("tp")

    def swap(self, value):
        return lax.ppermute(value, "fsdp", [(i, i ^ 1) for i in range(self.n_f)])

    def move(self, value, bit):
        return lax.ppermute(value, "fsdp", [(i, i ^ (2 * bit)) for i in range(self.n_f)])

    def turn(self, value, r):
        return lax.ppermute(value, "tp", [(i, (i + r) % self.n_t) for i in range(self.n_t)])

    def in_order(self, mine, other, axis):
        first = jnp.where(self.core == 0, mine, other)
        second = jnp.where(self.core == 0, other, mine)
        return jnp.concatenate([first, second], axis=axis)

    def halves(self, value, axis):
        size = value.shape[axis] // 2
        return (
            lax.dynamic_slice_in_dim(value, self.core * size, size, axis),
            lax.dynamic_slice_in_dim(value, (1 - self.core) * size, size, axis),
        )

    def relative(self, value):
        width = value.shape[-1] // self.chips
        blocks = [
            lax.dynamic_slice_in_dim(value, (self.k ^ p) * width, width, value.ndim - 1) for p in range(self.chips)
        ]
        return jnp.concatenate(blocks, axis=-1)

    def spread_out(self, value):
        if value.shape[0] < self.n_t:
            value = jnp.pad(value, ((0, self.n_t - value.shape[0]),) + ((0, 0),) * (value.ndim - 1))
        return lax.all_to_all(value, "tp", split_axis=0, concat_axis=0, tiled=True)

    def all_sum(self, value):
        return self.chip_sum(self.line_sum(value))

    def chip_sum(self, value):
        for bit in [1] + [2 * b for b in bits_of(self.chips)]:
            value = value + lax.ppermute(value, "fsdp", [(i, i ^ bit) for i in range(self.n_f)])
        return value

    def line_sum(self, value):
        total = value
        for r in range(1, self.n_t):
            total = total + self.turn(value, r)
        return total

def rms_terms(value):
    return lax.rsqrt(jnp.mean(value * value, axis=-1, keepdims=True) + EPS_NORM)


def rms_back(value, gain, d_normed):
    inv = rms_terms(value)
    unit = value * inv
    dn = d_normed * gain
    return inv * (dn - unit * jnp.mean(dn * unit, axis=-1, keepdims=True))


class Gather:
    def __init__(self, at, shard):
        self.at = at
        self.parts = {(0, 0): shard}

    def turn(self, r, by=None):
        by = by or r
        self.parts[r, 0] = self.at.turn(self.parts[r - by, 0], by)

    def move(self, r, to, via):
        self.parts[r, to] = self.at.move(self.parts[r, to ^ via], via)

    def full(self, r):
        return [self.parts[r, p] for p in range(self.at.chips)]

    def rest(self):
        for r in range(1, self.at.n_t):
            self.turn(r)
        for r in range(self.at.n_t):
            for p in range(1, self.at.chips):
                self.move(r, p, p & -p)
        return [self.full(r) for r in range(self.at.n_t)]


def first_bit(at, r, late=False):
    return at.chips // 2 if r == 3 or (r == 0 and not late) else 1


class Scatter:
    def __init__(self, at, late=False):
        self.at = at
        self.bit = lambda r: first_bit(at, r, late)
        self.near, self.far, self.two, self.one, self.end = {}, {}, {}, {}, {}

    def put(self, r, stacked):
        self.near[r], self.far[r] = stacked

    def cross(self, *turns):
        for r in turns:
            self.far[r] = self.at.move(self.far[r], self.bit(r))

    def add(self, *turns):
        sums = add_stacks([(self.near.pop(r), self.far.pop(r)) for r in turns])
        return dict(zip(turns, sums))

    def pass_on(self, sums):
        for r, (keep, give) in sums.items():
            self.two[r] = keep, self.at.move(give, 3 - self.bit(r))

    def fold(self, *turns):
        self.pass_on(self.add(*turns))

    def close(self, *turns):
        for r in turns:
            keep, came = self.two.pop(r)
            self.one[r] = (keep.astype(F32) + came.astype(F32)).astype(BF16)

    def home(self, r):
        self.end[r] = self.at.turn(self.one.pop(r), self.at.n_t - r)

    def merge(self, r):
        self.end[r] = self.at.turn(self.one.pop(r), self.at.n_t - 1)

    def join(self, r):
        self.one[r - 1] = (self.one[r - 1].astype(F32) + self.end.pop(r).astype(F32)).astype(BF16)

    def total(self):
        return sum(v.astype(F32) for v in list(self.one.values()) + list(self.end.values()))

    def state(self):
        return self.near, self.far, self.two, self.one, self.end

    def take(self, state):
        self.near, self.far, self.two, self.one, self.end = state

    def rest(self):
        for r in range(self.at.n_t):
            have = {}
            for stack, group in zip((self.near.pop(r), self.far.pop(r)), sides(self.at.chips, self.bit(r))):
                have.update({p: stack[i] for i, p in enumerate(group)})
            for bit in bits_of(self.at.chips):
                for p in [p for p in have if p & bit]:
                    came = self.at.move(have.pop(p), bit)
                    have[p ^ bit] = (have[p ^ bit].astype(F32) + came.astype(F32)).astype(BF16)
            self.one[r] = have[0]
            if r:
                self.home(r)


class Routing:
    def __init__(self, at, value, order, source):
        self.at, self.order = at, order
        self.per_chip = value.shape[0]
        self.have, self.where = [value], [0]
        reach = [0]
        for bit in order[:-1]:
            reach += [w | bit for w in reach]
        tables = []
        for chip in (at.k ^ order[-1], at.k):
            ask = lax.dynamic_slice_in_dim(source, chip * self.per_chip, self.per_chip, 0)
            distance = (ask // self.per_chip) ^ at.k
            src = sum(jnp.where(distance == w, i, 0) for i, w in enumerate(reach))
            near = (distance & order[-1]) == 0
            slot = ask % self.per_chip
            if chip is not at.k:
                tables.append((src, slot))
            else:
                tables.append(
                    (
                        jnp.where(near, src, len(reach)),
                        jnp.where(near, slot, jnp.arange(self.per_chip, dtype=jnp.int32)),
                    )
                )
        self.ask, self.keep = (jnp.stack(t) for t in tables)

    def step(self):
        bit = self.order[len(self.where).bit_length() - 1]
        self.have = self.have + [self.at.move(v, bit) for v in self.have]
        self.where = self.where + [w | bit for w in self.where]

    def last(self, give):
        self.have = self.have + [self.at.move(give, self.order[-1])]


def local(
    tokens, lengths, perm, cotangent, norm1_gain, input_weight, conv_w, decay_log, decay_bias, out_gain, w_out,
    norm2_gain, gate_up_weight, down_weight
):
    at = Place()
    slots, piece, dim = tokens.shape
    n_f, n_t, chips = at.n_f, at.n_t, at.chips
    heads_all = conv_w.shape[0]
    heads = heads_all // 2
    local_heads = input_weight.shape[1]
    cols = input_weight.shape[2]
    by_turn = local_heads == 2
    laps = list(range(n_t))
    bits = bits_of(chips)
    fast = by_turn and chips == 4 and n_t == 4
    per_chip = 2 * slots
    seq = n_t * piece
    steps = seq // SPAN // PER_STEP // 2

    pad = SMALL - (cols - 6 * HD)
    if by_turn:
        packed = jnp.transpose(input_weight, (1, 2, 0))
        zeros = jnp.zeros((local_heads, pad, packed.shape[2]), BF16)
        packed = jnp.concatenate([w_out.reshape(local_heads, HD, -1), packed, zeros], axis=1)
        mine, give = at.halves(packed, 0)
        m_own = at.in_order(mine[0], at.swap(give[0]), 1)
        head_ids = ((at.t - jnp.arange(n_t, dtype=jnp.int32)) % n_t) * 2 + at.core
    else:
        m_own = None
        head_ids = at.core * heads + jnp.arange(heads, dtype=jnp.int32)
    mine, give = at.halves(tokens, 2)
    both = at.in_order(mine, at.swap(give), 0)
    both, m_own, gate_up_weight, down_weight, cotangent = sync(both, m_own, gate_up_weight, down_weight, cotangent)
    packed = jnp.concatenate([jnp.transpose(gate_up_weight, (1, 2, 0)), down_weight[None]], axis=0)
    mine, give = at.halves(packed, 1)
    f_own = at.in_order(mine, at.swap(give), 2)
    f_own = f_own.reshape(-1, f_own.shape[2])
    mine, give = at.halves(cotangent, 2)
    cot_both = at.in_order(mine, at.swap(give), 0)

    own = head_ids[:, None] == jnp.arange(heads_all, dtype=jnp.int32)[None, :]
    taps = jnp.pad(jnp.transpose(conv_w, (0, 2, 1)), ((0, 0), (0, 8 - TAPS), (0, 0)))
    conv_t = jnp.sum(jnp.where(own[:, :, None, None], taps[None], 0.0), axis=1)
    scal = jnp.stack(
        [
            jnp.sum(jnp.where(own, jnp.exp(decay_log)[None], 0.0), axis=1),
            jnp.sum(jnp.where(own, decay_bias[None], 0.0), axis=1),
        ],
        axis=1,
    )
    gain1 = at.relative(norm1_gain)
    gain2 = at.relative(norm2_gain)
    gain_o = out_gain[None]
    start_state = jnp.zeros((heads, HD, HD), F32)

    seq_id = jnp.minimum(at.k * per_chip + at.t, lengths.shape[0] - 1)
    length = jnp.where(at.t < per_chip, lax.dynamic_index_in_dim(lengths, seq_id, 0, keepdims=False), 0)
    live = (jnp.arange(seq, dtype=jnp.int32) < length).astype(BF16)[:, None]
    slot_ids = jnp.arange(perm.shape[0], dtype=jnp.int32)
    source = jnp.sum(jnp.where(perm[None, :] == slot_ids[:, None], slot_ids[None, :], 0), axis=1)
    quarter = dim // 4
    routes = [
        Routing(at, cot_both[:, :, :quarter], bits, source),
        Routing(at, cot_both[:, :, quarter:], bits[::-1], source),
    ]

    def route_state():
        return [r.have for r in routes]

    def set_routes(state):
        for r, v in zip(routes, state):
            r.have = v

    def routed():
        groups = [r.have for r in routes]
        return select_blocks(groups, jnp.concatenate([r.keep for r in routes], axis=0), per_chip)

    def sequence(half):
        half = half.reshape(seq, -1)
        return at.relative(at.in_order(half, at.swap(half), 1))

    def norm_first(x):
        return (x * rms_terms(x) * gain1).astype(BF16)

    f = Gather(at, f_own)
    proj = {}

    def asked():
        return select_blocks([r.have for r in routes], jnp.concatenate([r.ask for r in routes], axis=0), per_chip, True)

    if fast:
        m = Gather(at, m_own)

        def run(r):
            proj[r] = project(r, normed_one, m.full(r), conv_t, scal)

        def without(parts, *keys):
            return {k: v for k, v in parts.items() if k not in keys}

        came = at.spread_out(both)
        for p in range(1, chips):
            m.move(0, p, p)
        m.parts, f.parts, came, cot_both, conv_t, scal, gain1, gain2, live, extra = sync(
            m.parts, f.parts, came, cot_both, conv_t, scal, gain1, gain2, live, [(r.ask, r.keep) for r in routes]
        )
        for r, (ask, keep), part in zip(routes, extra, (cot_both[:, :, :quarter], cot_both[:, :, quarter:])):
            r.ask, r.keep, r.have = ask, keep, [part]
        m.turn(1)
        m.turn(3)
        for r in routes:
            r.step()
        x = sequence(came)
        normed_one = norm_first(x.astype(F32))
        run(0)
        state = route_state()
        m.parts, f.parts, state, proj[0], normed_one, x = sync(m.parts, f.parts, state, proj[0], normed_one, x)
        set_routes(state)
        for r in (1, 3):
            m.move(r, 1, 1)
            m.move(r, 2, 2)
        m.turn(2, 1)
        give = asked()
        m.parts, f.parts, give = sync(m.parts, f.parts, give)
        m.move(1, 3, 1)
        m.move(3, 3, 2)
        f.turn(1)
        m.parts, f.parts, give = sync(m.parts, f.parts, give)
        m.move(2, 1, 1)
        m.move(2, 2, 2)
        for r, part in zip(routes, give):
            r.last(part)
        f.turn(3)
        run(1)
        run(3)
        state = route_state()
        m.parts, proj, normed_one, f.parts, state = sync(m.parts, proj, normed_one, f.parts, state)
        set_routes(state)
        m.move(2, 3, 1)
        f.turn(2, 1)
        f.move(0, 1, 1)
        f.move(0, 2, 2)
        cot_home = routed()
        early = without(f.parts, (0, 1), (0, 2))
        m.parts, early, cot_home, normed_one = sync(m.parts, early, cot_home, normed_one)
        f.parts.update(early)
        cot_came = at.spread_out(cot_home)
        f.move(1, 1, 1)
        f.move(1, 2, 2)
        run(2)
        early = without(f.parts, (1, 1), (1, 2))
        proj, early = sync(proj, early)
        f.parts.update(early)
        m_parts = [m.full(r) for r in laps]
    else:
        x = sequence(at.spread_out(both))
        normed_one = norm_first(x.astype(F32))
        if by_turn:
            m_parts = Gather(at, m_own).rest()
        else:
            full = lax.all_gather(lax.all_gather(input_weight, "tp", axis=1, tiled=True), "fsdp", axis=0, tiled=True)
            full = at.relative(jnp.transpose(full, (1, 2, 0)))
            full_out = lax.all_gather(lax.all_gather(w_out, "tp", axis=0, tiled=True), "fsdp", axis=1, tiled=True)
            full_out = at.relative(full_out).reshape(heads_all, HD, dim)
            zeros = jnp.zeros((heads_all, pad, dim), BF16)
            full = at.halves(jnp.concatenate([full_out, full, zeros], axis=1), 0)[0]
            m_parts = [jnp.split(full[h], chips, axis=1) for h in range(heads)]
        for h in range(heads):
            proj[h] = project(h, normed_one, m_parts[h], conv_t, scal)
        for r in routes:
            for _ in bits[1:]:
                r.step()
        for r, part in zip(routes, asked()):
            r.last(part)
        cot_came = at.spread_out(routed())
        f_parts = f.rest()

    raw, gate, q, k, v, rows = (list(group) for group in zip(*[proj[h] for h in range(heads)]))
    if fast:
        f.move(0, 3, 2)
    first = recur(gain_o, start_state, q, k, v, gate, rows, 0, steps)
    if fast:
        first, f.parts, cot_came = sync(first, f.parts, cot_came)
        f.move(1, 3, 1)
        for r in (3, 2):
            f.move(r, 1, 1)
            f.move(r, 2, 2)
    second = recur(gain_o, first[1], q, k, v, gate, rows, steps, steps, first[0])
    if fast:
        early = without(f.parts, (2, 1), (2, 2))
        second, early = sync(second, early)
        f.parts.update(early)
    z = second[0]
    mix = mix_out(z, m_parts)
    mid = x.astype(F32) + (mix.astype(F32) + at.swap(mix).astype(F32))
    normed_two = (mid * rms_terms(mid) * gain2).astype(BF16)
    dy = live * sequence(cot_came)

    f_rs = Scatter(at)
    half = n_t // 2
    group_a, group_b = laps[:half], laps[half:][::-1]
    bits_a, bits_b = [first_bit(at, r) for r in group_a], [first_bit(at, r) for r in group_b]
    if fast:
        normed_two, dy, f.parts = sync(normed_two, dy, f.parts)
        f.move(2, 3, 1)
        f.move(3, 3, 2)
        f_parts = {r: f.full(r) for r in group_a}
    net, db, grads = ffn(normed_two, dy, [f_parts[r] for r in group_a], bits_a, last=False)
    if fast:
        net, db, grads, f.parts = sync(net, db, grads, f.parts)
        f_parts = {r: f.full(r) for r in group_b}
    for r, g in zip(group_a, grads):
        f_rs.put(r, g)
    if fast:
        f_rs.cross(0, 1)
    net, db, grads = ffn(normed_two, dy, [f_parts[r] for r in group_b], bits_b, (net, db))
    if fast:
        net, db, grads, state = sync(net, db, grads, f_rs.state())
        f_rs.take(state)
    for r, g in zip(group_b, grads):
        f_rs.put(r, g)

    db_other = at.swap(db)
    if fast:
        f_rs.fold(0, 1)
        f_rs.cross(3, 2)
    d_mix, dz, g_gain2, g_out = mix_back(gain2[None], db, db_other, mid, dy, z, m_parts)
    if fast:
        dz, d_mix, g_out, f_rs.two, net = sync(dz, d_mix, g_out, f_rs.two, net)
    net_other = at.swap(net)
    back = recur_back(gain_o, start_state, dz, q, k, v, gate, rows, *second[2:], steps, steps)
    if fast:
        back, state, net_other, dz = sync(back, f_rs.state(), net_other, dz)
        f_rs.take(state)
        f_rs.close(0, 1)
        f_rs.fold(3, 2)

    def give_back(value):
        mine = at.halves(at.relative(value.astype(BF16)), 1)[0]
        return mine.reshape(n_t, piece, dim // 2)

    def settle(came):
        mine, give = at.halves(came[:per_chip], 0)
        return at.in_order(mine, at.swap(give), 2)

    g_gain_o = back[2]
    out_home = give_back(live.astype(F32) * (mid + (net.astype(F32) + net_other.astype(F32))))
    out_came = lax.all_to_all(out_home, "tp", split_axis=0, concat_axis=0, tiled=True)
    back = recur_back(
        gain_o, back[3], dz, q, k, v, gate, rows, *first[2:], 0, steps, tuple(back[0]) + tuple(back[1])
    )
    g_gain_o = g_gain_o + back[2]
    ds, drows = back[:2]
    if fast:
        ds, drows, out_came, state = sync(ds, drows, out_came, f_rs.state())
        f_rs.take(state)
        f_rs.close(3, 2)
        f_rs.merge(2)
        f_rs.home(3)

    dps, g_conv, g_small = {}, {}, {}
    m_rs = Scatter(at, late=True)

    def run_back(h):
        dps[h], g_conv[h], g_small[h], grads = project_back(
            h, normed_one, conv_t, scal, raw[h], rows[h], ds[h], drows[h], g_out[h], m_rs.bit(h)
        )
        m_rs.put(h, grads)

    def moved(group, key):
        return {r: v for r, v in group.items() if r == key}

    if fast:
        run_back(2)
        dps, m_rs.near, m_rs.far, ds = sync(dps, m_rs.near, m_rs.far, ds)
        m_rs.cross(2)
        run_back(1)
        dps, m_rs.near, far, ds, f_state = sync(dps, m_rs.near, moved(m_rs.far, 1), ds, f_rs.state())
        m_rs.far.update(far)
        f_rs.take(f_state)
        f_rs.join(2)
        f_rs.home(1)
        m_rs.cross(1)
        run_back(3)
        far = {r: m_rs.far[r] for r in (2, 3)}
        dps, m_rs.near, far, ds = sync(dps, m_rs.near, far, ds)
        m_rs.far.update(far)
        m_rs.fold(2)
        m_rs.cross(3)
        run_back(0)
        far = {r: m_rs.far[r] for r in (0, 1)}
        dps, m_rs.near, far, m_rs.two, f_rs.end = sync(dps, m_rs.near, far, m_rs.two, f_rs.end)
        m_rs.far.update(far)
        m_rs.close(2)
        sums = m_rs.add(1, 3)
        dps, m_rs.one, sums = sync(dps, m_rs.one, sums)
        m_rs.merge(2)
        m_rs.pass_on(sums)
        m_rs.cross(0)
    else:
        for h in range(heads):
            run_back(h)
    output = settle(out_came)
    da, g_gain1 = input_back([dps[h] for h in range(heads)], m_parts, x)
    if fast:
        da, g_gain1, m_rs.two, m_rs.end = sync(da, g_gain1, m_rs.two, m_rs.end)
        m_rs.close(1, 3)
        m_rs.join(2)
        m_rs.home(1)
        m_rs.home(3)
    da_other = at.swap(da)
    d_x_norm = rms_back(x.astype(F32), gain1, da.astype(F32) + da_other.astype(F32))
    dx_home = give_back(d_mix.astype(F32) + d_x_norm)

    small = [jnp.sum(g_small[h], axis=0) for h in range(heads)]
    conv_all = sum(jnp.where(own[h][:, None, None], g_conv[h][None, :TAPS], 0.0) for h in range(heads)).reshape(-1, HD)
    decay_all = sum(jnp.where(own[h][:, None], small[h][None], 0.0) for h in range(heads))
    gains = jnp.concatenate([at.relative(g_gain1[0]), 0.5 * at.relative(g_gain2[0])]).reshape(-1, HD)
    sums = jnp.concatenate([conv_all, decay_all, gains, g_gain_o], axis=0)
    if fast:
        dx_home, sums, m_rs.near, m_rs.end = sync(dx_home, at.line_sum(sums), m_rs.near, m_rs.end)
        m_rs.fold(0)
        sums = at.chip_sum(sums)
    else:
        sums = at.all_sum(sums)
    dx_came = lax.all_to_all(dx_home, "tp", split_axis=0, concat_axis=0, tiled=True)
    if fast:
        dx_came, m_rs.two, m_rs.end = sync(dx_came, m_rs.two, m_rs.end)
        m_rs.close(0)
    input_grad = settle(dx_came)
    n_conv = conv_all.shape[0]
    g_conv_all = jnp.transpose(sums[:n_conv].reshape(heads_all, TAPS, -1), (0, 2, 1))
    decay_sum = sums[n_conv : n_conv + heads_all]
    gain_sum = sums[n_conv + heads_all : -1].reshape(2, dim)

    def to_core(value, joined):
        mine, give = at.halves(value.astype(BF16), value.ndim - 1)
        return at.in_order(mine, at.swap(give), joined).astype(F32)

    if not fast:
        f_rs.rest()
    f_total = f_rs.total()
    g_ffn = to_core(f_total.reshape(3, -1, f_total.shape[1]), 1)
    grad_gate_up = jnp.transpose(g_ffn[:2], (2, 0, 1))
    grad_down = g_ffn[2]
    if by_turn:
        if not fast:
            m_rs.rest()
        joined = to_core(m_rs.total()[None], 0)
    else:
        joined = []
        for h in range(heads):
            have = {}
            for stack, group in zip((m_rs.near[h], m_rs.far[h]), sides(chips, m_rs.bit(h))):
                have.update({p: stack[i] for i, p in enumerate(group)})
            joined.append(jnp.concatenate([have[p] for p in range(chips)], axis=1))
        joined = jnp.stack(joined)
        spread = jnp.zeros((heads_all,) + joined.shape[1:], BF16)
        spread = lax.dynamic_update_slice_in_dim(spread, at.relative(joined), at.core * heads, 0)
        spread = lax.psum_scatter(spread, "tp", scatter_dimension=0, tiled=True)
        joined = lax.psum_scatter(spread, "fsdp", scatter_dimension=2, tiled=True).astype(F32)
    grad_in = jnp.transpose(joined[:, HD : HD + cols], (2, 0, 1))
    grad_out = joined[:, :HD].reshape(local_heads * HD, -1)
    return (
        output, input_grad, gain_sum[0], grad_in, g_conv_all, decay_sum[:, 0], decay_sum[:, 1], sums[-1], grad_out,
        gain_sum[1], grad_gate_up, grad_down
    )


def solution(mesh):
    tokens = P("fsdp", "tp", None)
    rows = P("tp", "fsdp")
    split = P("fsdp", None, "tp")
    return jax.shard_map(
        local,
        mesh=mesh,
        in_specs=(tokens, P(), P(), tokens, P(), tokens, P(), P(), P(), P(), rows, P(), split, rows),
        out_specs=(tokens, tokens, P(), tokens, P(), P(), P(), P(), rows, P(), split, rows),
        check_vma=False,
    )
```

```python
import functools

import jax
import jax.numpy as jnp
from jax import lax
from jax.experimental import pallas as pl
from jax.experimental.pallas import tpu as pltpu
from jax.sharding import PartitionSpec as P

HD = 128
NH = 2
SPAN = 64
SUB = SPAN * NH
TAPS = 4
SMALL = 16
UNITS = 6 * HD + SMALL
EPS_NORM = 1e-05
EPS_UNIT = 1e-06
F32 = jnp.float32
BF16 = jnp.bfloat16
FAR = -1e30
VMEM_BYTES = 56 * 1024 * 1024
EXACT = lax.Precision.HIGHEST


def params(**kw):
    return pltpu.CompilerParams(vmem_limit_bytes=VMEM_BYTES, **kw)


def cost(flops, nbytes, trans=0):
    return pl.CostEstimate(flops=int(flops), bytes_accessed=int(nbytes), transcendentals=int(trans))


def nn(a, b):
    return lax.dot_general(a, b, (((1,), (0,)), ((), ())), preferred_element_type=F32)


def nt(a, b):
    return lax.dot_general(a, b, (((1,), (1,)), ((), ())), preferred_element_type=F32)


def tn(a, b):
    return lax.dot_general(a, b, (((0,), (0,)), ((), ())), preferred_element_type=F32)


def exact_nn(a, b):
    return lax.dot_general(a, b, (((1,), (0,)), ((), ())), precision=EXACT, preferred_element_type=F32)


def sigmoid(v):
    return 1.0 / (1.0 + jnp.exp(-v))


def sides(pieces, bit):
    return [p for p in range(pieces) if not p & bit], [p for p in range(pieces) if p & bit]


def stacks(pieces, shape):
    return [jax.ShapeDtypeStruct((pieces // 2,) + shape, BF16)] * 2


def add_kernel(count, *refs):
    ins, outs = refs[: 2 * count], refs[2 * count :]
    for i in range(count):
        for j in range(2):
            outs[2 * i + j][...] = (ins[2 * i][j].astype(F32) + ins[2 * i + 1][j].astype(F32)).astype(BF16)


def add_stacks(pairs):
    flat = [v for pair in pairs for v in pair]
    steps = 3
    blocks = [pl.BlockSpec((2, v.shape[1] // steps, v.shape[2]), lambda i: (0, i, 0)) for v in flat]
    single = [pl.BlockSpec((v.shape[1] // steps, v.shape[2]), lambda i: (i, 0)) for v in flat]
    res = pl.pallas_call(
        functools.partial(add_kernel, len(pairs)),
        out_shape=[jax.ShapeDtypeStruct(v.shape[1:], BF16) for v in flat],
        grid=(steps,),
        in_specs=blocks,
        out_specs=single,
        compiler_params=params(),
        cost_estimate=cost(1e6, 1e6),
        name="add_stacks",
    )(*flat)
    return [res[2 * i : 2 * i + 2] for i in range(len(pairs))]


def lane_sum(value):
    return jnp.sum(value, axis=-1, keepdims=True)


def conv_shifts(ref, start, rows, lanes):
    window = ref[start : start + rows + 8, lanes]
    views = [pltpu.roll(window, TAPS - 1 - j, 0)[8 : 8 + rows] for j in range(TAPS - 1)]
    return views + [window[8 : 8 + rows]]


def conv_shifts_back(ref, start, rows, lanes):
    window = ref[start : start + rows + 8, lanes]
    views = [pltpu.roll(window, rows + 8 - (TAPS - 1 - j), 0)[:rows] for j in range(TAPS - 1)]
    return views + [window[:rows]]


def iota(shape, dim):
    return lax.broadcasted_iota(jnp.int32, shape, dim)


def project_kernel(pieces, h, scal_ref, a_ref, cw_ref, *refs):
    parts = refs[:pieces]
    raw_ref, gate_ref, q_ref, k_ref, v_ref, rows_ref, raw_s, mix_s, aux_s = refs[pieces:]
    tile = a_ref.shape[0]
    depth = parts[0].shape[1]
    head = 8

    @pl.when(pl.program_id(0) == 0)
    def _():
        raw_s[0:head, :] = jnp.zeros_like(raw_s[0:head, :])

    @pl.when(pl.program_id(0) > 0)
    def _():
        raw_s[0:head, :] = raw_s[tile : tile + head, :]

    acc = jnp.zeros((tile, UNITS), F32)
    for p in range(pieces):
        acc += nt(a_ref[:, p * depth : (p + 1) * depth], parts[p][HD:])
    raw_s[head : tile + head, :] = acc[:, : 5 * HD]
    raw_ref[...] = acc[:, : 5 * HD].astype(BF16)
    gate_ref[...] = acc[:, 5 * HD : 6 * HD].astype(BF16)

    small = acc[:, 6 * HD :]
    rate, bias = scal_ref[h, 0], scal_ref[h, 1]
    arg = small[:, 2:3] + bias
    soft = jnp.maximum(arg, 0.0) + jnp.log(1.0 + jnp.exp(-jnp.abs(arg)))
    beta = sigmoid(small[:, 0:2])
    lane = iota((tile, HD), 1)
    aux_s[pl.ds(0, tile, 2), :] = jnp.where(
        lane == 0, beta[:, 0:1], jnp.where(lane == 1, -rate * soft, jnp.where(lane == 2, arg, 0.0))
    )
    aux_s[pl.ds(1, tile, 2), :] = jnp.where(lane == 0, beta[:, 1:2], 0.0)
    upper = jnp.where(iota((SUB, SUB), 0) <= iota((SUB, SUB), 1), 1.0, 0.0)
    for b in range(tile // SPAN):
        rows = jnp.transpose(aux_s[b * SUB : (b + 1) * SUB, :])[:8]
        cum = exact_nn(rows, upper)
        rows_ref[b] = jnp.where(iota((8, SUB), 0) == 3, cum[1:2], rows)

    chunk = 64
    for g in range(5):
        taps = cw_ref[0, :, g * HD : (g + 1) * HD]
        for i in range(tile // chunk):
            start = i * chunk
            views = conv_shifts(raw_s, start, chunk, slice(g * HD, (g + 1) * HD))
            pre = views[0] * taps[0:1]
            for j in range(1, TAPS):
                pre += views[j] * taps[j : j + 1]
            act = pre * sigmoid(pre)
            if g < 3:
                act = act * lax.rsqrt(lane_sum(act * act) + EPS_UNIT)
            if g == 0:
                q_ref[start : start + chunk, :] = act.astype(BF16)
            else:
                mix_s[pl.ds(2 * start + (g + 1) % 2, chunk, 2), :] = act
        if g in (2, 4):
            (k_ref if g == 2 else v_ref)[...] = mix_s[...].astype(BF16)


def project(h, normed, parts, conv_t, scal):
    seq, dim = normed.shape
    pieces = len(parts)
    tile = min(256, seq)
    fix = lambda i: (0, 0)
    along = lambda i: (i, 0)
    outs = [((seq, 5 * HD), BF16, 1), ((seq, HD), BF16, 1), ((seq, HD), BF16, 1), ((NH * seq, HD), BF16, NH), ((NH * seq, HD), BF16, NH)]
    return pl.pallas_call(
        functools.partial(project_kernel, pieces, h),
        out_shape=[jax.ShapeDtypeStruct(s, d) for s, d, _ in outs] + [jax.ShapeDtypeStruct((seq // SPAN, 8, SUB), F32)],
        grid=(seq // tile,),
        in_specs=[
            pl.BlockSpec(memory_space=pltpu.SMEM),
            pl.BlockSpec((tile, dim), along),
            pl.BlockSpec((1,) + conv_t.shape[1:], lambda i: (h, 0, 0)),
        ]
        + [pl.BlockSpec(w.shape, fix) for w in parts],
        out_specs=[pl.BlockSpec((tile * n, s[1]), along) for s, _, n in outs]
        + [pl.BlockSpec((tile // SPAN, 8, SUB), lambda i: (i, 0, 0))],
        scratch_shapes=[
            pltpu.VMEM((tile + 8, 5 * HD), F32),
            pltpu.VMEM((NH * tile, HD), F32),
            pltpu.VMEM((NH * tile, HD), F32),
        ],
        compiler_params=params(),
        cost_estimate=cost(2 * seq * dim * UNITS, 8e6),
        name="project",
    )(scal, normed, conv_t, *parts)


BASE = 16


def unit_lower_inverses(lowers):
    n, groups = SUB, SUB // BASE
    lane = iota((BASE, n), 1)
    group = lane // BASE
    packed = []
    for low in lowers:
        p = jnp.where(group == 0, low[:BASE], 0.0)
        for b in range(1, groups):
            p = jnp.where(group == b, low[b * BASE : (b + 1) * BASE], p)
        packed.append(p)
    eye = jnp.where(lane % BASE == iota((BASE, n), 0), 1.0, 0.0)
    invs = [eye] * len(lowers)
    first = group * BASE
    for j in range(BASE - 1):
        coefs = [jnp.take_along_axis(p, first + j, axis=1) for p in packed]
        invs = [x - c * x[j : j + 1] for x, c in zip(invs, coefs)]
    fulls = [
        jnp.concatenate([jnp.where(group == b, x, 0.0).astype(BF16) for b in range(groups)], axis=0) for x in invs
    ]
    row, col = iota((n, n), 0), iota((n, n), 1)
    size = BASE
    while size < n:
        odd = range(1, n // size, 2)
        mask = jnp.logical_and(row // size == col // size + 1, row // (2 * size) == col // (2 * size))
        crosses = [jnp.where(mask, low, 0.0).astype(BF16) for low in lowers]
        picks = [jnp.concatenate([f[b * size : (b + 1) * size] for b in odd], axis=0) for f in fulls]
        halves = [nn(p, c).astype(BF16) for p, c in zip(picks, crosses)]
        belows = [(p.astype(F32) - nn(h, f)).astype(BF16) for p, h, f in zip(picks, halves, fulls)]
        fulls = [
            jnp.concatenate(
                [
                    below[(b // 2) * size : (b // 2 + 1) * size] if b % 2 else f[b * size : (b + 1) * size]
                    for b in range(n // size)
                ],
                axis=0,
            )
            for f, below in zip(fulls, belows)
        ]
        size *= 2
    return fulls


def turned(value, eye):
    return nt(eye, value)


def decay_terms(rows_ref, cums, items):
    out = []
    pick_row = iota((8, SUB), 0)
    for i, (b, h) in enumerate(items):
        rows = rows_ref[h][b]
        g = rows[3:4, :]
        g_last = g[:, SUB - 1 :]
        e = jnp.exp(g)
        wide = jnp.where(pick_row == 1, e, jnp.where(pick_row == 2, jnp.exp(g_last - g), rows))
        wide = jnp.where(pick_row == 4, rows[0:1, :] * e, wide)
        cols = jnp.transpose(jnp.concatenate([wide] * (SUB // 8), axis=0))
        cums[i] = cols
        c_col = cums[i, pl.ds(1, SPAN, 2), :][:, 3:4]
        out.append((cols[:, 0:1], cols[:, 1:2], cols[:, 2:3], cols[:, 3:4], cols[:, 4:5], g, c_col, g_last))
    return out


PER_STEP = 2


def recur_kernel(heads, more, gain_ref, start_ref, *refs):
    q_r, k_r, v_r, g_r, rows_r = (refs[i * heads : (i + 1) * heads] for i in range(5))
    refs = refs[: 5 * heads] + refs[5 * heads + more :]
    z_ref, end_ref = refs[5 * heads : 5 * heads + 2]
    o_r = refs[5 * heads + 2 : 6 * heads + 2]
    u_r = refs[6 * heads + 2 : 7 * heads + 2]
    s_ref, t_ref, cums = refs[7 * heads + 2 :]

    @pl.when(pl.program_id(0) == 0)
    def _():
        end_ref[...] = start_ref[...]

    row, col = iota((SUB, SUB), 0), iota((SUB, SUB), 1)
    strict = col < row
    vis = iota((SPAN, SUB), 1) // NH <= iota((SPAN, SUB), 0)
    items = [(b, h) for b in range(PER_STEP) for h in range(heads)]
    tok = [pl.ds(b * SPAN, SPAN) for b, _ in items]
    sub = [pl.ds(b * SUB, SUB) for b, _ in items]
    eye = jnp.where(row == col, 1.0, 0.0).astype(BF16)
    terms = decay_terms(rows_r, cums, items)
    ks = [k_r[h][sub[i]] for i, (b, h) in enumerate(items)]
    qs = [q_r[h][tok[i]] for i, (b, h) in enumerate(items)]
    prods = [nt(jnp.concatenate([k, q], axis=0), k) for k, q in zip(ks, qs)]
    lowers = [
        t[0] * jnp.exp(jnp.where(strict, t[3] - t[5], FAR)) * p[:SUB] for p, t in zip(prods, terms)
    ]
    inner = [(jnp.exp(jnp.where(vis, t[6] - t[5], FAR)) * p[SUB:]).astype(BF16) for p, t in zip(prods, terms)]
    inverses = unit_lower_inverses(lowers)
    for (b, h), inv in zip(items, inverses):
        t_ref[b, h] = inv
    solved, backs = [], []
    for i, (b, h) in enumerate(items):
        t = terms[i]
        k = ks[i].astype(F32)
        right = jnp.concatenate([t[0] * v_r[h][sub[i]].astype(F32), t[4] * k], axis=1)
        solved.append(nn(inverses[i], right.astype(BF16)))
        weighted = turned((t[2] * k).astype(BF16), eye).astype(BF16)
        backs.append(jnp.concatenate([weighted, inner[i]], axis=0))
    gain = gain_ref[...]
    for b in range(PER_STEP):
        mine = [i for i, it in enumerate(items) if it[0] == b]
        olds = [end_ref[items[i][1]] for i in mine]
        old_bs = [o.astype(BF16) for o in olds]
        reads = [
            nn(jnp.concatenate([solved[i][:, HD:].astype(BF16), qs[i]], axis=0), ob) for i, ob in zip(mine, old_bs)
        ]
        ubs = [(solved[i][:, :HD] - r[:SUB]).astype(BF16) for i, r in zip(mine, reads)]
        adds = [nn(backs[i], ub) for i, ub in zip(mine, ubs)]
        for i, old, ob, r, ub, add in zip(mine, olds, old_bs, reads, ubs, adds):
            h = items[i][1]
            c_col, g_last = terms[i][6:]
            end_ref[h] = jnp.exp(g_last) * old + add[:HD]
            s_ref[b, h] = ob
            u_r[h][sub[i], :] = ub
            o = jnp.exp(c_col) * r[SUB:] + add[HD:]
            o_r[h][tok[i], :] = o.astype(BF16)
            scaled = o * lax.rsqrt(jnp.mean(o * o, axis=-1, keepdims=True) + EPS_NORM) * gain
            gate = g_r[h][tok[i]].astype(F32)
            z_ref[tok[i], h * HD : (h + 1) * HD] = (scaled * gate * sigmoid(gate)).astype(BF16)


def recur_specs(heads, at):
    tok = pl.BlockSpec((PER_STEP * SPAN, HD), lambda i: (at(i), 0))
    sub = pl.BlockSpec((PER_STEP * SUB, HD), lambda i: (at(i), 0))
    rows = pl.BlockSpec((PER_STEP, 8, SUB), lambda i: (at(i), 0, 0))
    wide = pl.BlockSpec((PER_STEP * SPAN, heads * HD), lambda i: (at(i), 0))
    mat = pl.BlockSpec((PER_STEP, heads, HD, HD), lambda i: (at(i), 0, 0, 0))
    one = pl.BlockSpec((1, HD), lambda i: (0, 0))
    state = pl.BlockSpec((heads, HD, HD), lambda i: (0, 0, 0))
    return tok, sub, rows, wide, mat, one, state


def recur(gain, start, q, k, v, gate, rows, first, steps, z=None):
    heads = len(q)
    tok, sub, row, wide, mat, one, state = recur_specs(heads, lambda i: i + first)
    o_tok, o_sub, _, _, o_mat, _, _ = recur_specs(heads, lambda i: i)
    n = steps * PER_STEP
    more = [] if z is None else [z]

    def shape(s, d):
        return jax.ShapeDtypeStruct(s, d)

    res = pl.pallas_call(
        functools.partial(recur_kernel, heads, len(more)),
        out_shape=[shape((q[0].shape[0], heads * HD), BF16), shape((heads, HD, HD), F32)]
        + [shape((n * SPAN, HD), BF16)] * heads
        + [shape((n * SUB, HD), BF16)] * heads
        + [shape((n, heads, HD, HD), BF16)] * 2,
        grid=(steps,),
        in_specs=[one, state]
        + [tok] * heads
        + [sub] * (2 * heads)
        + [tok] * heads
        + [row] * heads
        + [pl.BlockSpec(memory_space=pl.ANY)] * len(more),
        out_specs=[wide, state] + [o_tok] * heads + [o_sub] * heads + [o_mat] * 2,
        scratch_shapes=[pltpu.VMEM((PER_STEP * heads, SUB, SUB), F32)],
        compiler_params=params(),
        input_output_aliases={2 + 5 * heads: 0} if more else {},
        cost_estimate=cost(heads * n * 20 * 4.2e6, 1e6),
        name="recur",
    )(gain, start, *q, *k, *v, *gate, *rows, *more)
    return res[0], res[1], res[2 : 2 + heads], res[2 + heads : 2 + 2 * heads], res[2 + 2 * heads], res[3 + 2 * heads]


def recur_back_kernel(heads, more, gain_ref, start_ref, dz_ref, *refs):
    q_r, k_r, v_r, g_r, rows_r, o_r, u_r = (refs[i * heads : (i + 1) * heads] for i in range(7))
    s_ref, t_ref = refs[7 * heads : 7 * heads + 2]
    refs = refs[: 7 * heads + 2] + refs[7 * heads + 2 + more :]
    d_r = refs[7 * heads + 2 : 8 * heads + 2]
    drows_r = refs[8 * heads + 2 : 9 * heads + 2]
    dgain_ref, end_ref, cums, mixed = refs[9 * heads + 2 :]

    @pl.when(pl.program_id(0) == 0)
    def _():
        end_ref[...] = start_ref[...]
        dgain_ref[...] = jnp.zeros_like(dgain_ref)

    row, col = iota((SUB, SUB), 0), iota((SUB, SUB), 1)
    strict = col < row
    later = jnp.where(row >= col, 1.0, 0.0)
    vis = iota((SPAN, SUB), 1) // NH <= iota((SPAN, SUB), 0)
    gain = gain_ref[...]
    items = [(b, h) for b in reversed(range(PER_STEP)) for h in range(heads)]
    every = range(len(items))
    tok = [pl.ds(b * SPAN, SPAN) for b, _ in items]
    sub = [pl.ds(b * SUB, SUB) for b, _ in items]
    terms = decay_terms(rows_r, cums, items)
    ks = [k_r[h][sub[i]] for i, (b, h) in enumerate(items)]
    qs = [q_r[h][tok[i]] for i, (b, h) in enumerate(items)]
    us = [u_r[h][sub[i]] for i, (b, h) in enumerate(items)]
    ss = [s_ref[b, h] for b, h in items]
    prods = [nt(jnp.concatenate([k, q], axis=0), k) for k, q in zip(ks, qs)]

    dos = []
    dgain = jnp.zeros((1, HD), F32)
    for i, (b, h) in enumerate(items):
        dz = dz_ref[tok[i], h * HD : (h + 1) * HD].astype(F32)
        o = o_r[h][tok[i]].astype(F32)
        gate = g_r[h][tok[i]].astype(F32)
        inv_rms = lax.rsqrt(jnp.mean(o * o, axis=-1, keepdims=True) + EPS_NORM)
        n = o * inv_rms
        sg = sigmoid(gate)
        dy = dz * gate * sg
        d_r[h][tok[i], 5 * HD :] = (dz * n * gain * sg * (1.0 + gate * (1.0 - sg))).astype(BF16)
        dgain += jnp.sum(dy * n, axis=0, keepdims=True)
        dn = dy * gain
        dos.append((inv_rms * (dn - n * jnp.mean(dn * n, axis=-1, keepdims=True))).astype(BF16))
    dgain_ref[...] += dgain

    eye = jnp.where(row == col, 1.0, 0.0).astype(BF16)
    reads = [jnp.exp(jnp.where(vis, t[6] - t[5], FAR)) for t in terms]
    ecs = [jnp.exp(t[6]) for t in terms]
    kfs = [k.astype(F32) for k in ks]
    qfs = [q.astype(F32) for q in qs]
    lefts = [
        jnp.concatenate([turned((p[SUB:] * r).astype(BF16), eye).astype(BF16), (t[2] * k).astype(BF16)], axis=1)
        for p, r, t, k in zip(prods, reads, terms, kfs)
    ]
    downs = [
        turned(jnp.concatenate([(ec * q).astype(BF16), (-t[4] * k).astype(BF16)], axis=0), eye).astype(BF16)
        for ec, q, t, k in zip(ecs, qfs, terms, kfs)
    ]
    solves = [turned(t_ref[b, h], eye).astype(BF16) for b, h in items]

    drs, dsbs, dots = [None] * len(items), [None] * len(items), [None] * len(items)
    for b in reversed(range(PER_STEP)):
        mine = [i for i, it in enumerate(items) if it[0] == b]
        dss = {i: end_ref[items[i][1]] for i in mine}
        for i in mine:
            dsbs[i] = dss[i].astype(BF16)
            dots[i] = jnp.sum(dss[i] * ss[i].astype(F32), axis=0, keepdims=True)
        dus = {i: nn(lefts[i], jnp.concatenate([dos[i], dsbs[i]], axis=0)).astype(BF16) for i in mine}
        for i in mine:
            drs[i] = nn(solves[i], dus[i])
        for i in mine:
            add = nn(downs[i], jnp.concatenate([dos[i], drs[i].astype(BF16)], axis=0))
            end_ref[items[i][1]] = jnp.exp(terms[i][7]) * dss[i] + add

    drbs = [d.astype(BF16) for d in drs]
    from_s = [nt(jnp.concatenate([a, c], axis=0), s) for a, c, s in zip(drbs, dos, ss)]
    from_u = [nt(jnp.concatenate([a, c], axis=0), u) for a, c, u in zip(drbs, dos, us)]
    ks0 = [nn(k, s) for k, s in zip(ks, ss)]
    dws = [nt(u, d) for u, d in zip(us, dsbs)]
    dgs, dbs, dks, minus, dcs, syms = [], [], [], [], [], []
    nms = []
    for i, (b, h) in enumerate(items):
        beta, e_col, e_rest, g_col, beta_e, g_row, c_col, g_last = terms[i]
        k, q = kfs[i], qfs[i]
        mixed[i] = beta * drs[i]
        d_r[h][tok[i], 3 * HD : 4 * HD] = mixed[i, pl.ds(0, SPAN, 2), :].astype(BF16)
        d_r[h][tok[i], 4 * HD : 5 * HD] = mixed[i, pl.ds(1, SPAN, 2), :].astype(BF16)
        t1 = beta_e * from_s[i][:SUB]
        t3 = e_rest * dws[i]
        fade = jnp.exp(jnp.where(strict, g_col - g_row, FAR))
        y = -from_u[i][:SUB] * fade
        le = y * prods[i][:SUB]
        hh = beta * le
        kt3 = k * t3
        dbs.append(lane_sum(drs[i] * (v_r[h][sub[i]].astype(F32) - e_col * ks0[i]) + le))
        dg = lane_sum(hh - k * t1 - kt3)
        d_last = lane_sum(jnp.sum(kt3, axis=0, keepdims=True) + jnp.exp(g_last) * dots[i])
        dgs.append(dg + jnp.where(row[:, :1] == SUB - 1, d_last, 0.0))
        dks.append(t3 - t1)
        dkk = beta * y
        syms.append(dkk + turned(dkk.astype(BF16), eye))
        nm = from_u[i][SUB:] * reads[i]
        hm = nm * prods[i][SUB:]
        t2 = ecs[i] * from_s[i][SUB:]
        nms.append((nm.astype(BF16), t2))
        dcs.append(lane_sum(hm + q * t2))
        minus.append(jnp.sum(hh, axis=0, keepdims=True) + jnp.sum(hm, axis=0, keepdims=True))
    tops = [
        nn(jnp.concatenate([s.astype(BF16), nm], axis=0), k) for s, (nm, _), k in zip(syms, nms, ks)
    ]
    turns = [nn(turned(nm, eye).astype(BF16), q) for (nm, _), q in zip(nms, qs)]
    for i, (b, h) in enumerate(items):
        d_r[h][tok[i], :HD] = (tops[i][SUB:] + nms[i][1]).astype(BF16)
        mixed[i] = dks[i] + tops[i][:SUB] + turns[i]
        d_r[h][tok[i], HD : 2 * HD] = mixed[i, pl.ds(0, SPAN, 2), :].astype(BF16)
        d_r[h][tok[i], 2 * HD : 3 * HD] = mixed[i, pl.ds(1, SPAN, 2), :].astype(BF16)
        cums[i] = jnp.where(col == 0, dbs[i], jnp.where(col == 1, dgs[i], 0.0))
        odd = pl.ds(1, SPAN, 2)
        cums[i, odd, :] = cums[i, odd, :] + jnp.where(col[:SPAN] == 1, dcs[i], 0.0)
        rows = jnp.transpose(cums[i])[:8]
        first = iota((8, SUB), 0)
        summed = exact_nn(rows - jnp.where(first == 1, minus[i], 0.0), later)
        drows_r[h][b] = jnp.where(first == 0, rows, summed)


def recur_back(gain, start, dz, q, k, v, gate, rows, o, u, s, t, first, steps, done=()):
    heads = len(q)
    tok, sub, row, wide, mat, one, state = recur_specs(heads, lambda i: first + steps - 1 - i)
    o_tok, o_sub, _, _, o_mat, _, _ = recur_specs(heads, lambda i: steps - 1 - i)
    n = steps * PER_STEP
    seq = q[0].shape[0]
    d_spec = pl.BlockSpec((PER_STEP * SPAN, 6 * HD), lambda i: (first + steps - 1 - i, 0))

    def shape(s, d):
        return jax.ShapeDtypeStruct(s, d)

    res = pl.pallas_call(
        functools.partial(recur_back_kernel, heads, len(done)),
        out_shape=[shape((seq, 6 * HD), BF16)] * heads
        + [shape((seq // SPAN, 8, SUB), F32)] * heads
        + [shape((1, HD), F32), shape((heads, HD, HD), F32)],
        grid=(steps,),
        in_specs=[one, state, wide]
        + [tok] * heads
        + [sub] * (2 * heads)
        + [tok] * heads
        + [row] * heads
        + [o_tok] * heads
        + [o_sub] * heads
        + [o_mat] * 2
        + [pl.BlockSpec(memory_space=pl.ANY)] * len(done),
        out_specs=[d_spec] * heads + [row] * heads + [one, state],
        scratch_shapes=[pltpu.VMEM((PER_STEP * heads, SUB, SUB), F32)] * 2,
        compiler_params=params(),
        input_output_aliases={5 + 7 * heads + i: i for i in range(len(done))},
        cost_estimate=cost(heads * n * 30 * 4.2e6, 1e6),
        name="recur_back",
    )(gain, start, dz, *q, *k, *v, *gate, *rows, *o, *u, s, t, *done)
    return res[:heads], res[heads : 2 * heads], res[2 * heads], res[2 * heads + 1]


def project_back_kernel(pieces, bit, h, scal_ref, a_ref, cw_ref, raw_ref, rows_ref, d_ref, drow_ref, *refs):
    outer, refs = refs[:pieces], refs[pieces:]
    dp_ref, dcw_ref, dsm_ref = refs[:3]
    stacked = refs[3:5]
    raw_s, ds_s, acc, aux_s = refs[5:]
    tile = a_ref.shape[0]
    depth = outer[0].shape[1]
    chunk = 64
    step, steps = pl.program_id(0), pl.num_programs(0)
    base = pl.multiple_of((steps - 1 - step) * tile, tile)

    @pl.when(step == 0)
    def _():
        ds_s[tile : tile + 8, :] = jnp.zeros_like(ds_s[tile : tile + 8, :])
        dcw_ref[...] = jnp.zeros_like(dcw_ref)
        dsm_ref[...] = jnp.zeros_like(dsm_ref)

    @pl.when(step > 0)
    def _():
        ds_s[tile : tile + 8, :] = ds_s[0:8, :]

    @pl.when(step == steps - 1)
    def _():
        raw_s[0:8, :] = jnp.zeros_like(raw_s[0:8, :])

    @pl.when(step < steps - 1)
    def _():
        before = raw_ref[pl.ds(pl.multiple_of(base - 16, 16), 16), :].astype(F32)
        raw_s[0:8, :] = before[8:]

    raw_s[8 : tile + 8, :] = raw_ref[pl.ds(base, tile), :].astype(F32)
    for g in range(5):
        lanes = slice(g * HD, (g + 1) * HD)
        taps = cw_ref[0, :, lanes]
        sums = [jnp.zeros((8, HD), F32)] * TAPS
        for i in range(tile // chunk):
            start = i * chunk
            shifted = conv_shifts(raw_s, start, chunk, lanes)
            pre = shifted[0] * taps[0:1]
            for j in range(1, TAPS):
                pre = pre + shifted[j] * taps[j : j + 1]
            sg = sigmoid(pre)
            act = pre * sg
            d = d_ref[start : start + chunk, lanes].astype(F32)
            if g < 3:
                inv = lax.rsqrt(lane_sum(act * act) + EPS_UNIT)
                unit = act * inv
                d = inv * (d - unit * lane_sum(d * unit))
            d = d * (sg + act * (1.0 - sg))
            ds_s[start : start + chunk, lanes] = d
            sums = [s + jnp.sum((d * x).reshape(chunk // 8, 8, HD), axis=0) for s, x in zip(sums, shifted)]
        for j in range(TAPS):
            dcw_ref[j : j + 1, lanes] += jnp.sum(sums[j], axis=0, keepdims=True)
        for i in range(tile // chunk):
            start = i * chunk
            views = conv_shifts_back(ds_s, start, chunk, lanes)
            total = views[0] * taps[0:1]
            for j in range(1, TAPS):
                total = total + views[j] * taps[j : j + 1]
            dp_ref[start : start + chunk, lanes] = total.astype(BF16)

    rate = scal_ref[h, 0]
    lane = iota((SPAN, HD), 1)
    total = jnp.zeros((8, HD), F32)
    for b in range(tile // SPAN):
        both = jnp.concatenate([rows_ref[b], drow_ref[b]] + [jnp.zeros((8, SUB), F32)] * (SUB // 8 - 2), axis=0)
        aux_s[b] = jnp.transpose(both)
        even, odd = aux_s[b, pl.ds(0, SPAN, 2), :], aux_s[b, pl.ds(1, SPAN, 2), :]
        b1, b2, dg = even[:, 0:1], odd[:, 0:1], even[:, 9:10]
        darg = -rate * dg * sigmoid(even[:, 2:3])
        d1 = even[:, 8:9] * b1 * (1.0 - b1)
        d2 = odd[:, 8:9] * b2 * (1.0 - b2)
        vals = jnp.where(lane == 0, d1, jnp.where(lane == 1, d2, jnp.where(lane == 2, darg, 0.0)))
        here = pl.ds(b * SPAN, SPAN)
        dp_ref[here, 6 * HD :] = vals[:, :SMALL].astype(BF16)
        dp_ref[here, 5 * HD : 6 * HD] = d_ref[here, 5 * HD :]
        extra = jnp.where(lane == 0, dg * even[:, 1:2], jnp.where(lane == 1, darg, 0.0))
        total += jnp.sum(extra.reshape(SPAN // 8, 8, HD), axis=0)
    dsm_ref[...] += total

    term = tn(dp_ref[...], a_ref[...])

    @pl.when(step == 0)
    def _():
        acc[...] = term

    @pl.when(step > 0)
    def _():
        acc[...] += term

    @pl.when(step == steps - 1)
    def _():
        for stack, group in zip(stacked, sides(pieces, bit)):
            for i, p in enumerate(group):
                stack[i, :HD] = outer[p][...]
                stack[i, HD:] = acc[:, p * depth : (p + 1) * depth].astype(BF16)


def project_back(h, normed, conv_t, scal, raw, rows, d, drows, outer, bit):
    seq, dim = normed.shape
    pieces = len(outer)
    depth = outer[0].shape[1]
    tile = min(512, seq)
    end = seq // tile - 1
    along = lambda i: (end - i, 0)
    deep = pl.BlockSpec((tile // SPAN, 8, SUB), lambda i: (end - i, 0, 0))
    fix = lambda i: (0, 0)
    outs = [((seq, UNITS), BF16), ((8, 5 * HD), F32), ((8, HD), F32)]
    shapes = [jax.ShapeDtypeStruct(s, t) for s, t in outs] + stacks(pieces, (HD + UNITS, depth))
    res = pl.pallas_call(
        functools.partial(project_back_kernel, pieces, bit, h),
        out_shape=shapes,
        grid=(seq // tile,),
        in_specs=[
            pl.BlockSpec(memory_space=pltpu.SMEM),
            pl.BlockSpec((tile, dim), along),
            pl.BlockSpec((1,) + conv_t.shape[1:], lambda i: (h, 0, 0)),
            pl.BlockSpec(raw.shape, fix),
            deep,
            pl.BlockSpec((tile, 6 * HD), along),
            deep,
        ]
        + [pl.BlockSpec(g.shape, fix) for g in outer],
        out_specs=[pl.BlockSpec((tile, UNITS), along)]
        + [pl.BlockSpec(s, fix) for s, _ in outs[1:]]
        + [pl.BlockSpec(v.shape, lambda i: (0, 0, 0)) for v in shapes[3:]],
        scratch_shapes=[
            pltpu.VMEM((tile + 8, 5 * HD), F32),
            pltpu.VMEM((tile + 8, 5 * HD), F32),
            pltpu.VMEM((UNITS, dim), F32),
            pltpu.VMEM((tile // SPAN, SUB, SUB), F32),
        ],
        compiler_params=params(),
        cost_estimate=cost(2 * seq * dim * UNITS, 1e6),
        name="project_back",
    )(scal, normed, conv_t, raw, rows, d, drows, *outer)
    return res[0], res[1], res[2], res[3:]


def input_back_kernel(heads, pieces, *refs):
    dps, parts = refs[:heads], refs[heads : heads + heads * pieces]
    x_ref, da_ref, dgain_ref = refs[heads + heads * pieces :]
    depth = parts[0].shape[1]
    x = x_ref[...].astype(F32)
    unit = x * lax.rsqrt(jnp.mean(x * x, axis=-1, keepdims=True) + EPS_NORM)
    shares = []
    for p in range(pieces):
        total = nn(
            jnp.concatenate([d[:, 6 * HD :] for d in dps], axis=1),
            jnp.concatenate([parts[h * pieces + p][7 * HD :] for h in range(heads)], axis=0),
        )
        for h in range(heads):
            total += nn(dps[h][:, : 6 * HD], parts[h * pieces + p][HD : 7 * HD])
        low = total.astype(BF16)
        lanes = slice(p * depth, (p + 1) * depth)
        da_ref[:, lanes] = low
        shares.append(jnp.sum(low.astype(F32) * unit[:, lanes], axis=0, keepdims=True))
    share = jnp.concatenate(shares, axis=1)

    @pl.when(pl.program_id(0) == 0)
    def _():
        dgain_ref[...] = share

    @pl.when(pl.program_id(0) > 0)
    def _():
        dgain_ref[...] += share


def input_back(dps, parts, x):
    seq = dps[0].shape[0]
    heads, pieces = len(parts), len(parts[0])
    flat = [w for head in parts for w in head]
    dim = pieces * flat[0].shape[1]
    tile = min(256, seq)
    along = lambda i: (i, 0)
    return pl.pallas_call(
        functools.partial(input_back_kernel, heads, pieces),
        out_shape=[jax.ShapeDtypeStruct((seq, dim), BF16), jax.ShapeDtypeStruct((1, dim), F32)],
        grid=(seq // tile,),
        in_specs=[pl.BlockSpec((tile, UNITS), along)] * heads
        + [pl.BlockSpec(w.shape, lambda i: (0, 0)) for w in flat]
        + [pl.BlockSpec((tile, dim), along)],
        out_specs=[pl.BlockSpec((tile, dim), along), pl.BlockSpec((1, dim), lambda i: (0, 0))],
        compiler_params=params(),
        cost_estimate=cost(2 * seq * dim * UNITS * heads, 1e6),
        name="input_back",
    )(*dps, *flat, x)


def mix_kernel(heads, pieces, z_ref, *refs):
    parts, out_ref = refs[:-1], refs[-1]
    depth = parts[0].shape[1]
    for p in range(pieces):
        right = jnp.concatenate([parts[h * pieces + p][...] for h in range(heads)], axis=0)
        out_ref[:, p * depth : (p + 1) * depth] = nn(z_ref[...], right).astype(BF16)


def outer_specs(parts):
    return [pl.BlockSpec((HD, w.shape[1]), lambda i: (0, 0)) for head in parts for w in head]


def mix_out(z, parts):
    seq = z.shape[0]
    heads, pieces = len(parts), len(parts[0])
    dim = pieces * parts[0][0].shape[1]
    tile = min(256, seq)
    along = lambda i: (i, 0)
    return pl.pallas_call(
        functools.partial(mix_kernel, heads, pieces),
        out_shape=jax.ShapeDtypeStruct((seq, dim), BF16),
        grid=(seq // tile,),
        in_specs=[pl.BlockSpec((tile, z.shape[1]), along)] + outer_specs(parts),
        out_specs=pl.BlockSpec((tile, dim), along),
        compiler_params=params(),
        cost_estimate=cost(2 * seq * dim * z.shape[1], 1e6),
        name="mix_out",
    )(z, *[w for head in parts for w in head])


def mix_back_kernel(heads, pieces, gain_ref, own_ref, other_ref, mid_ref, dy_ref, z_ref, *refs):
    parts, refs = refs[: heads * pieces], refs[heads * pieces :]
    dmix_ref, dz_ref, dgain_ref = refs[:3]
    grads, acc = refs[3:-1], refs[-1]
    depth = parts[0].shape[1]
    step, steps = pl.program_id(0), pl.num_programs(0)
    mid = mid_ref[...]
    dn = own_ref[...].astype(F32) + other_ref[...].astype(F32)
    inv = lax.rsqrt(jnp.mean(mid * mid, axis=-1, keepdims=True) + EPS_NORM)
    unit = mid * inv
    prod = dn * unit
    share = jnp.sum(prod, axis=0, keepdims=True)
    scaled = dn * gain_ref[...]
    back = inv * (scaled - unit * jnp.mean(prod * gain_ref[...], axis=-1, keepdims=True))
    dmix_ref[...] = (dy_ref[...].astype(F32) + back).astype(BF16)

    @pl.when(step == 0)
    def _():
        dgain_ref[...] = share
        acc[...] = jnp.zeros_like(acc)

    @pl.when(step > 0)
    def _():
        dgain_ref[...] += share

    dz = jnp.zeros((z_ref.shape[0], heads * HD), F32)
    for p in range(pieces):
        lanes = slice(p * depth, (p + 1) * depth)
        right = jnp.concatenate([parts[h * pieces + p][...] for h in range(heads)], axis=0)
        dz += nt(dmix_ref[:, lanes], right)
    acc[...] += tn(z_ref[...], dmix_ref[...])
    dz_ref[...] = dz.astype(BF16)

    @pl.when(step == steps - 1)
    def _():
        for h in range(heads):
            for p in range(pieces):
                grads[h * pieces + p][...] = acc[h * HD : (h + 1) * HD, p * depth : (p + 1) * depth].astype(BF16)


def mix_back(gain, own, other, mid, dy, z, parts):
    seq, dim = mid.shape
    heads, pieces = len(parts), len(parts[0])
    wide = z.shape[1]
    tile = min(256, seq)
    row = pl.BlockSpec((tile, dim), lambda i: (i, 0))
    one = pl.BlockSpec((1, dim), lambda i: (0, 0))
    zs = pl.BlockSpec((tile, wide), lambda i: (i, 0))
    res = pl.pallas_call(
        functools.partial(mix_back_kernel, heads, pieces),
        out_shape=[
            jax.ShapeDtypeStruct((seq, dim), BF16),
            jax.ShapeDtypeStruct((seq, wide), BF16),
            jax.ShapeDtypeStruct((1, dim), F32),
        ]
        + [jax.ShapeDtypeStruct((HD, dim // pieces), BF16)] * (heads * pieces),
        grid=(seq // tile,),
        in_specs=[one, row, row, row, row, zs] + outer_specs(parts),
        out_specs=[row, zs, one] + outer_specs(parts),
        scratch_shapes=[pltpu.VMEM((wide, dim), F32)],
        compiler_params=params(),
        cost_estimate=cost(4 * seq * dim * wide, 1e6),
        name="mix_back",
    )(gain, own, other, mid, dy, z, *[w for head in parts for w in head])
    return res[0], res[1], res[2], [res[3 + h * pieces : 3 + (h + 1) * pieces] for h in range(heads)]


def select_kernel(counts, apart, table_ref, *refs):
    j = pl.program_id(0)
    first = 0
    for g, n in enumerate(counts):
        width = refs[first].shape[2]
        value = refs[first][...]
        for i in range(1, n):
            value = jnp.where(table_ref[2 * g, j] == i, refs[first + i][...], value)
        if apart:
            refs[sum(counts) + g][...] = value
        else:
            refs[-1][:, :, g * width : (g + 1) * width] = value
        first += n


def select_blocks(groups, table, count, apart=False):
    specs, flat = [], []
    for g, sources in enumerate(groups):
        for i, value in enumerate(sources):

            def where(j, t, g=g, i=i):
                return (jnp.where(t[2 * g, j] == i, t[2 * g + 1, j], 0), 0, 0)

            specs.append(pl.BlockSpec((1,) + value.shape[1:], where))
            flat.append(value)
    piece, width = flat[0].shape[1:]
    total = width if apart else width * len(groups)
    outs = len(groups) if apart else 1
    res = pl.pallas_call(
        functools.partial(select_kernel, [len(g) for g in groups], apart),
        out_shape=[jax.ShapeDtypeStruct((count, piece, total), flat[0].dtype)] * outs,
        grid_spec=pltpu.PrefetchScalarGridSpec(
            num_scalar_prefetch=1,
            grid=(count,),
            in_specs=specs,
            out_specs=[pl.BlockSpec((1, piece, total), lambda j, t: (j, 0, 0))] * outs,
        ),
        compiler_params=params(),
        cost_estimate=cost(1e6, 1e6),
        name="select_blocks",
    )(table, *flat)
    return res if apart else res[0]


def ffn_kernel(pieces, chunks, bits, more, b_ref, dy_ref, *refs):
    weights = refs[: pieces * chunks]
    refs = refs[pieces * chunks :]
    sums_in, refs = (refs[:2], refs[2:]) if more else (None, refs)
    out_ref, db_ref = refs[:2]
    stacked = refs[2 : 2 + 2 * chunks]
    b_s, dy_s, hid_s, dg_s, du_s = refs[2 + 2 * chunks :]
    depth = weights[0].shape[1]
    units = weights[0].shape[0] // 3
    tile = b_ref.shape[0]
    step, steps = pl.program_id(0), pl.num_programs(0)

    def weight(p, i):
        return jnp.concatenate(
            [weights[c * pieces + p][i * units : (i + 1) * units] for c in range(chunks)], axis=0
        )

    rows = pl.ds(pl.multiple_of(step * tile, tile), tile)
    b_s[rows, :] = b_ref[...]
    dy_s[rows, :] = dy_ref[...]
    gate = jnp.zeros((tile, units * chunks), F32)
    up = jnp.zeros((tile, units * chunks), F32)
    dh = jnp.zeros((tile, units * chunks), F32)
    for p in range(pieces):
        lanes = slice(p * depth, (p + 1) * depth)
        block, dblock = b_ref[:, lanes], dy_ref[:, lanes]
        gate += nt(block, weight(p, 0))
        up += nt(block, weight(p, 1))
        dh += nt(dblock, weight(p, 2))
    sg = sigmoid(gate)
    act = gate * sg
    hid = (act * up).astype(BF16)
    du = (dh * act).astype(BF16)
    dg = (dh * up * (sg + act * (1.0 - sg))).astype(BF16)
    hid_s[rows, :] = hid
    dg_s[rows, :] = dg
    du_s[rows, :] = du
    for p in range(pieces):
        lanes = slice(p * depth, (p + 1) * depth)
        o = nn(hid, weight(p, 2))
        d = nn(dg, weight(p, 0)) + nn(du, weight(p, 1))
        if more:
            o += sums_in[0][:, lanes].astype(F32)
            d += sums_in[1][:, lanes].astype(F32)
        out_ref[:, lanes] = o.astype(out_ref.dtype)
        db_ref[:, lanes] = d.astype(db_ref.dtype)

    @pl.when(step == steps - 1)
    def _():
        for i, (left, right) in enumerate([(dg_s, b_s), (du_s, b_s), (hid_s, dy_s)]):
            g = tn(left[...], right[...]).astype(BF16)
            for c in range(chunks):
                for stack, group in zip(stacked[2 * c : 2 * c + 2], sides(pieces, bits[c])):
                    for n, p in enumerate(group):
                        stack[n, i * units : (i + 1) * units] = g[
                            c * units : (c + 1) * units, p * depth : (p + 1) * depth
                        ]


def ffn(normed, dy, parts, bits, sums=None, last=True):
    seq, dim = normed.shape
    chunks, pieces = len(parts), len(parts[0])
    flat = [w for chunk in parts for w in chunk]
    units = flat[0].shape[0] // 3
    tile = min(256, seq)
    row = pl.BlockSpec((tile, dim), lambda i: (i, 0))
    more = () if sums is None else tuple(sums)
    grads = stacks(pieces, flat[0].shape) * chunks
    res = pl.pallas_call(
        functools.partial(ffn_kernel, pieces, chunks, bits, bool(more)),
        out_shape=[jax.ShapeDtypeStruct((seq, dim), BF16 if last else F32)] * 2 + grads,
        grid=(seq // tile,),
        in_specs=[row, row] + [pl.BlockSpec(w.shape, lambda i: (0, 0)) for w in flat] + [row] * len(more),
        out_specs=[row, row] + [pl.BlockSpec(g.shape, lambda i: (0, 0, 0)) for g in grads],
        scratch_shapes=[pltpu.VMEM((seq, dim), BF16)] * 2 + [pltpu.VMEM((seq, units * chunks), BF16)] * 3,
        compiler_params=params(),
        cost_estimate=cost(18 * seq * dim * units * chunks, 1e6),
        name="ffn",
    )(normed, dy, *flat, *more)
    return res[0], res[1], [res[2 + 2 * c : 4 + 2 * c] for c in range(chunks)]


def sync(*trees):
    leaves, tree = jax.tree.flatten(trees)
    return jax.tree.unflatten(tree, lax.optimization_barrier(leaves))


def bits_of(n):
    return [1 << i for i in range(n.bit_length() - 1)]


class Place:
    def __init__(self):
        self.n_f = lax.axis_size("fsdp")
        self.n_t = lax.axis_size("tp")
        self.chips = self.n_f // 2
        f = lax.axis_index("fsdp")
        self.f = f
        self.core = f % 2
        self.k = f // 2
        self.t = lax.axis_index("tp")

    def swap(self, value):
        return lax.ppermute(value, "fsdp", [(i, i ^ 1) for i in range(self.n_f)])

    def move(self, value, bit):
        return lax.ppermute(value, "fsdp", [(i, i ^ (2 * bit)) for i in range(self.n_f)])

    def turn(self, value, r):
        return lax.ppermute(value, "tp", [(i, (i + r) % self.n_t) for i in range(self.n_t)])

    def in_order(self, mine, other, axis):
        first = jnp.where(self.core == 0, mine, other)
        second = jnp.where(self.core == 0, other, mine)
        return jnp.concatenate([first, second], axis=axis)

    def halves(self, value, axis):
        size = value.shape[axis] // 2
        return (
            lax.dynamic_slice_in_dim(value, self.core * size, size, axis),
            lax.dynamic_slice_in_dim(value, (1 - self.core) * size, size, axis),
        )

    def relative(self, value):
        width = value.shape[-1] // self.chips
        blocks = [
            lax.dynamic_slice_in_dim(value, (self.k ^ p) * width, width, value.ndim - 1) for p in range(self.chips)
        ]
        return jnp.concatenate(blocks, axis=-1)

    def spread_out(self, value):
        if value.shape[0] < self.n_t:
            value = jnp.pad(value, ((0, self.n_t - value.shape[0]),) + ((0, 0),) * (value.ndim - 1))
        return lax.all_to_all(value, "tp", split_axis=0, concat_axis=0, tiled=True)

    def all_sum(self, value):
        return self.chip_sum(self.line_sum(value))

    def chip_sum(self, value):
        for bit in [1] + [2 * b for b in bits_of(self.chips)]:
            value = value + lax.ppermute(value, "fsdp", [(i, i ^ bit) for i in range(self.n_f)])
        return value

    def line_sum(self, value):
        total = value
        for r in range(1, self.n_t):
            total = total + self.turn(value, r)
        return total

def rms_terms(value):
    return lax.rsqrt(jnp.mean(value * value, axis=-1, keepdims=True) + EPS_NORM)


def rms_back(value, gain, d_normed):
    inv = rms_terms(value)
    unit = value * inv
    dn = d_normed * gain
    return inv * (dn - unit * jnp.mean(dn * unit, axis=-1, keepdims=True))


class Gather:
    def __init__(self, at, shard):
        self.at = at
        self.parts = {(0, 0): shard}

    def turn(self, r, by=None):
        by = by or r
        self.parts[r, 0] = self.at.turn(self.parts[r - by, 0], by)

    def move(self, r, to, via):
        self.parts[r, to] = self.at.move(self.parts[r, to ^ via], via)

    def full(self, r):
        return [self.parts[r, p] for p in range(self.at.chips)]

    def rest(self):
        for r in range(1, self.at.n_t):
            self.turn(r)
        for r in range(self.at.n_t):
            for p in range(1, self.at.chips):
                self.move(r, p, p & -p)
        return [self.full(r) for r in range(self.at.n_t)]


def first_bit(at, r, late=False):
    return at.chips // 2 if r == 3 or r == (2 if late else 0) else 1


class Scatter:
    def __init__(self, at, late=False):
        self.at = at
        self.bit = lambda r: first_bit(at, r, late)
        self.near, self.far, self.two, self.one, self.end = {}, {}, {}, {}, {}

    def put(self, r, stacked):
        self.near[r], self.far[r] = stacked

    def cross(self, *turns):
        for r in turns:
            self.far[r] = self.at.move(self.far[r], self.bit(r))

    def add(self, *turns):
        sums = add_stacks([(self.near.pop(r), self.far.pop(r)) for r in turns])
        return dict(zip(turns, sums))

    def pass_on(self, sums):
        for r, (keep, give) in sums.items():
            self.two[r] = keep, self.at.move(give, 3 - self.bit(r))

    def fold(self, *turns):
        self.pass_on(self.add(*turns))

    def close(self, *turns):
        for r in turns:
            keep, came = self.two.pop(r)
            self.one[r] = (keep.astype(F32) + came.astype(F32)).astype(BF16)

    def home(self, r):
        self.end[r] = self.at.turn(self.one.pop(r), self.at.n_t - r)

    def merge(self, r):
        self.end[r] = self.at.turn(self.one.pop(r), self.at.n_t - 1)

    def join(self, r):
        self.one[r - 1] = (self.one[r - 1].astype(F32) + self.end.pop(r).astype(F32)).astype(BF16)

    def total(self):
        return sum(v.astype(F32) for v in list(self.one.values()) + list(self.end.values()))

    def state(self):
        return self.near, self.far, self.two, self.one, self.end

    def take(self, state):
        self.near, self.far, self.two, self.one, self.end = state

    def rest(self):
        for r in range(self.at.n_t):
            have = {}
            for stack, group in zip((self.near.pop(r), self.far.pop(r)), sides(self.at.chips, self.bit(r))):
                have.update({p: stack[i] for i, p in enumerate(group)})
            for bit in bits_of(self.at.chips):
                for p in [p for p in have if p & bit]:
                    came = self.at.move(have.pop(p), bit)
                    have[p ^ bit] = (have[p ^ bit].astype(F32) + came.astype(F32)).astype(BF16)
            self.one[r] = have[0]
            if r:
                self.home(r)


class Routing:
    def __init__(self, at, value, order, source):
        self.at, self.order = at, order
        self.per_chip = value.shape[0]
        self.have, self.where = [value], [0]
        reach = [0]
        for bit in order[:-1]:
            reach += [w | bit for w in reach]
        tables = []
        for chip in (at.k ^ order[-1], at.k):
            ask = lax.dynamic_slice_in_dim(source, chip * self.per_chip, self.per_chip, 0)
            distance = (ask // self.per_chip) ^ at.k
            src = sum(jnp.where(distance == w, i, 0) for i, w in enumerate(reach))
            near = (distance & order[-1]) == 0
            slot = ask % self.per_chip
            if chip is not at.k:
                tables.append((src, slot))
            else:
                tables.append(
                    (
                        jnp.where(near, src, len(reach)),
                        jnp.where(near, slot, jnp.arange(self.per_chip, dtype=jnp.int32)),
                    )
                )
        self.ask, self.keep = (jnp.stack(t) for t in tables)

    def step(self):
        bit = self.order[len(self.where).bit_length() - 1]
        self.have = self.have + [self.at.move(v, bit) for v in self.have]
        self.where = self.where + [w | bit for w in self.where]

    def last(self, give):
        self.have = self.have + [self.at.move(give, self.order[-1])]


def local(
    tokens, lengths, perm, cotangent, norm1_gain, input_weight, conv_w, decay_log, decay_bias, out_gain, w_out,
    norm2_gain, gate_up_weight, down_weight
):
    at = Place()
    slots, piece, dim = tokens.shape
    n_f, n_t, chips = at.n_f, at.n_t, at.chips
    heads_all = conv_w.shape[0]
    heads = heads_all // 2
    local_heads = input_weight.shape[1]
    cols = input_weight.shape[2]
    by_turn = local_heads == 2
    laps = list(range(n_t))
    bits = bits_of(chips)
    fast = by_turn and chips == 4 and n_t == 4
    per_chip = 2 * slots
    seq = n_t * piece
    steps = seq // SPAN // PER_STEP // 2

    pad = SMALL - (cols - 6 * HD)
    if by_turn:
        packed = jnp.transpose(input_weight, (1, 2, 0))
        zeros = jnp.zeros((local_heads, pad, packed.shape[2]), BF16)
        packed = jnp.concatenate([w_out.reshape(local_heads, HD, -1), packed, zeros], axis=1)
        mine, give = at.halves(packed, 0)
        m_own = at.in_order(mine[0], at.swap(give[0]), 1)
        head_ids = ((at.t - jnp.arange(n_t, dtype=jnp.int32)) % n_t) * 2 + at.core
    else:
        m_own = None
        head_ids = at.core * heads + jnp.arange(heads, dtype=jnp.int32)
    mine, give = at.halves(tokens, 2)
    both = at.in_order(mine, at.swap(give), 0)
    both, m_own, gate_up_weight, down_weight, cotangent = sync(both, m_own, gate_up_weight, down_weight, cotangent)
    packed = jnp.concatenate([jnp.transpose(gate_up_weight, (1, 2, 0)), down_weight[None]], axis=0)
    mine, give = at.halves(packed, 1)
    f_own = at.in_order(mine, at.swap(give), 2)
    f_own = f_own.reshape(-1, f_own.shape[2])
    mine, give = at.halves(cotangent, 2)
    cot_both = at.in_order(mine, at.swap(give), 0)

    own = head_ids[:, None] == jnp.arange(heads_all, dtype=jnp.int32)[None, :]
    taps = jnp.pad(jnp.transpose(conv_w, (0, 2, 1)), ((0, 0), (0, 8 - TAPS), (0, 0)))
    conv_t = jnp.sum(jnp.where(own[:, :, None, None], taps[None], 0.0), axis=1)
    scal = jnp.stack(
        [
            jnp.sum(jnp.where(own, jnp.exp(decay_log)[None], 0.0), axis=1),
            jnp.sum(jnp.where(own, decay_bias[None], 0.0), axis=1),
        ],
        axis=1,
    )
    gain1 = at.relative(norm1_gain)
    gain2 = at.relative(norm2_gain)
    gain_o = out_gain[None]
    start_state = jnp.zeros((heads, HD, HD), F32)

    seq_id = jnp.minimum(at.k * per_chip + at.t, lengths.shape[0] - 1)
    length = jnp.where(at.t < per_chip, lax.dynamic_index_in_dim(lengths, seq_id, 0, keepdims=False), 0)
    live = (jnp.arange(seq, dtype=jnp.int32) < length).astype(BF16)[:, None]
    slot_ids = jnp.arange(perm.shape[0], dtype=jnp.int32)
    source = jnp.sum(jnp.where(perm[None, :] == slot_ids[:, None], slot_ids[None, :], 0), axis=1)
    quarter = dim // 4
    routes = [
        Routing(at, cot_both[:, :, :quarter], bits, source),
        Routing(at, cot_both[:, :, quarter:], bits[::-1], source),
    ]

    def route_state():
        return [r.have for r in routes]

    def set_routes(state):
        for r, v in zip(routes, state):
            r.have = v

    def routed():
        groups = [r.have for r in routes]
        return select_blocks(groups, jnp.concatenate([r.keep for r in routes], axis=0), per_chip)

    def sequence(half):
        half = half.reshape(seq, -1)
        return at.relative(at.in_order(half, at.swap(half), 1))

    def norm_first(x):
        return (x * rms_terms(x) * gain1).astype(BF16)

    f = Gather(at, f_own)
    proj = {}

    def asked():
        return select_blocks([r.have for r in routes], jnp.concatenate([r.ask for r in routes], axis=0), per_chip, True)

    if fast:
        m = Gather(at, m_own)

        def run(r):
            proj[r] = project(r, normed_one, m.full(r), conv_t, scal)

        def without(parts, *keys):
            return {k: v for k, v in parts.items() if k not in keys}

        came = at.spread_out(both)
        for p in range(1, chips):
            m.move(0, p, p)
        m.parts, f.parts, came, cot_both, conv_t, scal, gain1, gain2, live, extra = sync(
            m.parts, f.parts, came, cot_both, conv_t, scal, gain1, gain2, live, [(r.ask, r.keep) for r in routes]
        )
        for r, (ask, keep), part in zip(routes, extra, (cot_both[:, :, :quarter], cot_both[:, :, quarter:])):
            r.ask, r.keep, r.have = ask, keep, [part]
        m.turn(1)
        m.turn(3)
        for r in routes:
            r.step()
        x = sequence(came)
        normed_one = norm_first(x.astype(F32))
        run(0)
        state = route_state()
        m.parts, f.parts, state, proj[0], normed_one, x = sync(m.parts, f.parts, state, proj[0], normed_one, x)
        set_routes(state)
        for r in (1, 3):
            m.move(r, 1, 1)
            m.move(r, 2, 2)
        m.turn(2, 1)
        give = asked()
        m.parts, f.parts, give = sync(m.parts, f.parts, give)
        m.move(1, 3, 1)
        m.move(3, 3, 2)
        f.turn(1)
        m.parts, f.parts, give = sync(m.parts, f.parts, give)
        m.move(2, 1, 1)
        m.move(2, 2, 2)
        for r, part in zip(routes, give):
            r.last(part)
        f.turn(3)
        run(1)
        run(3)
        state = route_state()
        m.parts, proj, normed_one, f.parts, state = sync(m.parts, proj, normed_one, f.parts, state)
        set_routes(state)
        m.move(2, 3, 1)
        f.turn(2, 1)
        f.move(0, 1, 1)
        f.move(0, 2, 2)
        cot_home = routed()
        early = without(f.parts, (0, 1), (0, 2))
        m.parts, early, cot_home, normed_one = sync(m.parts, early, cot_home, normed_one)
        f.parts.update(early)
        cot_came = at.spread_out(cot_home)
        f.move(1, 1, 1)
        f.move(1, 2, 2)
        run(2)
        early = without(f.parts, (1, 1), (1, 2))
        proj, early = sync(proj, early)
        f.parts.update(early)
        m_parts = [m.full(r) for r in laps]
    else:
        x = sequence(at.spread_out(both))
        normed_one = norm_first(x.astype(F32))
        if by_turn:
            m_parts = Gather(at, m_own).rest()
        else:
            full = lax.all_gather(lax.all_gather(input_weight, "tp", axis=1, tiled=True), "fsdp", axis=0, tiled=True)
            full = at.relative(jnp.transpose(full, (1, 2, 0)))
            full_out = lax.all_gather(lax.all_gather(w_out, "tp", axis=0, tiled=True), "fsdp", axis=1, tiled=True)
            full_out = at.relative(full_out).reshape(heads_all, HD, dim)
            zeros = jnp.zeros((heads_all, pad, dim), BF16)
            full = at.halves(jnp.concatenate([full_out, full, zeros], axis=1), 0)[0]
            m_parts = [jnp.split(full[h], chips, axis=1) for h in range(heads)]
        for h in range(heads):
            proj[h] = project(h, normed_one, m_parts[h], conv_t, scal)
        for r in routes:
            for _ in bits[1:]:
                r.step()
        for r, part in zip(routes, asked()):
            r.last(part)
        cot_came = at.spread_out(routed())
        f_parts = f.rest()

    raw, gate, q, k, v, rows = (list(group) for group in zip(*[proj[h] for h in range(heads)]))
    if fast:
        f.move(0, 3, 2)
    first = recur(gain_o, start_state, q, k, v, gate, rows, 0, steps)
    if fast:
        first, f.parts, cot_came = sync(first, f.parts, cot_came)
        f.move(1, 3, 1)
        for r in (3, 2):
            f.move(r, 1, 1)
            f.move(r, 2, 2)
    second = recur(gain_o, first[1], q, k, v, gate, rows, steps, steps, first[0])
    if fast:
        early = without(f.parts, (2, 1), (2, 2))
        second, early = sync(second, early)
        f.parts.update(early)
    z = second[0]
    mix = mix_out(z, m_parts)
    mid = x.astype(F32) + (mix.astype(F32) + at.swap(mix).astype(F32))
    normed_two = (mid * rms_terms(mid) * gain2).astype(BF16)
    dy = live * sequence(cot_came)

    f_rs = Scatter(at)
    half = n_t // 2
    group_a, group_b = laps[:half], laps[half:][::-1]
    bits_a, bits_b = [first_bit(at, r) for r in group_a], [first_bit(at, r) for r in group_b]
    if fast:
        normed_two, dy, f.parts = sync(normed_two, dy, f.parts)
        f.move(2, 3, 1)
        f.move(3, 3, 2)
        f_parts = {r: f.full(r) for r in group_a}
    net, db, grads = ffn(normed_two, dy, [f_parts[r] for r in group_a], bits_a, last=False)
    if fast:
        net, db, grads, f.parts = sync(net, db, grads, f.parts)
        f_parts = {r: f.full(r) for r in group_b}
    for r, g in zip(group_a, grads):
        f_rs.put(r, g)
    if fast:
        f_rs.cross(0, 1)
    net, db, grads = ffn(normed_two, dy, [f_parts[r] for r in group_b], bits_b, (net, db))
    if fast:
        net, db, grads, state = sync(net, db, grads, f_rs.state())
        f_rs.take(state)
    for r, g in zip(group_b, grads):
        f_rs.put(r, g)

    db_other = at.swap(db)
    if fast:
        f_rs.fold(0, 1)
        f_rs.cross(3, 2)
    d_mix, dz, g_gain2, g_out = mix_back(gain2[None], db, db_other, mid, dy, z, m_parts)
    if fast:
        dz, d_mix, g_out, f_rs.two, net = sync(dz, d_mix, g_out, f_rs.two, net)
    net_other = at.swap(net)
    back = recur_back(gain_o, start_state, dz, q, k, v, gate, rows, *second[2:], steps, steps)
    if fast:
        back, state, net_other, dz = sync(back, f_rs.state(), net_other, dz)
        f_rs.take(state)
        f_rs.close(0, 1)
        f_rs.fold(3, 2)

    def give_back(value):
        mine = at.halves(at.relative(value.astype(BF16)), 1)[0]
        return mine.reshape(n_t, piece, dim // 2)

    def settle(came):
        mine, give = at.halves(came[:per_chip], 0)
        return at.in_order(mine, at.swap(give), 2)

    g_gain_o = back[2]
    out_home = give_back(live.astype(F32) * (mid + (net.astype(F32) + net_other.astype(F32))))
    out_came = lax.all_to_all(out_home, "tp", split_axis=0, concat_axis=0, tiled=True)
    back = recur_back(
        gain_o, back[3], dz, q, k, v, gate, rows, *first[2:], 0, steps, tuple(back[0]) + tuple(back[1])
    )
    g_gain_o = g_gain_o + back[2]
    ds, drows = back[:2]
    if fast:
        ds, drows, out_came, state = sync(ds, drows, out_came, f_rs.state())
        f_rs.take(state)
        f_rs.close(3, 2)
        f_rs.merge(2)
        f_rs.home(3)

    dps, g_conv, g_small = {}, {}, {}
    m_rs = Scatter(at, late=True)

    def run_back(h):
        dps[h], g_conv[h], g_small[h], grads = project_back(
            h, normed_one, conv_t, scal, raw[h], rows[h], ds[h], drows[h], g_out[h], m_rs.bit(h)
        )
        m_rs.put(h, grads)

    def moved(group, key):
        return {r: v for r, v in group.items() if r == key}

    if fast:
        run_back(2)
        dps, m_rs.near, m_rs.far, ds = sync(dps, m_rs.near, m_rs.far, ds)
        m_rs.cross(2)
        run_back(1)
        dps, m_rs.near, far, ds, f_state = sync(dps, m_rs.near, moved(m_rs.far, 1), ds, f_rs.state())
        m_rs.far.update(far)
        f_rs.take(f_state)
        f_rs.join(2)
        f_rs.home(1)
        m_rs.cross(1)
        run_back(3)
        dps, m_rs.near, m_rs.far, ds = sync(dps, m_rs.near, m_rs.far, ds)
        m_rs.fold(1, 2)
        m_rs.cross(3)
        run_back(0)
        far = {0: m_rs.far[0]}
        dps, m_rs.near, far, m_rs.two, f_rs.end = sync(dps, m_rs.near, far, m_rs.two, f_rs.end)
        m_rs.far.update(far)
        m_rs.close(1, 2)
        dps, m_rs.one = sync(dps, m_rs.one)
        m_rs.merge(2)
        m_rs.cross(0)
    else:
        for h in range(heads):
            run_back(h)
    output = settle(out_came)
    da, g_gain1 = input_back([dps[h] for h in range(heads)], m_parts, x)
    if fast:
        far = {3: m_rs.far[3]}
        da, g_gain1, far, m_rs.end = sync(da, g_gain1, far, m_rs.end)
        m_rs.far.update(far)
        m_rs.join(2)
        m_rs.home(1)
        m_rs.fold(3)
    da_other = at.swap(da)
    d_x_norm = rms_back(x.astype(F32), gain1, da.astype(F32) + da_other.astype(F32))
    dx_home = give_back(d_mix.astype(F32) + d_x_norm)

    small = [jnp.sum(g_small[h], axis=0) for h in range(heads)]
    conv_all = sum(jnp.where(own[h][:, None, None], g_conv[h][None, :TAPS], 0.0) for h in range(heads)).reshape(-1, HD)
    decay_all = sum(jnp.where(own[h][:, None], small[h][None], 0.0) for h in range(heads))
    gains = jnp.concatenate([at.relative(g_gain1[0]), 0.5 * at.relative(g_gain2[0])]).reshape(-1, HD)
    sums = jnp.concatenate([conv_all, decay_all, gains, g_gain_o], axis=0)
    if fast:
        dx_home, sums, m_rs.near, m_rs.end = sync(dx_home, at.line_sum(sums), m_rs.near, m_rs.end)
        m_rs.close(3)
        m_rs.home(3)
        m_rs.fold(0)
        sums = at.chip_sum(sums)
    else:
        sums = at.all_sum(sums)
    dx_came = lax.all_to_all(dx_home, "tp", split_axis=0, concat_axis=0, tiled=True)
    if fast:
        dx_came, m_rs.two, m_rs.end = sync(dx_came, m_rs.two, m_rs.end)
        m_rs.close(0)
    input_grad = settle(dx_came)
    n_conv = conv_all.shape[0]
    g_conv_all = jnp.transpose(sums[:n_conv].reshape(heads_all, TAPS, -1), (0, 2, 1))
    decay_sum = sums[n_conv : n_conv + heads_all]
    gain_sum = sums[n_conv + heads_all : -1].reshape(2, dim)

    def to_core(value, joined):
        mine, give = at.halves(value.astype(BF16), value.ndim - 1)
        return at.in_order(mine, at.swap(give), joined).astype(F32)

    if not fast:
        f_rs.rest()
    f_total = f_rs.total()
    g_ffn = to_core(f_total.reshape(3, -1, f_total.shape[1]), 1)
    grad_gate_up = jnp.transpose(g_ffn[:2], (2, 0, 1))
    grad_down = g_ffn[2]
    if by_turn:
        if not fast:
            m_rs.rest()
        joined = to_core(m_rs.total()[None], 0)
    else:
        joined = []
        for h in range(heads):
            have = {}
            for stack, group in zip((m_rs.near[h], m_rs.far[h]), sides(chips, m_rs.bit(h))):
                have.update({p: stack[i] for i, p in enumerate(group)})
            joined.append(jnp.concatenate([have[p] for p in range(chips)], axis=1))
        joined = jnp.stack(joined)
        spread = jnp.zeros((heads_all,) + joined.shape[1:], BF16)
        spread = lax.dynamic_update_slice_in_dim(spread, at.relative(joined), at.core * heads, 0)
        spread = lax.psum_scatter(spread, "tp", scatter_dimension=0, tiled=True)
        joined = lax.psum_scatter(spread, "fsdp", scatter_dimension=2, tiled=True).astype(F32)
    grad_in = jnp.transpose(joined[:, HD : HD + cols], (2, 0, 1))
    grad_out = joined[:, :HD].reshape(local_heads * HD, -1)
    return (
        output, input_grad, gain_sum[0], grad_in, g_conv_all, decay_sum[:, 0], decay_sum[:, 1], sums[-1], grad_out,
        gain_sum[1], grad_gate_up, grad_down
    )


def solution(mesh):
    tokens = P("fsdp", "tp", None)
    rows = P("tp", "fsdp")
    split = P("fsdp", None, "tp")
    return jax.shard_map(
        local,
        mesh=mesh,
        in_specs=(tokens, P(), P(), tokens, P(), tokens, P(), P(), P(), P(), rows, P(), split, rows),
        out_specs=(tokens, tokens, P(), tokens, P(), P(), P(), P(), rows, P(), split, rows),
        check_vma=False,
    )
```

```python
import functools

import jax
import jax.numpy as jnp
from jax import lax
from jax.experimental import pallas as pl
from jax.experimental.pallas import tpu as pltpu
from jax.sharding import PartitionSpec as P

HD = 128
NH = 2
SPAN = 64
SUB = SPAN * NH
TAPS = 4
SMALL = 16
UNITS = 6 * HD + SMALL
EPS_NORM = 1e-05
EPS_UNIT = 1e-06
F32 = jnp.float32
BF16 = jnp.bfloat16
FAR = -1e30
VMEM_BYTES = 56 * 1024 * 1024
EXACT = lax.Precision.HIGHEST


def params(**kw):
    return pltpu.CompilerParams(vmem_limit_bytes=VMEM_BYTES, **kw)


def cost(flops, nbytes, trans=0):
    return pl.CostEstimate(flops=int(flops), bytes_accessed=int(nbytes), transcendentals=int(trans))


def nn(a, b):
    return lax.dot_general(a, b, (((1,), (0,)), ((), ())), preferred_element_type=F32)


def nt(a, b):
    return lax.dot_general(a, b, (((1,), (1,)), ((), ())), preferred_element_type=F32)


def tn(a, b):
    return lax.dot_general(a, b, (((0,), (0,)), ((), ())), preferred_element_type=F32)


def exact_nn(a, b):
    return lax.dot_general(a, b, (((1,), (0,)), ((), ())), precision=EXACT, preferred_element_type=F32)


def sigmoid(v):
    return 1.0 / (1.0 + jnp.exp(-v))


def sides(pieces, bit):
    return [p for p in range(pieces) if not p & bit], [p for p in range(pieces) if p & bit]


def stacks(pieces, shape):
    return [jax.ShapeDtypeStruct((pieces // 2,) + shape, BF16)] * 2


def add_kernel(count, *refs):
    ins, outs = refs[: 2 * count], refs[2 * count :]
    for i in range(count):
        for j in range(2):
            outs[2 * i + j][...] = (ins[2 * i][j].astype(F32) + ins[2 * i + 1][j].astype(F32)).astype(BF16)


def add_stacks(pairs):
    flat = [v for pair in pairs for v in pair]
    steps = 3
    blocks = [pl.BlockSpec((2, v.shape[1] // steps, v.shape[2]), lambda i: (0, i, 0)) for v in flat]
    single = [pl.BlockSpec((v.shape[1] // steps, v.shape[2]), lambda i: (i, 0)) for v in flat]
    res = pl.pallas_call(
        functools.partial(add_kernel, len(pairs)),
        out_shape=[jax.ShapeDtypeStruct(v.shape[1:], BF16) for v in flat],
        grid=(steps,),
        in_specs=blocks,
        out_specs=single,
        compiler_params=params(),
        cost_estimate=cost(1e6, 1e6),
        name="add_stacks",
    )(*flat)
    return [res[2 * i : 2 * i + 2] for i in range(len(pairs))]


def lane_sum(value):
    return jnp.sum(value, axis=-1, keepdims=True)


def conv_shifts(ref, start, rows, lanes):
    window = ref[start : start + rows + 8, lanes]
    views = [pltpu.roll(window, TAPS - 1 - j, 0)[8 : 8 + rows] for j in range(TAPS - 1)]
    return views + [window[8 : 8 + rows]]


def conv_shifts_back(ref, start, rows, lanes):
    window = ref[start : start + rows + 8, lanes]
    views = [pltpu.roll(window, rows + 8 - (TAPS - 1 - j), 0)[:rows] for j in range(TAPS - 1)]
    return views + [window[:rows]]


def iota(shape, dim):
    return lax.broadcasted_iota(jnp.int32, shape, dim)


def project_kernel(pieces, h, scal_ref, a_ref, cw_ref, *refs):
    parts = refs[:pieces]
    raw_ref, gate_ref, q_ref, k_ref, v_ref, rows_ref, raw_s, mix_s, aux_s = refs[pieces:]
    tile = a_ref.shape[0]
    depth = parts[0].shape[1]
    head = 8

    @pl.when(pl.program_id(0) == 0)
    def _():
        raw_s[0:head, :] = jnp.zeros_like(raw_s[0:head, :])

    @pl.when(pl.program_id(0) > 0)
    def _():
        raw_s[0:head, :] = raw_s[tile : tile + head, :]

    acc = jnp.zeros((tile, UNITS), F32)
    for p in range(pieces):
        acc += nt(a_ref[:, p * depth : (p + 1) * depth], parts[p][HD:])
    raw_s[head : tile + head, :] = acc[:, : 5 * HD]
    raw_ref[...] = acc[:, : 5 * HD].astype(BF16)
    gate_ref[...] = acc[:, 5 * HD : 6 * HD].astype(BF16)

    small = acc[:, 6 * HD :]
    rate, bias = scal_ref[h, 0], scal_ref[h, 1]
    arg = small[:, 2:3] + bias
    soft = jnp.maximum(arg, 0.0) + jnp.log(1.0 + jnp.exp(-jnp.abs(arg)))
    beta = sigmoid(small[:, 0:2])
    lane = iota((tile, HD), 1)
    aux_s[pl.ds(0, tile, 2), :] = jnp.where(
        lane == 0, beta[:, 0:1], jnp.where(lane == 1, -rate * soft, jnp.where(lane == 2, arg, 0.0))
    )
    aux_s[pl.ds(1, tile, 2), :] = jnp.where(lane == 0, beta[:, 1:2], 0.0)
    upper = jnp.where(iota((SUB, SUB), 0) <= iota((SUB, SUB), 1), 1.0, 0.0)
    for b in range(tile // SPAN):
        rows = jnp.transpose(aux_s[b * SUB : (b + 1) * SUB, :])[:8]
        cum = exact_nn(rows, upper)
        rows_ref[b] = jnp.where(iota((8, SUB), 0) == 3, cum[1:2], rows)

    chunk = 64
    for g in range(5):
        taps = cw_ref[0, :, g * HD : (g + 1) * HD]
        for i in range(tile // chunk):
            start = i * chunk
            views = conv_shifts(raw_s, start, chunk, slice(g * HD, (g + 1) * HD))
            pre = views[0] * taps[0:1]
            for j in range(1, TAPS):
                pre += views[j] * taps[j : j + 1]
            act = pre * sigmoid(pre)
            if g < 3:
                act = act * lax.rsqrt(lane_sum(act * act) + EPS_UNIT)
            if g == 0:
                q_ref[start : start + chunk, :] = act.astype(BF16)
            else:
                mix_s[pl.ds(2 * start + (g + 1) % 2, chunk, 2), :] = act
        if g in (2, 4):
            (k_ref if g == 2 else v_ref)[...] = mix_s[...].astype(BF16)


def project(h, normed, parts, conv_t, scal):
    seq, dim = normed.shape
    pieces = len(parts)
    tile = min(256, seq)
    fix = lambda i: (0, 0)
    along = lambda i: (i, 0)
    outs = [((seq, 5 * HD), BF16, 1), ((seq, HD), BF16, 1), ((seq, HD), BF16, 1), ((NH * seq, HD), BF16, NH), ((NH * seq, HD), BF16, NH)]
    return pl.pallas_call(
        functools.partial(project_kernel, pieces, h),
        out_shape=[jax.ShapeDtypeStruct(s, d) for s, d, _ in outs] + [jax.ShapeDtypeStruct((seq // SPAN, 8, SUB), F32)],
        grid=(seq // tile,),
        in_specs=[
            pl.BlockSpec(memory_space=pltpu.SMEM),
            pl.BlockSpec((tile, dim), along),
            pl.BlockSpec((1,) + conv_t.shape[1:], lambda i: (h, 0, 0)),
        ]
        + [pl.BlockSpec(w.shape, fix) for w in parts],
        out_specs=[pl.BlockSpec((tile * n, s[1]), along) for s, _, n in outs]
        + [pl.BlockSpec((tile // SPAN, 8, SUB), lambda i: (i, 0, 0))],
        scratch_shapes=[
            pltpu.VMEM((tile + 8, 5 * HD), F32),
            pltpu.VMEM((NH * tile, HD), F32),
            pltpu.VMEM((NH * tile, HD), F32),
        ],
        compiler_params=params(),
        cost_estimate=cost(2 * seq * dim * UNITS, 8e6),
        name="project",
    )(scal, normed, conv_t, *parts)


BASE = 16


def unit_lower_inverses(lowers):
    n, groups = SUB, SUB // BASE
    lane = iota((BASE, n), 1)
    group = lane // BASE
    packed = []
    for low in lowers:
        p = jnp.where(group == 0, low[:BASE], 0.0)
        for b in range(1, groups):
            p = jnp.where(group == b, low[b * BASE : (b + 1) * BASE], p)
        packed.append(p)
    eye = jnp.where(lane % BASE == iota((BASE, n), 0), 1.0, 0.0)
    invs = [eye] * len(lowers)
    first = group * BASE
    for j in range(BASE - 1):
        coefs = [jnp.take_along_axis(p, first + j, axis=1) for p in packed]
        invs = [x - c * x[j : j + 1] for x, c in zip(invs, coefs)]
    fulls = [
        jnp.concatenate([jnp.where(group == b, x, 0.0).astype(BF16) for b in range(groups)], axis=0) for x in invs
    ]
    row, col = iota((n, n), 0), iota((n, n), 1)
    size = BASE
    while size < n:
        odd = range(1, n // size, 2)
        mask = jnp.logical_and(row // size == col // size + 1, row // (2 * size) == col // (2 * size))
        crosses = [jnp.where(mask, low, 0.0).astype(BF16) for low in lowers]
        picks = [jnp.concatenate([f[b * size : (b + 1) * size] for b in odd], axis=0) for f in fulls]
        halves = [nn(p, c).astype(BF16) for p, c in zip(picks, crosses)]
        belows = [(p.astype(F32) - nn(h, f)).astype(BF16) for p, h, f in zip(picks, halves, fulls)]
        fulls = [
            jnp.concatenate(
                [
                    below[(b // 2) * size : (b // 2 + 1) * size] if b % 2 else f[b * size : (b + 1) * size]
                    for b in range(n // size)
                ],
                axis=0,
            )
            for f, below in zip(fulls, belows)
        ]
        size *= 2
    return fulls


def turned(value, eye):
    return nt(eye, value)


def decay_terms(rows_ref, cums, items):
    out = []
    pick_row = iota((8, SUB), 0)
    for i, (b, h) in enumerate(items):
        rows = rows_ref[h][b]
        g = rows[3:4, :]
        g_last = g[:, SUB - 1 :]
        e = jnp.exp(g)
        wide = jnp.where(pick_row == 1, e, jnp.where(pick_row == 2, jnp.exp(g_last - g), rows))
        wide = jnp.where(pick_row == 4, rows[0:1, :] * e, wide)
        cols = jnp.transpose(jnp.concatenate([wide] * (SUB // 8), axis=0))
        cums[i] = cols
        c_col = cums[i, pl.ds(1, SPAN, 2), :][:, 3:4]
        out.append((cols[:, 0:1], cols[:, 1:2], cols[:, 2:3], cols[:, 3:4], cols[:, 4:5], g, c_col, g_last))
    return out


PER_STEP = 2


def recur_kernel(heads, more, gain_ref, start_ref, *refs):
    q_r, k_r, v_r, g_r, rows_r = (refs[i * heads : (i + 1) * heads] for i in range(5))
    refs = refs[: 5 * heads] + refs[5 * heads + more :]
    z_ref, end_ref = refs[5 * heads : 5 * heads + 2]
    o_r = refs[5 * heads + 2 : 6 * heads + 2]
    u_r = refs[6 * heads + 2 : 7 * heads + 2]
    s_ref, t_ref, cums = refs[7 * heads + 2 :]

    @pl.when(pl.program_id(0) == 0)
    def _():
        end_ref[...] = start_ref[...]

    row, col = iota((SUB, SUB), 0), iota((SUB, SUB), 1)
    strict = col < row
    vis = iota((SPAN, SUB), 1) // NH <= iota((SPAN, SUB), 0)
    items = [(b, h) for b in range(PER_STEP) for h in range(heads)]
    tok = [pl.ds(b * SPAN, SPAN) for b, _ in items]
    sub = [pl.ds(b * SUB, SUB) for b, _ in items]
    eye = jnp.where(row == col, 1.0, 0.0).astype(BF16)
    terms = decay_terms(rows_r, cums, items)
    ks = [k_r[h][sub[i]] for i, (b, h) in enumerate(items)]
    qs = [q_r[h][tok[i]] for i, (b, h) in enumerate(items)]
    prods = [nt(jnp.concatenate([k, q], axis=0), k) for k, q in zip(ks, qs)]
    lowers = [
        t[0] * jnp.exp(jnp.where(strict, t[3] - t[5], FAR)) * p[:SUB] for p, t in zip(prods, terms)
    ]
    inner = [(jnp.exp(jnp.where(vis, t[6] - t[5], FAR)) * p[SUB:]).astype(BF16) for p, t in zip(prods, terms)]
    inverses = unit_lower_inverses(lowers)
    for (b, h), inv in zip(items, inverses):
        t_ref[b, h] = inv
    solved, backs = [], []
    for i, (b, h) in enumerate(items):
        t = terms[i]
        k = ks[i].astype(F32)
        right = jnp.concatenate([t[0] * v_r[h][sub[i]].astype(F32), t[4] * k], axis=1)
        solved.append(nn(inverses[i], right.astype(BF16)))
        weighted = turned((t[2] * k).astype(BF16), eye).astype(BF16)
        backs.append(jnp.concatenate([weighted, inner[i]], axis=0))
    gain = gain_ref[...]
    for b in range(PER_STEP):
        mine = [i for i, it in enumerate(items) if it[0] == b]
        olds = [end_ref[items[i][1]] for i in mine]
        old_bs = [o.astype(BF16) for o in olds]
        reads = [
            nn(jnp.concatenate([solved[i][:, HD:].astype(BF16), qs[i]], axis=0), ob) for i, ob in zip(mine, old_bs)
        ]
        ubs = [(solved[i][:, :HD] - r[:SUB]).astype(BF16) for i, r in zip(mine, reads)]
        adds = [nn(backs[i], ub) for i, ub in zip(mine, ubs)]
        for i, old, ob, r, ub, add in zip(mine, olds, old_bs, reads, ubs, adds):
            h = items[i][1]
            c_col, g_last = terms[i][6:]
            end_ref[h] = jnp.exp(g_last) * old + add[:HD]
            s_ref[b, h] = ob
            u_r[h][sub[i], :] = ub
            o = jnp.exp(c_col) * r[SUB:] + add[HD:]
            o_r[h][tok[i], :] = o.astype(BF16)
            scaled = o * lax.rsqrt(jnp.mean(o * o, axis=-1, keepdims=True) + EPS_NORM) * gain
            gate = g_r[h][tok[i]].astype(F32)
            z_ref[tok[i], h * HD : (h + 1) * HD] = (scaled * gate * sigmoid(gate)).astype(BF16)


def recur_specs(heads, at):
    tok = pl.BlockSpec((PER_STEP * SPAN, HD), lambda i: (at(i), 0))
    sub = pl.BlockSpec((PER_STEP * SUB, HD), lambda i: (at(i), 0))
    rows = pl.BlockSpec((PER_STEP, 8, SUB), lambda i: (at(i), 0, 0))
    wide = pl.BlockSpec((PER_STEP * SPAN, heads * HD), lambda i: (at(i), 0))
    mat = pl.BlockSpec((PER_STEP, heads, HD, HD), lambda i: (at(i), 0, 0, 0))
    one = pl.BlockSpec((1, HD), lambda i: (0, 0))
    state = pl.BlockSpec((heads, HD, HD), lambda i: (0, 0, 0))
    return tok, sub, rows, wide, mat, one, state


def recur(gain, start, q, k, v, gate, rows, first, steps, z=None):
    heads = len(q)
    tok, sub, row, wide, mat, one, state = recur_specs(heads, lambda i: i + first)
    o_tok, o_sub, _, _, o_mat, _, _ = recur_specs(heads, lambda i: i)
    n = steps * PER_STEP
    more = [] if z is None else [z]

    def shape(s, d):
        return jax.ShapeDtypeStruct(s, d)

    res = pl.pallas_call(
        functools.partial(recur_kernel, heads, len(more)),
        out_shape=[shape((q[0].shape[0], heads * HD), BF16), shape((heads, HD, HD), F32)]
        + [shape((n * SPAN, HD), BF16)] * heads
        + [shape((n * SUB, HD), BF16)] * heads
        + [shape((n, heads, HD, HD), BF16)] * 2,
        grid=(steps,),
        in_specs=[one, state]
        + [tok] * heads
        + [sub] * (2 * heads)
        + [tok] * heads
        + [row] * heads
        + [pl.BlockSpec(memory_space=pl.ANY)] * len(more),
        out_specs=[wide, state] + [o_tok] * heads + [o_sub] * heads + [o_mat] * 2,
        scratch_shapes=[pltpu.VMEM((PER_STEP * heads, SUB, SUB), F32)],
        compiler_params=params(),
        input_output_aliases={2 + 5 * heads: 0} if more else {},
        cost_estimate=cost(heads * n * 20 * 4.2e6, 1e6),
        name="recur",
    )(gain, start, *q, *k, *v, *gate, *rows, *more)
    return res[0], res[1], res[2 : 2 + heads], res[2 + heads : 2 + 2 * heads], res[2 + 2 * heads], res[3 + 2 * heads]


def recur_back_kernel(heads, more, gain_ref, start_ref, dz_ref, *refs):
    q_r, k_r, v_r, g_r, rows_r, o_r, u_r = (refs[i * heads : (i + 1) * heads] for i in range(7))
    s_ref, t_ref = refs[7 * heads : 7 * heads + 2]
    refs = refs[: 7 * heads + 2] + refs[7 * heads + 2 + more :]
    d_r = refs[7 * heads + 2 : 8 * heads + 2]
    drows_r = refs[8 * heads + 2 : 9 * heads + 2]
    dgain_ref, end_ref, cums, mixed = refs[9 * heads + 2 :]

    @pl.when(pl.program_id(0) == 0)
    def _():
        end_ref[...] = start_ref[...]
        dgain_ref[...] = jnp.zeros_like(dgain_ref)

    row, col = iota((SUB, SUB), 0), iota((SUB, SUB), 1)
    strict = col < row
    later = jnp.where(row >= col, 1.0, 0.0)
    vis = iota((SPAN, SUB), 1) // NH <= iota((SPAN, SUB), 0)
    gain = gain_ref[...]
    items = [(b, h) for b in reversed(range(PER_STEP)) for h in range(heads)]
    every = range(len(items))
    tok = [pl.ds(b * SPAN, SPAN) for b, _ in items]
    sub = [pl.ds(b * SUB, SUB) for b, _ in items]
    terms = decay_terms(rows_r, cums, items)
    ks = [k_r[h][sub[i]] for i, (b, h) in enumerate(items)]
    qs = [q_r[h][tok[i]] for i, (b, h) in enumerate(items)]
    us = [u_r[h][sub[i]] for i, (b, h) in enumerate(items)]
    ss = [s_ref[b, h] for b, h in items]
    prods = [nt(jnp.concatenate([k, q], axis=0), k) for k, q in zip(ks, qs)]

    dos = []
    dgain = jnp.zeros((1, HD), F32)
    for i, (b, h) in enumerate(items):
        dz = dz_ref[tok[i], h * HD : (h + 1) * HD].astype(F32)
        o = o_r[h][tok[i]].astype(F32)
        gate = g_r[h][tok[i]].astype(F32)
        inv_rms = lax.rsqrt(jnp.mean(o * o, axis=-1, keepdims=True) + EPS_NORM)
        n = o * inv_rms
        sg = sigmoid(gate)
        dy = dz * gate * sg
        d_r[h][tok[i], 5 * HD :] = (dz * n * gain * sg * (1.0 + gate * (1.0 - sg))).astype(BF16)
        dgain += jnp.sum(dy * n, axis=0, keepdims=True)
        dn = dy * gain
        dos.append((inv_rms * (dn - n * jnp.mean(dn * n, axis=-1, keepdims=True))).astype(BF16))
    dgain_ref[...] += dgain

    eye = jnp.where(row == col, 1.0, 0.0).astype(BF16)
    reads = [jnp.exp(jnp.where(vis, t[6] - t[5], FAR)) for t in terms]
    ecs = [jnp.exp(t[6]) for t in terms]
    kfs = [k.astype(F32) for k in ks]
    qfs = [q.astype(F32) for q in qs]
    lefts = [
        jnp.concatenate([turned((p[SUB:] * r).astype(BF16), eye).astype(BF16), (t[2] * k).astype(BF16)], axis=1)
        for p, r, t, k in zip(prods, reads, terms, kfs)
    ]
    downs = [
        turned(jnp.concatenate([(ec * q).astype(BF16), (-t[4] * k).astype(BF16)], axis=0), eye).astype(BF16)
        for ec, q, t, k in zip(ecs, qfs, terms, kfs)
    ]
    solves = [turned(t_ref[b, h], eye).astype(BF16) for b, h in items]

    drs, dsbs, dots = [None] * len(items), [None] * len(items), [None] * len(items)
    for b in reversed(range(PER_STEP)):
        mine = [i for i, it in enumerate(items) if it[0] == b]
        dss = {i: end_ref[items[i][1]] for i in mine}
        for i in mine:
            dsbs[i] = dss[i].astype(BF16)
            dots[i] = jnp.sum(dss[i] * ss[i].astype(F32), axis=0, keepdims=True)
        dus = {i: nn(lefts[i], jnp.concatenate([dos[i], dsbs[i]], axis=0)).astype(BF16) for i in mine}
        for i in mine:
            drs[i] = nn(solves[i], dus[i])
        for i in mine:
            add = nn(downs[i], jnp.concatenate([dos[i], drs[i].astype(BF16)], axis=0))
            end_ref[items[i][1]] = jnp.exp(terms[i][7]) * dss[i] + add

    drbs = [d.astype(BF16) for d in drs]
    from_s = [nt(jnp.concatenate([a, c], axis=0), s) for a, c, s in zip(drbs, dos, ss)]
    from_u = [nt(jnp.concatenate([a, c], axis=0), u) for a, c, u in zip(drbs, dos, us)]
    ks0 = [nn(k, s) for k, s in zip(ks, ss)]
    dws = [nt(u, d) for u, d in zip(us, dsbs)]
    dgs, dbs, dks, minus, dcs, syms = [], [], [], [], [], []
    nms = []
    for i, (b, h) in enumerate(items):
        beta, e_col, e_rest, g_col, beta_e, g_row, c_col, g_last = terms[i]
        k, q = kfs[i], qfs[i]
        mixed[i] = beta * drs[i]
        d_r[h][tok[i], 3 * HD : 4 * HD] = mixed[i, pl.ds(0, SPAN, 2), :].astype(BF16)
        d_r[h][tok[i], 4 * HD : 5 * HD] = mixed[i, pl.ds(1, SPAN, 2), :].astype(BF16)
        t1 = beta_e * from_s[i][:SUB]
        t3 = e_rest * dws[i]
        fade = jnp.exp(jnp.where(strict, g_col - g_row, FAR))
        y = -from_u[i][:SUB] * fade
        le = y * prods[i][:SUB]
        hh = beta * le
        kt3 = k * t3
        dbs.append(lane_sum(drs[i] * (v_r[h][sub[i]].astype(F32) - e_col * ks0[i]) + le))
        dg = lane_sum(hh - k * t1 - kt3)
        d_last = lane_sum(jnp.sum(kt3, axis=0, keepdims=True) + jnp.exp(g_last) * dots[i])
        dgs.append(dg + jnp.where(row[:, :1] == SUB - 1, d_last, 0.0))
        dks.append(t3 - t1)
        dkk = beta * y
        syms.append(dkk + turned(dkk.astype(BF16), eye))
        nm = from_u[i][SUB:] * reads[i]
        hm = nm * prods[i][SUB:]
        t2 = ecs[i] * from_s[i][SUB:]
        nms.append((nm.astype(BF16), t2))
        dcs.append(lane_sum(hm + q * t2))
        minus.append(jnp.sum(hh, axis=0, keepdims=True) + jnp.sum(hm, axis=0, keepdims=True))
    tops = [
        nn(jnp.concatenate([s.astype(BF16), nm], axis=0), k) for s, (nm, _), k in zip(syms, nms, ks)
    ]
    turns = [nn(turned(nm, eye).astype(BF16), q) for (nm, _), q in zip(nms, qs)]
    for i, (b, h) in enumerate(items):
        d_r[h][tok[i], :HD] = (tops[i][SUB:] + nms[i][1]).astype(BF16)
        mixed[i] = dks[i] + tops[i][:SUB] + turns[i]
        d_r[h][tok[i], HD : 2 * HD] = mixed[i, pl.ds(0, SPAN, 2), :].astype(BF16)
        d_r[h][tok[i], 2 * HD : 3 * HD] = mixed[i, pl.ds(1, SPAN, 2), :].astype(BF16)
        cums[i] = jnp.where(col == 0, dbs[i], jnp.where(col == 1, dgs[i], 0.0))
        odd = pl.ds(1, SPAN, 2)
        cums[i, odd, :] = cums[i, odd, :] + jnp.where(col[:SPAN] == 1, dcs[i], 0.0)
        rows = jnp.transpose(cums[i])[:8]
        first = iota((8, SUB), 0)
        summed = exact_nn(rows - jnp.where(first == 1, minus[i], 0.0), later)
        drows_r[h][b] = jnp.where(first == 0, rows, summed)


def recur_back(gain, start, dz, q, k, v, gate, rows, o, u, s, t, first, steps, done=()):
    heads = len(q)
    tok, sub, row, wide, mat, one, state = recur_specs(heads, lambda i: first + steps - 1 - i)
    o_tok, o_sub, _, _, o_mat, _, _ = recur_specs(heads, lambda i: steps - 1 - i)
    n = steps * PER_STEP
    seq = q[0].shape[0]
    d_spec = pl.BlockSpec((PER_STEP * SPAN, 6 * HD), lambda i: (first + steps - 1 - i, 0))

    def shape(s, d):
        return jax.ShapeDtypeStruct(s, d)

    res = pl.pallas_call(
        functools.partial(recur_back_kernel, heads, len(done)),
        out_shape=[shape((seq, 6 * HD), BF16)] * heads
        + [shape((seq // SPAN, 8, SUB), F32)] * heads
        + [shape((1, HD), F32), shape((heads, HD, HD), F32)],
        grid=(steps,),
        in_specs=[one, state, wide]
        + [tok] * heads
        + [sub] * (2 * heads)
        + [tok] * heads
        + [row] * heads
        + [o_tok] * heads
        + [o_sub] * heads
        + [o_mat] * 2
        + [pl.BlockSpec(memory_space=pl.ANY)] * len(done),
        out_specs=[d_spec] * heads + [row] * heads + [one, state],
        scratch_shapes=[pltpu.VMEM((PER_STEP * heads, SUB, SUB), F32)] * 2,
        compiler_params=params(),
        input_output_aliases={5 + 7 * heads + i: i for i in range(len(done))},
        cost_estimate=cost(heads * n * 30 * 4.2e6, 1e6),
        name="recur_back",
    )(gain, start, dz, *q, *k, *v, *gate, *rows, *o, *u, s, t, *done)
    return res[:heads], res[heads : 2 * heads], res[2 * heads], res[2 * heads + 1]


def project_back_kernel(pieces, bit, h, scal_ref, a_ref, cw_ref, raw_ref, rows_ref, d_ref, drow_ref, *refs):
    outer, refs = refs[:pieces], refs[pieces:]
    dp_ref, dcw_ref, dsm_ref = refs[:3]
    stacked = refs[3:5]
    raw_s, ds_s, acc, aux_s = refs[5:]
    tile = a_ref.shape[0]
    depth = outer[0].shape[1]
    chunk = 64
    step, steps = pl.program_id(0), pl.num_programs(0)
    base = pl.multiple_of((steps - 1 - step) * tile, tile)

    @pl.when(step == 0)
    def _():
        ds_s[tile : tile + 8, :] = jnp.zeros_like(ds_s[tile : tile + 8, :])
        dcw_ref[...] = jnp.zeros_like(dcw_ref)
        dsm_ref[...] = jnp.zeros_like(dsm_ref)

    @pl.when(step > 0)
    def _():
        ds_s[tile : tile + 8, :] = ds_s[0:8, :]

    @pl.when(step == steps - 1)
    def _():
        raw_s[0:8, :] = jnp.zeros_like(raw_s[0:8, :])

    @pl.when(step < steps - 1)
    def _():
        before = raw_ref[pl.ds(pl.multiple_of(base - 16, 16), 16), :].astype(F32)
        raw_s[0:8, :] = before[8:]

    raw_s[8 : tile + 8, :] = raw_ref[pl.ds(base, tile), :].astype(F32)
    for g in range(5):
        lanes = slice(g * HD, (g + 1) * HD)
        taps = cw_ref[0, :, lanes]
        sums = [jnp.zeros((8, HD), F32)] * TAPS
        for i in range(tile // chunk):
            start = i * chunk
            shifted = conv_shifts(raw_s, start, chunk, lanes)
            pre = shifted[0] * taps[0:1]
            for j in range(1, TAPS):
                pre = pre + shifted[j] * taps[j : j + 1]
            sg = sigmoid(pre)
            act = pre * sg
            d = d_ref[start : start + chunk, lanes].astype(F32)
            if g < 3:
                inv = lax.rsqrt(lane_sum(act * act) + EPS_UNIT)
                unit = act * inv
                d = inv * (d - unit * lane_sum(d * unit))
            d = d * (sg + act * (1.0 - sg))
            ds_s[start : start + chunk, lanes] = d
            sums = [s + jnp.sum((d * x).reshape(chunk // 8, 8, HD), axis=0) for s, x in zip(sums, shifted)]
        for j in range(TAPS):
            dcw_ref[j : j + 1, lanes] += jnp.sum(sums[j], axis=0, keepdims=True)
        for i in range(tile // chunk):
            start = i * chunk
            views = conv_shifts_back(ds_s, start, chunk, lanes)
            total = views[0] * taps[0:1]
            for j in range(1, TAPS):
                total = total + views[j] * taps[j : j + 1]
            dp_ref[start : start + chunk, lanes] = total.astype(BF16)

    rate = scal_ref[h, 0]
    lane = iota((SPAN, HD), 1)
    total = jnp.zeros((8, HD), F32)
    for b in range(tile // SPAN):
        both = jnp.concatenate([rows_ref[b], drow_ref[b]] + [jnp.zeros((8, SUB), F32)] * (SUB // 8 - 2), axis=0)
        aux_s[b] = jnp.transpose(both)
        even, odd = aux_s[b, pl.ds(0, SPAN, 2), :], aux_s[b, pl.ds(1, SPAN, 2), :]
        b1, b2, dg = even[:, 0:1], odd[:, 0:1], even[:, 9:10]
        darg = -rate * dg * sigmoid(even[:, 2:3])
        d1 = even[:, 8:9] * b1 * (1.0 - b1)
        d2 = odd[:, 8:9] * b2 * (1.0 - b2)
        vals = jnp.where(lane == 0, d1, jnp.where(lane == 1, d2, jnp.where(lane == 2, darg, 0.0)))
        here = pl.ds(b * SPAN, SPAN)
        dp_ref[here, 6 * HD :] = vals[:, :SMALL].astype(BF16)
        dp_ref[here, 5 * HD : 6 * HD] = d_ref[here, 5 * HD :]
        extra = jnp.where(lane == 0, dg * even[:, 1:2], jnp.where(lane == 1, darg, 0.0))
        total += jnp.sum(extra.reshape(SPAN // 8, 8, HD), axis=0)
    dsm_ref[...] += total

    term = tn(dp_ref[...], a_ref[...])

    @pl.when(step == 0)
    def _():
        acc[...] = term

    @pl.when(step > 0)
    def _():
        acc[...] += term

    @pl.when(step == steps - 1)
    def _():
        for stack, group in zip(stacked, sides(pieces, bit)):
            for i, p in enumerate(group):
                stack[i, :HD] = outer[p][...]
                stack[i, HD:] = acc[:, p * depth : (p + 1) * depth].astype(BF16)


def project_back(h, normed, conv_t, scal, raw, rows, d, drows, outer, bit):
    seq, dim = normed.shape
    pieces = len(outer)
    depth = outer[0].shape[1]
    tile = min(512, seq)
    end = seq // tile - 1
    along = lambda i: (end - i, 0)
    deep = pl.BlockSpec((tile // SPAN, 8, SUB), lambda i: (end - i, 0, 0))
    fix = lambda i: (0, 0)
    outs = [((seq, UNITS), BF16), ((8, 5 * HD), F32), ((8, HD), F32)]
    shapes = [jax.ShapeDtypeStruct(s, t) for s, t in outs] + stacks(pieces, (HD + UNITS, depth))
    res = pl.pallas_call(
        functools.partial(project_back_kernel, pieces, bit, h),
        out_shape=shapes,
        grid=(seq // tile,),
        in_specs=[
            pl.BlockSpec(memory_space=pltpu.SMEM),
            pl.BlockSpec((tile, dim), along),
            pl.BlockSpec((1,) + conv_t.shape[1:], lambda i: (h, 0, 0)),
            pl.BlockSpec(raw.shape, fix),
            deep,
            pl.BlockSpec((tile, 6 * HD), along),
            deep,
        ]
        + [pl.BlockSpec(g.shape, fix) for g in outer],
        out_specs=[pl.BlockSpec((tile, UNITS), along)]
        + [pl.BlockSpec(s, fix) for s, _ in outs[1:]]
        + [pl.BlockSpec(v.shape, lambda i: (0, 0, 0)) for v in shapes[3:]],
        scratch_shapes=[
            pltpu.VMEM((tile + 8, 5 * HD), F32),
            pltpu.VMEM((tile + 8, 5 * HD), F32),
            pltpu.VMEM((UNITS, dim), F32),
            pltpu.VMEM((tile // SPAN, SUB, SUB), F32),
        ],
        compiler_params=params(),
        cost_estimate=cost(2 * seq * dim * UNITS, 1e6),
        name="project_back",
    )(scal, normed, conv_t, raw, rows, d, drows, *outer)
    return res[0], res[1], res[2], res[3:]


def input_back_kernel(heads, pieces, *refs):
    dps, parts = refs[:heads], refs[heads : heads + heads * pieces]
    x_ref, da_ref, dgain_ref = refs[heads + heads * pieces :]
    depth = parts[0].shape[1]
    x = x_ref[...].astype(F32)
    unit = x * lax.rsqrt(jnp.mean(x * x, axis=-1, keepdims=True) + EPS_NORM)
    shares = []
    for p in range(pieces):
        total = nn(
            jnp.concatenate([d[:, 6 * HD :] for d in dps], axis=1),
            jnp.concatenate([parts[h * pieces + p][7 * HD :] for h in range(heads)], axis=0),
        )
        for h in range(heads):
            total += nn(dps[h][:, : 6 * HD], parts[h * pieces + p][HD : 7 * HD])
        low = total.astype(BF16)
        lanes = slice(p * depth, (p + 1) * depth)
        da_ref[:, lanes] = low
        shares.append(jnp.sum(low.astype(F32) * unit[:, lanes], axis=0, keepdims=True))
    share = jnp.concatenate(shares, axis=1)

    @pl.when(pl.program_id(0) == 0)
    def _():
        dgain_ref[...] = share

    @pl.when(pl.program_id(0) > 0)
    def _():
        dgain_ref[...] += share


def input_back(dps, parts, x):
    seq = dps[0].shape[0]
    heads, pieces = len(parts), len(parts[0])
    flat = [w for head in parts for w in head]
    dim = pieces * flat[0].shape[1]
    tile = min(256, seq)
    along = lambda i: (i, 0)
    return pl.pallas_call(
        functools.partial(input_back_kernel, heads, pieces),
        out_shape=[jax.ShapeDtypeStruct((seq, dim), BF16), jax.ShapeDtypeStruct((1, dim), F32)],
        grid=(seq // tile,),
        in_specs=[pl.BlockSpec((tile, UNITS), along)] * heads
        + [pl.BlockSpec(w.shape, lambda i: (0, 0)) for w in flat]
        + [pl.BlockSpec((tile, dim), along)],
        out_specs=[pl.BlockSpec((tile, dim), along), pl.BlockSpec((1, dim), lambda i: (0, 0))],
        compiler_params=params(),
        cost_estimate=cost(2 * seq * dim * UNITS * heads, 1e6),
        name="input_back",
    )(*dps, *flat, x)


def mix_kernel(heads, pieces, z_ref, *refs):
    parts, out_ref = refs[:-1], refs[-1]
    depth = parts[0].shape[1]
    for p in range(pieces):
        right = jnp.concatenate([parts[h * pieces + p][...] for h in range(heads)], axis=0)
        out_ref[:, p * depth : (p + 1) * depth] = nn(z_ref[...], right).astype(BF16)


def outer_specs(parts):
    return [pl.BlockSpec((HD, w.shape[1]), lambda i: (0, 0)) for head in parts for w in head]


def mix_out(z, parts):
    seq = z.shape[0]
    heads, pieces = len(parts), len(parts[0])
    dim = pieces * parts[0][0].shape[1]
    tile = min(256, seq)
    along = lambda i: (i, 0)
    return pl.pallas_call(
        functools.partial(mix_kernel, heads, pieces),
        out_shape=jax.ShapeDtypeStruct((seq, dim), BF16),
        grid=(seq // tile,),
        in_specs=[pl.BlockSpec((tile, z.shape[1]), along)] + outer_specs(parts),
        out_specs=pl.BlockSpec((tile, dim), along),
        compiler_params=params(),
        cost_estimate=cost(2 * seq * dim * z.shape[1], 1e6),
        name="mix_out",
    )(z, *[w for head in parts for w in head])


def mix_back_kernel(heads, pieces, gain_ref, own_ref, other_ref, mid_ref, dy_ref, z_ref, *refs):
    parts, refs = refs[: heads * pieces], refs[heads * pieces :]
    dmix_ref, dz_ref, dgain_ref = refs[:3]
    grads, acc = refs[3:-1], refs[-1]
    depth = parts[0].shape[1]
    step, steps = pl.program_id(0), pl.num_programs(0)
    mid = mid_ref[...]
    dn = own_ref[...].astype(F32) + other_ref[...].astype(F32)
    inv = lax.rsqrt(jnp.mean(mid * mid, axis=-1, keepdims=True) + EPS_NORM)
    unit = mid * inv
    prod = dn * unit
    share = jnp.sum(prod, axis=0, keepdims=True)
    scaled = dn * gain_ref[...]
    back = inv * (scaled - unit * jnp.mean(prod * gain_ref[...], axis=-1, keepdims=True))
    dmix_ref[...] = (dy_ref[...].astype(F32) + back).astype(BF16)

    @pl.when(step == 0)
    def _():
        dgain_ref[...] = share
        acc[...] = jnp.zeros_like(acc)

    @pl.when(step > 0)
    def _():
        dgain_ref[...] += share

    dz = jnp.zeros((z_ref.shape[0], heads * HD), F32)
    for p in range(pieces):
        lanes = slice(p * depth, (p + 1) * depth)
        right = jnp.concatenate([parts[h * pieces + p][...] for h in range(heads)], axis=0)
        dz += nt(dmix_ref[:, lanes], right)
    acc[...] += tn(z_ref[...], dmix_ref[...])
    dz_ref[...] = dz.astype(BF16)

    @pl.when(step == steps - 1)
    def _():
        for h in range(heads):
            for p in range(pieces):
                grads[h * pieces + p][...] = acc[h * HD : (h + 1) * HD, p * depth : (p + 1) * depth].astype(BF16)


def mix_back(gain, own, other, mid, dy, z, parts):
    seq, dim = mid.shape
    heads, pieces = len(parts), len(parts[0])
    wide = z.shape[1]
    tile = min(256, seq)
    row = pl.BlockSpec((tile, dim), lambda i: (i, 0))
    one = pl.BlockSpec((1, dim), lambda i: (0, 0))
    zs = pl.BlockSpec((tile, wide), lambda i: (i, 0))
    res = pl.pallas_call(
        functools.partial(mix_back_kernel, heads, pieces),
        out_shape=[
            jax.ShapeDtypeStruct((seq, dim), BF16),
            jax.ShapeDtypeStruct((seq, wide), BF16),
            jax.ShapeDtypeStruct((1, dim), F32),
        ]
        + [jax.ShapeDtypeStruct((HD, dim // pieces), BF16)] * (heads * pieces),
        grid=(seq // tile,),
        in_specs=[one, row, row, row, row, zs] + outer_specs(parts),
        out_specs=[row, zs, one] + outer_specs(parts),
        scratch_shapes=[pltpu.VMEM((wide, dim), F32)],
        compiler_params=params(),
        cost_estimate=cost(4 * seq * dim * wide, 1e6),
        name="mix_back",
    )(gain, own, other, mid, dy, z, *[w for head in parts for w in head])
    return res[0], res[1], res[2], [res[3 + h * pieces : 3 + (h + 1) * pieces] for h in range(heads)]


def select_kernel(counts, apart, table_ref, *refs):
    j = pl.program_id(0)
    first = 0
    for g, n in enumerate(counts):
        width = refs[first].shape[2]
        value = refs[first][...]
        for i in range(1, n):
            value = jnp.where(table_ref[2 * g, j] == i, refs[first + i][...], value)
        if apart:
            refs[sum(counts) + g][...] = value
        else:
            refs[-1][:, :, g * width : (g + 1) * width] = value
        first += n


def select_blocks(groups, table, count, apart=False):
    specs, flat = [], []
    for g, sources in enumerate(groups):
        for i, value in enumerate(sources):

            def where(j, t, g=g, i=i):
                return (jnp.where(t[2 * g, j] == i, t[2 * g + 1, j], 0), 0, 0)

            specs.append(pl.BlockSpec((1,) + value.shape[1:], where))
            flat.append(value)
    piece, width = flat[0].shape[1:]
    total = width if apart else width * len(groups)
    outs = len(groups) if apart else 1
    res = pl.pallas_call(
        functools.partial(select_kernel, [len(g) for g in groups], apart),
        out_shape=[jax.ShapeDtypeStruct((count, piece, total), flat[0].dtype)] * outs,
        grid_spec=pltpu.PrefetchScalarGridSpec(
            num_scalar_prefetch=1,
            grid=(count,),
            in_specs=specs,
            out_specs=[pl.BlockSpec((1, piece, total), lambda j, t: (j, 0, 0))] * outs,
        ),
        compiler_params=params(),
        cost_estimate=cost(1e6, 1e6),
        name="select_blocks",
    )(table, *flat)
    return res if apart else res[0]


def ffn_kernel(pieces, chunks, bits, more, b_ref, dy_ref, *refs):
    weights = refs[: pieces * chunks]
    refs = refs[pieces * chunks :]
    sums_in, refs = (refs[:2], refs[2:]) if more else (None, refs)
    out_ref, db_ref = refs[:2]
    stacked = refs[2 : 2 + 2 * chunks]
    b_s, dy_s, hid_s, dg_s, du_s = refs[2 + 2 * chunks :]
    depth = weights[0].shape[1]
    units = weights[0].shape[0] // 3
    tile = b_ref.shape[0]
    step, steps = pl.program_id(0), pl.num_programs(0)

    def weight(p, i):
        return jnp.concatenate(
            [weights[c * pieces + p][i * units : (i + 1) * units] for c in range(chunks)], axis=0
        )

    rows = pl.ds(pl.multiple_of(step * tile, tile), tile)
    b_s[rows, :] = b_ref[...]
    dy_s[rows, :] = dy_ref[...]
    gate = jnp.zeros((tile, units * chunks), F32)
    up = jnp.zeros((tile, units * chunks), F32)
    dh = jnp.zeros((tile, units * chunks), F32)
    for p in range(pieces):
        lanes = slice(p * depth, (p + 1) * depth)
        block, dblock = b_ref[:, lanes], dy_ref[:, lanes]
        gate += nt(block, weight(p, 0))
        up += nt(block, weight(p, 1))
        dh += nt(dblock, weight(p, 2))
    sg = sigmoid(gate)
    act = gate * sg
    hid = (act * up).astype(BF16)
    du = (dh * act).astype(BF16)
    dg = (dh * up * (sg + act * (1.0 - sg))).astype(BF16)
    hid_s[rows, :] = hid
    dg_s[rows, :] = dg
    du_s[rows, :] = du
    for p in range(pieces):
        lanes = slice(p * depth, (p + 1) * depth)
        o = nn(hid, weight(p, 2))
        d = nn(dg, weight(p, 0)) + nn(du, weight(p, 1))
        if more:
            o += sums_in[0][:, lanes].astype(F32)
            d += sums_in[1][:, lanes].astype(F32)
        out_ref[:, lanes] = o.astype(out_ref.dtype)
        db_ref[:, lanes] = d.astype(db_ref.dtype)

    @pl.when(step == steps - 1)
    def _():
        for i, (left, right) in enumerate([(dg_s, b_s), (du_s, b_s), (hid_s, dy_s)]):
            g = tn(left[...], right[...]).astype(BF16)
            for c in range(chunks):
                for stack, group in zip(stacked[2 * c : 2 * c + 2], sides(pieces, bits[c])):
                    for n, p in enumerate(group):
                        stack[n, i * units : (i + 1) * units] = g[
                            c * units : (c + 1) * units, p * depth : (p + 1) * depth
                        ]


def ffn(normed, dy, parts, bits, sums=None, last=True):
    seq, dim = normed.shape
    chunks, pieces = len(parts), len(parts[0])
    flat = [w for chunk in parts for w in chunk]
    units = flat[0].shape[0] // 3
    tile = min(256, seq)
    row = pl.BlockSpec((tile, dim), lambda i: (i, 0))
    more = () if sums is None else tuple(sums)
    grads = stacks(pieces, flat[0].shape) * chunks
    res = pl.pallas_call(
        functools.partial(ffn_kernel, pieces, chunks, bits, bool(more)),
        out_shape=[jax.ShapeDtypeStruct((seq, dim), BF16 if last else F32)] * 2 + grads,
        grid=(seq // tile,),
        in_specs=[row, row] + [pl.BlockSpec(w.shape, lambda i: (0, 0)) for w in flat] + [row] * len(more),
        out_specs=[row, row] + [pl.BlockSpec(g.shape, lambda i: (0, 0, 0)) for g in grads],
        scratch_shapes=[pltpu.VMEM((seq, dim), BF16)] * 2 + [pltpu.VMEM((seq, units * chunks), BF16)] * 3,
        compiler_params=params(),
        cost_estimate=cost(18 * seq * dim * units * chunks, 1e6),
        name="ffn",
    )(normed, dy, *flat, *more)
    return res[0], res[1], [res[2 + 2 * c : 4 + 2 * c] for c in range(chunks)]


def sync(*trees):
    leaves, tree = jax.tree.flatten(trees)
    return jax.tree.unflatten(tree, lax.optimization_barrier(leaves))


def bits_of(n):
    return [1 << i for i in range(n.bit_length() - 1)]


class Place:
    def __init__(self):
        self.n_f = lax.axis_size("fsdp")
        self.n_t = lax.axis_size("tp")
        self.chips = self.n_f // 2
        f = lax.axis_index("fsdp")
        self.f = f
        self.core = f % 2
        self.k = f // 2
        self.t = lax.axis_index("tp")

    def swap(self, value):
        return lax.ppermute(value, "fsdp", [(i, i ^ 1) for i in range(self.n_f)])

    def move(self, value, bit):
        return lax.ppermute(value, "fsdp", [(i, i ^ (2 * bit)) for i in range(self.n_f)])

    def turn(self, value, r):
        return lax.ppermute(value, "tp", [(i, (i + r) % self.n_t) for i in range(self.n_t)])

    def in_order(self, mine, other, axis):
        first = jnp.where(self.core == 0, mine, other)
        second = jnp.where(self.core == 0, other, mine)
        return jnp.concatenate([first, second], axis=axis)

    def halves(self, value, axis):
        size = value.shape[axis] // 2
        return (
            lax.dynamic_slice_in_dim(value, self.core * size, size, axis),
            lax.dynamic_slice_in_dim(value, (1 - self.core) * size, size, axis),
        )

    def relative(self, value):
        width = value.shape[-1] // self.chips
        blocks = [
            lax.dynamic_slice_in_dim(value, (self.k ^ p) * width, width, value.ndim - 1) for p in range(self.chips)
        ]
        return jnp.concatenate(blocks, axis=-1)

    def spread_out(self, value):
        if value.shape[0] < self.n_t:
            value = jnp.pad(value, ((0, self.n_t - value.shape[0]),) + ((0, 0),) * (value.ndim - 1))
        return lax.all_to_all(value, "tp", split_axis=0, concat_axis=0, tiled=True)

    def all_sum(self, value):
        return self.chip_sum(self.line_sum(value))

    def chip_sum(self, value):
        for bit in [1] + [2 * b for b in bits_of(self.chips)]:
            value = value + lax.ppermute(value, "fsdp", [(i, i ^ bit) for i in range(self.n_f)])
        return value

    def line_sum(self, value):
        total = value
        for r in range(1, self.n_t):
            total = total + self.turn(value, r)
        return total

def rms_terms(value):
    return lax.rsqrt(jnp.mean(value * value, axis=-1, keepdims=True) + EPS_NORM)


def rms_back(value, gain, d_normed):
    inv = rms_terms(value)
    unit = value * inv
    dn = d_normed * gain
    return inv * (dn - unit * jnp.mean(dn * unit, axis=-1, keepdims=True))


class Gather:
    def __init__(self, at, shard):
        self.at = at
        self.parts = {(0, 0): shard}

    def turn(self, r, by=None):
        by = by or r
        self.parts[r, 0] = self.at.turn(self.parts[r - by, 0], by)

    def move(self, r, to, via):
        self.parts[r, to] = self.at.move(self.parts[r, to ^ via], via)

    def full(self, r):
        return [self.parts[r, p] for p in range(self.at.chips)]

    def rest(self):
        for r in range(1, self.at.n_t):
            self.turn(r)
        for r in range(self.at.n_t):
            for p in range(1, self.at.chips):
                self.move(r, p, p & -p)
        return [self.full(r) for r in range(self.at.n_t)]


def first_bit(at, r, late=False):
    return at.chips // 2 if r == 3 or r == (2 if late else 0) else 1


class Scatter:
    def __init__(self, at, late=False):
        self.at = at
        self.bit = lambda r: first_bit(at, r, late)
        self.near, self.far, self.two, self.one, self.end = {}, {}, {}, {}, {}

    def put(self, r, stacked):
        self.near[r], self.far[r] = stacked

    def cross(self, *turns):
        for r in turns:
            self.far[r] = self.at.move(self.far[r], self.bit(r))

    def add(self, *turns):
        sums = add_stacks([(self.near.pop(r), self.far.pop(r)) for r in turns])
        return dict(zip(turns, sums))

    def pass_on(self, sums):
        for r, (keep, give) in sums.items():
            self.two[r] = keep, self.at.move(give, 3 - self.bit(r))

    def fold(self, *turns):
        self.pass_on(self.add(*turns))

    def close(self, *turns):
        for r in turns:
            keep, came = self.two.pop(r)
            self.one[r] = (keep.astype(F32) + came.astype(F32)).astype(BF16)

    def home(self, r):
        self.end[r] = self.at.turn(self.one.pop(r), self.at.n_t - r)

    def merge(self, r):
        self.end[r] = self.at.turn(self.one.pop(r), self.at.n_t - 1)

    def join(self, r):
        self.one[r - 1] = (self.one[r - 1].astype(F32) + self.end.pop(r).astype(F32)).astype(BF16)

    def total(self):
        return sum(v.astype(F32) for v in list(self.one.values()) + list(self.end.values()))

    def state(self):
        return self.near, self.far, self.two, self.one, self.end

    def take(self, state):
        self.near, self.far, self.two, self.one, self.end = state

    def rest(self):
        for r in range(self.at.n_t):
            have = {}
            for stack, group in zip((self.near.pop(r), self.far.pop(r)), sides(self.at.chips, self.bit(r))):
                have.update({p: stack[i] for i, p in enumerate(group)})
            for bit in bits_of(self.at.chips):
                for p in [p for p in have if p & bit]:
                    came = self.at.move(have.pop(p), bit)
                    have[p ^ bit] = (have[p ^ bit].astype(F32) + came.astype(F32)).astype(BF16)
            self.one[r] = have[0]
            if r:
                self.home(r)


class Routing:
    def __init__(self, at, value, order, source):
        self.at, self.order = at, order
        self.per_chip = value.shape[0]
        self.have, self.where = [value], [0]
        reach = [0]
        for bit in order[:-1]:
            reach += [w | bit for w in reach]
        tables = []
        for chip in (at.k ^ order[-1], at.k):
            ask = lax.dynamic_slice_in_dim(source, chip * self.per_chip, self.per_chip, 0)
            distance = (ask // self.per_chip) ^ at.k
            src = sum(jnp.where(distance == w, i, 0) for i, w in enumerate(reach))
            near = (distance & order[-1]) == 0
            slot = ask % self.per_chip
            if chip is not at.k:
                tables.append((src, slot))
            else:
                tables.append(
                    (
                        jnp.where(near, src, len(reach)),
                        jnp.where(near, slot, jnp.arange(self.per_chip, dtype=jnp.int32)),
                    )
                )
        self.ask, self.keep = (jnp.stack(t) for t in tables)

    def step(self):
        bit = self.order[len(self.where).bit_length() - 1]
        self.have = self.have + [self.at.move(v, bit) for v in self.have]
        self.where = self.where + [w | bit for w in self.where]

    def last(self, give):
        self.have = self.have + [self.at.move(give, self.order[-1])]


def local(
    tokens, lengths, perm, cotangent, norm1_gain, input_weight, conv_w, decay_log, decay_bias, out_gain, w_out,
    norm2_gain, gate_up_weight, down_weight
):
    at = Place()
    slots, piece, dim = tokens.shape
    n_f, n_t, chips = at.n_f, at.n_t, at.chips
    heads_all = conv_w.shape[0]
    heads = heads_all // 2
    local_heads = input_weight.shape[1]
    cols = input_weight.shape[2]
    by_turn = local_heads == 2
    laps = list(range(n_t))
    bits = bits_of(chips)
    fast = by_turn and chips == 4 and n_t == 4
    per_chip = 2 * slots
    seq = n_t * piece
    steps = seq // SPAN // PER_STEP // 2

    pad = SMALL - (cols - 6 * HD)
    if by_turn:
        packed = jnp.transpose(input_weight, (1, 2, 0))
        zeros = jnp.zeros((local_heads, pad, packed.shape[2]), BF16)
        packed = jnp.concatenate([w_out.reshape(local_heads, HD, -1), packed, zeros], axis=1)
        mine, give = at.halves(packed, 0)
        m_own = at.in_order(mine[0], at.swap(give[0]), 1)
        head_ids = ((at.t - jnp.arange(n_t, dtype=jnp.int32)) % n_t) * 2 + at.core
    else:
        m_own = None
        head_ids = at.core * heads + jnp.arange(heads, dtype=jnp.int32)
    mine, give = at.halves(tokens, 2)
    both = at.in_order(mine, at.swap(give), 0)
    both, m_own, gate_up_weight, down_weight, cotangent = sync(both, m_own, gate_up_weight, down_weight, cotangent)
    packed = jnp.concatenate([jnp.transpose(gate_up_weight, (1, 2, 0)), down_weight[None]], axis=0)
    mine, give = at.halves(packed, 1)
    f_own = at.in_order(mine, at.swap(give), 2)
    f_own = f_own.reshape(-1, f_own.shape[2])
    mine, give = at.halves(cotangent, 2)
    cot_both = at.in_order(mine, at.swap(give), 0)

    own = head_ids[:, None] == jnp.arange(heads_all, dtype=jnp.int32)[None, :]
    taps = jnp.pad(jnp.transpose(conv_w, (0, 2, 1)), ((0, 0), (0, 8 - TAPS), (0, 0)))
    conv_t = jnp.sum(jnp.where(own[:, :, None, None], taps[None], 0.0), axis=1)
    scal = jnp.stack(
        [
            jnp.sum(jnp.where(own, jnp.exp(decay_log)[None], 0.0), axis=1),
            jnp.sum(jnp.where(own, decay_bias[None], 0.0), axis=1),
        ],
        axis=1,
    )
    gain1 = at.relative(norm1_gain)
    gain2 = at.relative(norm2_gain)
    gain_o = out_gain[None]
    start_state = jnp.zeros((heads, HD, HD), F32)

    seq_id = jnp.minimum(at.k * per_chip + at.t, lengths.shape[0] - 1)
    length = jnp.where(at.t < per_chip, lax.dynamic_index_in_dim(lengths, seq_id, 0, keepdims=False), 0)
    live = (jnp.arange(seq, dtype=jnp.int32) < length).astype(BF16)[:, None]
    slot_ids = jnp.arange(perm.shape[0], dtype=jnp.int32)
    source = jnp.sum(jnp.where(perm[None, :] == slot_ids[:, None], slot_ids[None, :], 0), axis=1)
    quarter = dim // 4
    routes = [
        Routing(at, cot_both[:, :, :quarter], bits, source),
        Routing(at, cot_both[:, :, quarter:], bits[::-1], source),
    ]

    def route_state():
        return [r.have for r in routes]

    def set_routes(state):
        for r, v in zip(routes, state):
            r.have = v

    def routed():
        groups = [r.have for r in routes]
        return select_blocks(groups, jnp.concatenate([r.keep for r in routes], axis=0), per_chip)

    def sequence(half):
        half = half.reshape(seq, -1)
        return at.relative(at.in_order(half, at.swap(half), 1))

    def norm_first(x):
        return (x * rms_terms(x) * gain1).astype(BF16)

    f = Gather(at, f_own)
    proj = {}

    def asked():
        return select_blocks([r.have for r in routes], jnp.concatenate([r.ask for r in routes], axis=0), per_chip, True)

    if fast:
        m = Gather(at, m_own)

        def run(r):
            proj[r] = project(r, normed_one, m.full(r), conv_t, scal)

        def without(parts, *keys):
            return {k: v for k, v in parts.items() if k not in keys}

        came = at.spread_out(both)
        for p in range(1, chips):
            m.move(0, p, p)
        m.parts, f.parts, came, cot_both, conv_t, scal, gain1, gain2, live, extra = sync(
            m.parts, f.parts, came, cot_both, conv_t, scal, gain1, gain2, live, [(r.ask, r.keep) for r in routes]
        )
        for r, (ask, keep), part in zip(routes, extra, (cot_both[:, :, :quarter], cot_both[:, :, quarter:])):
            r.ask, r.keep, r.have = ask, keep, [part]
        m.turn(1)
        for r in routes:
            r.step()
        x = sequence(came)
        normed_one = norm_first(x.astype(F32))
        run(0)
        state = route_state()
        m.parts, f.parts, state, proj[0], normed_one, x = sync(m.parts, f.parts, state, proj[0], normed_one, x)
        set_routes(state)
        m.turn(3)
        m.move(1, 1, 1)
        m.move(1, 2, 2)
        give = asked()
        m.parts, f.parts, give = sync(m.parts, f.parts, give)
        m.turn(2, 1)
        m.move(3, 1, 1)
        m.move(3, 2, 2)
        m.parts, f.parts, give = sync(m.parts, f.parts, give)
        m.move(1, 3, 1)
        m.move(3, 3, 2)
        f.turn(1)
        m.parts, f.parts, give = sync(m.parts, f.parts, give)
        m.move(2, 1, 1)
        m.move(2, 2, 2)
        for r, part in zip(routes, give):
            r.last(part)
        f.turn(3)
        run(1)
        run(3)
        state = route_state()
        m.parts, proj, normed_one, f.parts, state = sync(m.parts, proj, normed_one, f.parts, state)
        set_routes(state)
        m.move(2, 3, 1)
        f.turn(2, 1)
        f.move(0, 1, 1)
        f.move(0, 2, 2)
        cot_home = routed()
        early = without(f.parts, (0, 1), (0, 2))
        m.parts, early, cot_home, normed_one = sync(m.parts, early, cot_home, normed_one)
        f.parts.update(early)
        cot_came = at.spread_out(cot_home)
        f.move(1, 1, 1)
        f.move(1, 2, 2)
        run(2)
        early = without(f.parts, (1, 1), (1, 2))
        proj, early = sync(proj, early)
        f.parts.update(early)
        m_parts = [m.full(r) for r in laps]
    else:
        x = sequence(at.spread_out(both))
        normed_one = norm_first(x.astype(F32))
        if by_turn:
            m_parts = Gather(at, m_own).rest()
        else:
            full = lax.all_gather(lax.all_gather(input_weight, "tp", axis=1, tiled=True), "fsdp", axis=0, tiled=True)
            full = at.relative(jnp.transpose(full, (1, 2, 0)))
            full_out = lax.all_gather(lax.all_gather(w_out, "tp", axis=0, tiled=True), "fsdp", axis=1, tiled=True)
            full_out = at.relative(full_out).reshape(heads_all, HD, dim)
            zeros = jnp.zeros((heads_all, pad, dim), BF16)
            full = at.halves(jnp.concatenate([full_out, full, zeros], axis=1), 0)[0]
            m_parts = [jnp.split(full[h], chips, axis=1) for h in range(heads)]
        for h in range(heads):
            proj[h] = project(h, normed_one, m_parts[h], conv_t, scal)
        for r in routes:
            for _ in bits[1:]:
                r.step()
        for r, part in zip(routes, asked()):
            r.last(part)
        cot_came = at.spread_out(routed())
        f_parts = f.rest()

    raw, gate, q, k, v, rows = (list(group) for group in zip(*[proj[h] for h in range(heads)]))
    if fast:
        f.move(0, 3, 2)
    first = recur(gain_o, start_state, q, k, v, gate, rows, 0, steps)
    if fast:
        first, f.parts, cot_came = sync(first, f.parts, cot_came)
        f.move(1, 3, 1)
        for r in (3, 2):
            f.move(r, 1, 1)
            f.move(r, 2, 2)
    second = recur(gain_o, first[1], q, k, v, gate, rows, steps, steps, first[0])
    if fast:
        early = without(f.parts, (2, 1), (2, 2))
        second, early = sync(second, early)
        f.parts.update(early)
    z = second[0]
    mix = mix_out(z, m_parts)
    mid = x.astype(F32) + (mix.astype(F32) + at.swap(mix).astype(F32))
    normed_two = (mid * rms_terms(mid) * gain2).astype(BF16)
    dy = live * sequence(cot_came)

    f_rs = Scatter(at)
    half = n_t // 2
    group_a, group_b = laps[:half], laps[half:][::-1]
    bits_a, bits_b = [first_bit(at, r) for r in group_a], [first_bit(at, r) for r in group_b]
    if fast:
        normed_two, dy, f.parts = sync(normed_two, dy, f.parts)
        f.move(2, 3, 1)
        f.move(3, 3, 2)
        f_parts = {r: f.full(r) for r in group_a}
    net, db, grads = ffn(normed_two, dy, [f_parts[r] for r in group_a], bits_a, last=False)
    if fast:
        net, db, grads, f.parts = sync(net, db, grads, f.parts)
        f_parts = {r: f.full(r) for r in group_b}
    for r, g in zip(group_a, grads):
        f_rs.put(r, g)
    if fast:
        f_rs.cross(0, 1)
    net, db, grads = ffn(normed_two, dy, [f_parts[r] for r in group_b], bits_b, (net, db))
    if fast:
        net, db, grads, state = sync(net, db, grads, f_rs.state())
        f_rs.take(state)
    for r, g in zip(group_b, grads):
        f_rs.put(r, g)

    db_other = at.swap(db)
    if fast:
        f_rs.fold(0, 1)
        f_rs.cross(3, 2)
    d_mix, dz, g_gain2, g_out = mix_back(gain2[None], db, db_other, mid, dy, z, m_parts)
    if fast:
        dz, d_mix, g_out, f_rs.two, net = sync(dz, d_mix, g_out, f_rs.two, net)
    net_other = at.swap(net)
    back = recur_back(gain_o, start_state, dz, q, k, v, gate, rows, *second[2:], steps, steps)
    if fast:
        back, state, net_other, dz = sync(back, f_rs.state(), net_other, dz)
        f_rs.take(state)
        f_rs.close(0, 1)
        f_rs.fold(3, 2)

    def give_back(value):
        mine = at.halves(at.relative(value.astype(BF16)), 1)[0]
        return mine.reshape(n_t, piece, dim // 2)

    def settle(came):
        mine, give = at.halves(came[:per_chip], 0)
        return at.in_order(mine, at.swap(give), 2)

    g_gain_o = back[2]
    out_home = give_back(live.astype(F32) * (mid + (net.astype(F32) + net_other.astype(F32))))
    out_came = lax.all_to_all(out_home, "tp", split_axis=0, concat_axis=0, tiled=True)
    back = recur_back(
        gain_o, back[3], dz, q, k, v, gate, rows, *first[2:], 0, steps, tuple(back[0]) + tuple(back[1])
    )
    g_gain_o = g_gain_o + back[2]
    ds, drows = back[:2]
    if fast:
        ds, drows, out_came, state = sync(ds, drows, out_came, f_rs.state())
        f_rs.take(state)
        f_rs.close(3, 2)
        f_rs.merge(2)
        f_rs.home(3)

    dps, g_conv, g_small = {}, {}, {}
    m_rs = Scatter(at, late=True)

    def run_back(h):
        dps[h], g_conv[h], g_small[h], grads = project_back(
            h, normed_one, conv_t, scal, raw[h], rows[h], ds[h], drows[h], g_out[h], m_rs.bit(h)
        )
        m_rs.put(h, grads)

    def moved(group, key):
        return {r: v for r, v in group.items() if r == key}

    if fast:
        run_back(2)
        dps, m_rs.near, m_rs.far, ds = sync(dps, m_rs.near, m_rs.far, ds)
        m_rs.cross(2)
        run_back(1)
        dps, m_rs.near, far, ds, f_state = sync(dps, m_rs.near, moved(m_rs.far, 1), ds, f_rs.state())
        m_rs.far.update(far)
        f_rs.take(f_state)
        f_rs.join(2)
        f_rs.home(1)
        m_rs.cross(1)
        run_back(3)
        dps, m_rs.near, m_rs.far, ds = sync(dps, m_rs.near, m_rs.far, ds)
        m_rs.fold(1, 2)
        m_rs.cross(3)
        run_back(0)
        far = {0: m_rs.far[0]}
        dps, m_rs.near, far, m_rs.two, f_rs.end = sync(dps, m_rs.near, far, m_rs.two, f_rs.end)
        m_rs.far.update(far)
        m_rs.close(1, 2)
        dps, m_rs.one = sync(dps, m_rs.one)
        m_rs.merge(2)
        m_rs.cross(0)
    else:
        for h in range(heads):
            run_back(h)
    output = settle(out_came)
    da, g_gain1 = input_back([dps[h] for h in range(heads)], m_parts, x)
    if fast:
        far = {3: m_rs.far[3]}
        da, g_gain1, far, m_rs.end = sync(da, g_gain1, far, m_rs.end)
        m_rs.far.update(far)
        m_rs.join(2)
        m_rs.home(1)
    da_other = at.swap(da)
    d_x_norm = rms_back(x.astype(F32), gain1, da.astype(F32) + da_other.astype(F32))
    dx_home = give_back(d_mix.astype(F32) + d_x_norm)

    small = [jnp.sum(g_small[h], axis=0) for h in range(heads)]
    conv_all = sum(jnp.where(own[h][:, None, None], g_conv[h][None, :TAPS], 0.0) for h in range(heads)).reshape(-1, HD)
    decay_all = sum(jnp.where(own[h][:, None], small[h][None], 0.0) for h in range(heads))
    gains = jnp.concatenate([at.relative(g_gain1[0]), 0.5 * at.relative(g_gain2[0])]).reshape(-1, HD)
    sums = jnp.concatenate([conv_all, decay_all, gains, g_gain_o], axis=0)
    if fast:
        dx_home, sums, m_rs.near, m_rs.end = sync(dx_home, sums, m_rs.near, m_rs.end)
        m_rs.fold(3)
        m_rs.close(3)
        m_rs.home(3)
        m_rs.fold(0)
        sums = at.chip_sum(at.line_sum(sums))
    else:
        sums = at.all_sum(sums)
    dx_came = lax.all_to_all(dx_home, "tp", split_axis=0, concat_axis=0, tiled=True)
    if fast:
        dx_came, m_rs.two, m_rs.end = sync(dx_came, m_rs.two, m_rs.end)
        m_rs.close(0)
    input_grad = settle(dx_came)
    n_conv = conv_all.shape[0]
    g_conv_all = jnp.transpose(sums[:n_conv].reshape(heads_all, TAPS, -1), (0, 2, 1))
    decay_sum = sums[n_conv : n_conv + heads_all]
    gain_sum = sums[n_conv + heads_all : -1].reshape(2, dim)

    def to_core(value, joined):
        mine, give = at.halves(value.astype(BF16), value.ndim - 1)
        return at.in_order(mine, at.swap(give), joined).astype(F32)

    if not fast:
        f_rs.rest()
    f_total = f_rs.total()
    g_ffn = to_core(f_total.reshape(3, -1, f_total.shape[1]), 1)
    grad_gate_up = jnp.transpose(g_ffn[:2], (2, 0, 1))
    grad_down = g_ffn[2]
    if by_turn:
        if not fast:
            m_rs.rest()
        joined = to_core(m_rs.total()[None], 0)
    else:
        joined = []
        for h in range(heads):
            have = {}
            for stack, group in zip((m_rs.near[h], m_rs.far[h]), sides(chips, m_rs.bit(h))):
                have.update({p: stack[i] for i, p in enumerate(group)})
            joined.append(jnp.concatenate([have[p] for p in range(chips)], axis=1))
        joined = jnp.stack(joined)
        spread = jnp.zeros((heads_all,) + joined.shape[1:], BF16)
        spread = lax.dynamic_update_slice_in_dim(spread, at.relative(joined), at.core * heads, 0)
        spread = lax.psum_scatter(spread, "tp", scatter_dimension=0, tiled=True)
        joined = lax.psum_scatter(spread, "fsdp", scatter_dimension=2, tiled=True).astype(F32)
    grad_in = jnp.transpose(joined[:, HD : HD + cols], (2, 0, 1))
    grad_out = joined[:, :HD].reshape(local_heads * HD, -1)
    return (
        output, input_grad, gain_sum[0], grad_in, g_conv_all, decay_sum[:, 0], decay_sum[:, 1], sums[-1], grad_out,
        gain_sum[1], grad_gate_up, grad_down
    )


def solution(mesh):
    tokens = P("fsdp", "tp", None)
    rows = P("tp", "fsdp")
    split = P("fsdp", None, "tp")
    return jax.shard_map(
        local,
        mesh=mesh,
        in_specs=(tokens, P(), P(), tokens, P(), tokens, P(), P(), P(), P(), rows, P(), split, rows),
        out_specs=(tokens, tokens, P(), tokens, P(), P(), P(), P(), rows, P(), split, rows),
        check_vma=False,
    )
```

```python
import functools

import jax
import jax.numpy as jnp
from jax import lax
from jax.experimental import pallas as pl
from jax.experimental.pallas import tpu as pltpu
from jax.sharding import PartitionSpec as P

HD = 128
NH = 2
SPAN = 64
SUB = SPAN * NH
TAPS = 4
SMALL = 16
UNITS = 6 * HD + SMALL
EPS_NORM = 1e-05
EPS_UNIT = 1e-06
F32 = jnp.float32
BF16 = jnp.bfloat16
FAR = -1e30
VMEM_BYTES = 56 * 1024 * 1024
EXACT = lax.Precision.HIGHEST


def params(**kw):
    return pltpu.CompilerParams(vmem_limit_bytes=VMEM_BYTES, **kw)


def cost(flops, nbytes, trans=0):
    return pl.CostEstimate(flops=int(flops), bytes_accessed=int(nbytes), transcendentals=int(trans))


def nn(a, b):
    return lax.dot_general(a, b, (((1,), (0,)), ((), ())), preferred_element_type=F32)


def nt(a, b):
    return lax.dot_general(a, b, (((1,), (1,)), ((), ())), preferred_element_type=F32)


def tn(a, b):
    return lax.dot_general(a, b, (((0,), (0,)), ((), ())), preferred_element_type=F32)


def exact_nn(a, b):
    return lax.dot_general(a, b, (((1,), (0,)), ((), ())), precision=EXACT, preferred_element_type=F32)


def sigmoid(v):
    return 1.0 / (1.0 + jnp.exp(-v))


def sides(pieces, bit):
    return [p for p in range(pieces) if not p & bit], [p for p in range(pieces) if p & bit]


def stacks(pieces, shape):
    return [jax.ShapeDtypeStruct((pieces // 2,) + shape, BF16)] * 2


def add_kernel(count, *refs):
    ins, outs = refs[: 2 * count], refs[2 * count :]
    for i in range(count):
        for j in range(2):
            outs[2 * i + j][...] = (ins[2 * i][j].astype(F32) + ins[2 * i + 1][j].astype(F32)).astype(BF16)


def add_stacks(pairs):
    flat = [v for pair in pairs for v in pair]
    steps = 3
    blocks = [pl.BlockSpec((2, v.shape[1] // steps, v.shape[2]), lambda i: (0, i, 0)) for v in flat]
    single = [pl.BlockSpec((v.shape[1] // steps, v.shape[2]), lambda i: (i, 0)) for v in flat]
    res = pl.pallas_call(
        functools.partial(add_kernel, len(pairs)),
        out_shape=[jax.ShapeDtypeStruct(v.shape[1:], BF16) for v in flat],
        grid=(steps,),
        in_specs=blocks,
        out_specs=single,
        compiler_params=params(),
        cost_estimate=cost(1e6, 1e6),
        name="add_stacks",
    )(*flat)
    return [res[2 * i : 2 * i + 2] for i in range(len(pairs))]


def lane_sum(value):
    return jnp.sum(value, axis=-1, keepdims=True)


def conv_shifts(ref, start, rows, lanes):
    window = ref[start : start + rows + 8, lanes]
    views = [pltpu.roll(window, TAPS - 1 - j, 0)[8 : 8 + rows] for j in range(TAPS - 1)]
    return views + [window[8 : 8 + rows]]


def conv_shifts_back(ref, start, rows, lanes):
    window = ref[start : start + rows + 8, lanes]
    views = [pltpu.roll(window, rows + 8 - (TAPS - 1 - j), 0)[:rows] for j in range(TAPS - 1)]
    return views + [window[:rows]]


def iota(shape, dim):
    return lax.broadcasted_iota(jnp.int32, shape, dim)


def project_kernel(pieces, h, scal_ref, a_ref, cw_ref, *refs):
    parts = refs[:pieces]
    raw_ref, gate_ref, q_ref, k_ref, v_ref, rows_ref, raw_s, mix_s, aux_s = refs[pieces:]
    tile = a_ref.shape[0]
    depth = parts[0].shape[1]
    head = 8

    @pl.when(pl.program_id(0) == 0)
    def _():
        raw_s[0:head, :] = jnp.zeros_like(raw_s[0:head, :])

    @pl.when(pl.program_id(0) > 0)
    def _():
        raw_s[0:head, :] = raw_s[tile : tile + head, :]

    acc = jnp.zeros((tile, UNITS), F32)
    for p in range(pieces):
        acc += nt(a_ref[:, p * depth : (p + 1) * depth], parts[p][HD:])
    raw_s[head : tile + head, :] = acc[:, : 5 * HD]
    raw_ref[...] = acc[:, : 5 * HD].astype(BF16)
    gate_ref[...] = acc[:, 5 * HD : 6 * HD].astype(BF16)

    small = acc[:, 6 * HD :]
    rate, bias = scal_ref[h, 0], scal_ref[h, 1]
    arg = small[:, 2:3] + bias
    soft = jnp.maximum(arg, 0.0) + jnp.log(1.0 + jnp.exp(-jnp.abs(arg)))
    beta = sigmoid(small[:, 0:2])
    lane = iota((tile, HD), 1)
    aux_s[pl.ds(0, tile, 2), :] = jnp.where(
        lane == 0, beta[:, 0:1], jnp.where(lane == 1, -rate * soft, jnp.where(lane == 2, arg, 0.0))
    )
    aux_s[pl.ds(1, tile, 2), :] = jnp.where(lane == 0, beta[:, 1:2], 0.0)
    upper = jnp.where(iota((SUB, SUB), 0) <= iota((SUB, SUB), 1), 1.0, 0.0)
    for b in range(tile // SPAN):
        rows = jnp.transpose(aux_s[b * SUB : (b + 1) * SUB, :])[:8]
        cum = exact_nn(rows, upper)
        rows_ref[b] = jnp.where(iota((8, SUB), 0) == 3, cum[1:2], rows)

    chunk = 64
    for g in range(5):
        taps = cw_ref[0, :, g * HD : (g + 1) * HD]
        for i in range(tile // chunk):
            start = i * chunk
            views = conv_shifts(raw_s, start, chunk, slice(g * HD, (g + 1) * HD))
            pre = views[0] * taps[0:1]
            for j in range(1, TAPS):
                pre += views[j] * taps[j : j + 1]
            act = pre * sigmoid(pre)
            if g < 3:
                act = act * lax.rsqrt(lane_sum(act * act) + EPS_UNIT)
            if g == 0:
                q_ref[start : start + chunk, :] = act.astype(BF16)
            else:
                mix_s[pl.ds(2 * start + (g + 1) % 2, chunk, 2), :] = act
        if g in (2, 4):
            (k_ref if g == 2 else v_ref)[...] = mix_s[...].astype(BF16)


def project(h, normed, parts, conv_t, scal):
    seq, dim = normed.shape
    pieces = len(parts)
    tile = min(256, seq)
    fix = lambda i: (0, 0)
    along = lambda i: (i, 0)
    outs = [((seq, 5 * HD), BF16, 1), ((seq, HD), BF16, 1), ((seq, HD), BF16, 1), ((NH * seq, HD), BF16, NH), ((NH * seq, HD), BF16, NH)]
    return pl.pallas_call(
        functools.partial(project_kernel, pieces, h),
        out_shape=[jax.ShapeDtypeStruct(s, d) for s, d, _ in outs] + [jax.ShapeDtypeStruct((seq // SPAN, 8, SUB), F32)],
        grid=(seq // tile,),
        in_specs=[
            pl.BlockSpec(memory_space=pltpu.SMEM),
            pl.BlockSpec((tile, dim), along),
            pl.BlockSpec((1,) + conv_t.shape[1:], lambda i: (h, 0, 0)),
        ]
        + [pl.BlockSpec(w.shape, fix) for w in parts],
        out_specs=[pl.BlockSpec((tile * n, s[1]), along) for s, _, n in outs]
        + [pl.BlockSpec((tile // SPAN, 8, SUB), lambda i: (i, 0, 0))],
        scratch_shapes=[
            pltpu.VMEM((tile + 8, 5 * HD), F32),
            pltpu.VMEM((NH * tile, HD), F32),
            pltpu.VMEM((NH * tile, HD), F32),
        ],
        compiler_params=params(),
        cost_estimate=cost(2 * seq * dim * UNITS, 8e6),
        name="project",
    )(scal, normed, conv_t, *parts)


BASE = 16


def unit_lower_inverses(lowers):
    n, groups = SUB, SUB // BASE
    lane = iota((BASE, n), 1)
    group = lane // BASE
    packed = []
    for low in lowers:
        p = jnp.where(group == 0, low[:BASE], 0.0)
        for b in range(1, groups):
            p = jnp.where(group == b, low[b * BASE : (b + 1) * BASE], p)
        packed.append(p)
    eye = jnp.where(lane % BASE == iota((BASE, n), 0), 1.0, 0.0)
    invs = [eye] * len(lowers)
    first = group * BASE
    for j in range(BASE - 1):
        coefs = [jnp.take_along_axis(p, first + j, axis=1) for p in packed]
        invs = [x - c * x[j : j + 1] for x, c in zip(invs, coefs)]
    fulls = [
        jnp.concatenate([jnp.where(group == b, x, 0.0).astype(BF16) for b in range(groups)], axis=0) for x in invs
    ]
    row, col = iota((n, n), 0), iota((n, n), 1)
    size = BASE
    while size < n:
        odd = range(1, n // size, 2)
        mask = jnp.logical_and(row // size == col // size + 1, row // (2 * size) == col // (2 * size))
        crosses = [jnp.where(mask, low, 0.0).astype(BF16) for low in lowers]
        picks = [jnp.concatenate([f[b * size : (b + 1) * size] for b in odd], axis=0) for f in fulls]
        halves = [nn(p, c).astype(BF16) for p, c in zip(picks, crosses)]
        belows = [(p.astype(F32) - nn(h, f)).astype(BF16) for p, h, f in zip(picks, halves, fulls)]
        fulls = [
            jnp.concatenate(
                [
                    below[(b // 2) * size : (b // 2 + 1) * size] if b % 2 else f[b * size : (b + 1) * size]
                    for b in range(n // size)
                ],
                axis=0,
            )
            for f, below in zip(fulls, belows)
        ]
        size *= 2
    return fulls


def turned(value, eye):
    return nt(eye, value)


def decay_terms(rows_ref, cums, items):
    out = []
    pick_row = iota((8, SUB), 0)
    for i, (b, h) in enumerate(items):
        rows = rows_ref[h][b]
        g = rows[3:4, :]
        g_last = g[:, SUB - 1 :]
        e = jnp.exp(g)
        wide = jnp.where(pick_row == 1, e, jnp.where(pick_row == 2, jnp.exp(g_last - g), rows))
        wide = jnp.where(pick_row == 4, rows[0:1, :] * e, wide)
        cols = jnp.transpose(jnp.concatenate([wide] * (SUB // 8), axis=0))
        cums[i] = cols
        c_col = cums[i, pl.ds(1, SPAN, 2), :][:, 3:4]
        out.append((cols[:, 0:1], cols[:, 1:2], cols[:, 2:3], cols[:, 3:4], cols[:, 4:5], g, c_col, g_last))
    return out


PER_STEP = 2


def recur_kernel(heads, more, gain_ref, start_ref, *refs):
    q_r, k_r, v_r, g_r, rows_r = (refs[i * heads : (i + 1) * heads] for i in range(5))
    refs = refs[: 5 * heads] + refs[5 * heads + more :]
    z_ref, end_ref = refs[5 * heads : 5 * heads + 2]
    o_r = refs[5 * heads + 2 : 6 * heads + 2]
    u_r = refs[6 * heads + 2 : 7 * heads + 2]
    s_ref, t_ref, cums = refs[7 * heads + 2 :]

    @pl.when(pl.program_id(0) == 0)
    def _():
        end_ref[...] = start_ref[...]

    row, col = iota((SUB, SUB), 0), iota((SUB, SUB), 1)
    strict = col < row
    vis = iota((SPAN, SUB), 1) // NH <= iota((SPAN, SUB), 0)
    items = [(b, h) for b in range(PER_STEP) for h in range(heads)]
    tok = [pl.ds(b * SPAN, SPAN) for b, _ in items]
    sub = [pl.ds(b * SUB, SUB) for b, _ in items]
    eye = jnp.where(row == col, 1.0, 0.0).astype(BF16)
    terms = decay_terms(rows_r, cums, items)
    ks = [k_r[h][sub[i]] for i, (b, h) in enumerate(items)]
    qs = [q_r[h][tok[i]] for i, (b, h) in enumerate(items)]
    prods = [nt(jnp.concatenate([k, q], axis=0), k) for k, q in zip(ks, qs)]
    lowers = [
        t[0] * jnp.exp(jnp.where(strict, t[3] - t[5], FAR)) * p[:SUB] for p, t in zip(prods, terms)
    ]
    inner = [(jnp.exp(jnp.where(vis, t[6] - t[5], FAR)) * p[SUB:]).astype(BF16) for p, t in zip(prods, terms)]
    inverses = unit_lower_inverses(lowers)
    for (b, h), inv in zip(items, inverses):
        t_ref[b, h] = inv
    solved, backs = [], []
    for i, (b, h) in enumerate(items):
        t = terms[i]
        k = ks[i].astype(F32)
        right = jnp.concatenate([t[0] * v_r[h][sub[i]].astype(F32), t[4] * k], axis=1)
        solved.append(nn(inverses[i], right.astype(BF16)))
        weighted = turned((t[2] * k).astype(BF16), eye).astype(BF16)
        backs.append(jnp.concatenate([weighted, inner[i]], axis=0))
    gain = gain_ref[...]
    for b in range(PER_STEP):
        mine = [i for i, it in enumerate(items) if it[0] == b]
        olds = [end_ref[items[i][1]] for i in mine]
        old_bs = [o.astype(BF16) for o in olds]
        reads = [
            nn(jnp.concatenate([solved[i][:, HD:].astype(BF16), qs[i]], axis=0), ob) for i, ob in zip(mine, old_bs)
        ]
        ubs = [(solved[i][:, :HD] - r[:SUB]).astype(BF16) for i, r in zip(mine, reads)]
        adds = [nn(backs[i], ub) for i, ub in zip(mine, ubs)]
        for i, old, ob, r, ub, add in zip(mine, olds, old_bs, reads, ubs, adds):
            h = items[i][1]
            c_col, g_last = terms[i][6:]
            end_ref[h] = jnp.exp(g_last) * old + add[:HD]
            s_ref[b, h] = ob
            u_r[h][sub[i], :] = ub
            o = jnp.exp(c_col) * r[SUB:] + add[HD:]
            o_r[h][tok[i], :] = o.astype(BF16)
            scaled = o * lax.rsqrt(jnp.mean(o * o, axis=-1, keepdims=True) + EPS_NORM) * gain
            gate = g_r[h][tok[i]].astype(F32)
            z_ref[tok[i], h * HD : (h + 1) * HD] = (scaled * gate * sigmoid(gate)).astype(BF16)


def recur_specs(heads, at):
    tok = pl.BlockSpec((PER_STEP * SPAN, HD), lambda i: (at(i), 0))
    sub = pl.BlockSpec((PER_STEP * SUB, HD), lambda i: (at(i), 0))
    rows = pl.BlockSpec((PER_STEP, 8, SUB), lambda i: (at(i), 0, 0))
    wide = pl.BlockSpec((PER_STEP * SPAN, heads * HD), lambda i: (at(i), 0))
    mat = pl.BlockSpec((PER_STEP, heads, HD, HD), lambda i: (at(i), 0, 0, 0))
    one = pl.BlockSpec((1, HD), lambda i: (0, 0))
    state = pl.BlockSpec((heads, HD, HD), lambda i: (0, 0, 0))
    return tok, sub, rows, wide, mat, one, state


def recur(gain, start, q, k, v, gate, rows, first, steps, z=None):
    heads = len(q)
    tok, sub, row, wide, mat, one, state = recur_specs(heads, lambda i: i + first)
    o_tok, o_sub, _, _, o_mat, _, _ = recur_specs(heads, lambda i: i)
    n = steps * PER_STEP
    more = [] if z is None else [z]

    def shape(s, d):
        return jax.ShapeDtypeStruct(s, d)

    res = pl.pallas_call(
        functools.partial(recur_kernel, heads, len(more)),
        out_shape=[shape((q[0].shape[0], heads * HD), BF16), shape((heads, HD, HD), F32)]
        + [shape((n * SPAN, HD), BF16)] * heads
        + [shape((n * SUB, HD), BF16)] * heads
        + [shape((n, heads, HD, HD), BF16)] * 2,
        grid=(steps,),
        in_specs=[one, state]
        + [tok] * heads
        + [sub] * (2 * heads)
        + [tok] * heads
        + [row] * heads
        + [pl.BlockSpec(memory_space=pl.ANY)] * len(more),
        out_specs=[wide, state] + [o_tok] * heads + [o_sub] * heads + [o_mat] * 2,
        scratch_shapes=[pltpu.VMEM((PER_STEP * heads, SUB, SUB), F32)],
        compiler_params=params(),
        input_output_aliases={2 + 5 * heads: 0} if more else {},
        cost_estimate=cost(heads * n * 20 * 4.2e6, 1e6),
        name="recur",
    )(gain, start, *q, *k, *v, *gate, *rows, *more)
    return res[0], res[1], res[2 : 2 + heads], res[2 + heads : 2 + 2 * heads], res[2 + 2 * heads], res[3 + 2 * heads]


def recur_back_kernel(heads, more, gain_ref, start_ref, dz_ref, *refs):
    q_r, k_r, v_r, g_r, rows_r, o_r, u_r = (refs[i * heads : (i + 1) * heads] for i in range(7))
    s_ref, t_ref = refs[7 * heads : 7 * heads + 2]
    refs = refs[: 7 * heads + 2] + refs[7 * heads + 2 + more :]
    d_r = refs[7 * heads + 2 : 8 * heads + 2]
    drows_r = refs[8 * heads + 2 : 9 * heads + 2]
    dgain_ref, end_ref, cums, mixed = refs[9 * heads + 2 :]

    @pl.when(pl.program_id(0) == 0)
    def _():
        end_ref[...] = start_ref[...]
        dgain_ref[...] = jnp.zeros_like(dgain_ref)

    row, col = iota((SUB, SUB), 0), iota((SUB, SUB), 1)
    strict = col < row
    later = jnp.where(row >= col, 1.0, 0.0)
    vis = iota((SPAN, SUB), 1) // NH <= iota((SPAN, SUB), 0)
    gain = gain_ref[...]
    items = [(b, h) for b in reversed(range(PER_STEP)) for h in range(heads)]
    every = range(len(items))
    tok = [pl.ds(b * SPAN, SPAN) for b, _ in items]
    sub = [pl.ds(b * SUB, SUB) for b, _ in items]
    terms = decay_terms(rows_r, cums, items)
    ks = [k_r[h][sub[i]] for i, (b, h) in enumerate(items)]
    qs = [q_r[h][tok[i]] for i, (b, h) in enumerate(items)]
    us = [u_r[h][sub[i]] for i, (b, h) in enumerate(items)]
    ss = [s_ref[b, h] for b, h in items]
    prods = [nt(jnp.concatenate([k, q], axis=0), k) for k, q in zip(ks, qs)]

    dos = []
    dgain = jnp.zeros((1, HD), F32)
    for i, (b, h) in enumerate(items):
        dz = dz_ref[tok[i], h * HD : (h + 1) * HD].astype(F32)
        o = o_r[h][tok[i]].astype(F32)
        gate = g_r[h][tok[i]].astype(F32)
        inv_rms = lax.rsqrt(jnp.mean(o * o, axis=-1, keepdims=True) + EPS_NORM)
        n = o * inv_rms
        sg = sigmoid(gate)
        dy = dz * gate * sg
        d_r[h][tok[i], 5 * HD :] = (dz * n * gain * sg * (1.0 + gate * (1.0 - sg))).astype(BF16)
        dgain += jnp.sum(dy * n, axis=0, keepdims=True)
        dn = dy * gain
        dos.append((inv_rms * (dn - n * jnp.mean(dn * n, axis=-1, keepdims=True))).astype(BF16))
    dgain_ref[...] += dgain

    eye = jnp.where(row == col, 1.0, 0.0).astype(BF16)
    reads = [jnp.exp(jnp.where(vis, t[6] - t[5], FAR)) for t in terms]
    ecs = [jnp.exp(t[6]) for t in terms]
    kfs = [k.astype(F32) for k in ks]
    qfs = [q.astype(F32) for q in qs]
    lefts = [
        jnp.concatenate([turned((p[SUB:] * r).astype(BF16), eye).astype(BF16), (t[2] * k).astype(BF16)], axis=1)
        for p, r, t, k in zip(prods, reads, terms, kfs)
    ]
    downs = [
        turned(jnp.concatenate([(ec * q).astype(BF16), (-t[4] * k).astype(BF16)], axis=0), eye).astype(BF16)
        for ec, q, t, k in zip(ecs, qfs, terms, kfs)
    ]
    solves = [turned(t_ref[b, h], eye).astype(BF16) for b, h in items]

    drs, dsbs, dots = [None] * len(items), [None] * len(items), [None] * len(items)
    for b in reversed(range(PER_STEP)):
        mine = [i for i, it in enumerate(items) if it[0] == b]
        dss = {i: end_ref[items[i][1]] for i in mine}
        for i in mine:
            dsbs[i] = dss[i].astype(BF16)
            dots[i] = jnp.sum(dss[i] * ss[i].astype(F32), axis=0, keepdims=True)
        dus = {i: nn(lefts[i], jnp.concatenate([dos[i], dsbs[i]], axis=0)).astype(BF16) for i in mine}
        for i in mine:
            drs[i] = nn(solves[i], dus[i])
        for i in mine:
            add = nn(downs[i], jnp.concatenate([dos[i], drs[i].astype(BF16)], axis=0))
            end_ref[items[i][1]] = jnp.exp(terms[i][7]) * dss[i] + add

    drbs = [d.astype(BF16) for d in drs]
    from_s = [nt(jnp.concatenate([a, c], axis=0), s) for a, c, s in zip(drbs, dos, ss)]
    from_u = [nt(jnp.concatenate([a, c], axis=0), u) for a, c, u in zip(drbs, dos, us)]
    ks0 = [nn(k, s) for k, s in zip(ks, ss)]
    dws = [nt(u, d) for u, d in zip(us, dsbs)]
    dgs, dbs, dks, minus, dcs, syms = [], [], [], [], [], []
    nms = []
    for i, (b, h) in enumerate(items):
        beta, e_col, e_rest, g_col, beta_e, g_row, c_col, g_last = terms[i]
        k, q = kfs[i], qfs[i]
        mixed[i] = beta * drs[i]
        d_r[h][tok[i], 3 * HD : 4 * HD] = mixed[i, pl.ds(0, SPAN, 2), :].astype(BF16)
        d_r[h][tok[i], 4 * HD : 5 * HD] = mixed[i, pl.ds(1, SPAN, 2), :].astype(BF16)
        t1 = beta_e * from_s[i][:SUB]
        t3 = e_rest * dws[i]
        fade = jnp.exp(jnp.where(strict, g_col - g_row, FAR))
        y = -from_u[i][:SUB] * fade
        le = y * prods[i][:SUB]
        hh = beta * le
        kt3 = k * t3
        dbs.append(lane_sum(drs[i] * (v_r[h][sub[i]].astype(F32) - e_col * ks0[i]) + le))
        dg = lane_sum(hh - k * t1 - kt3)
        d_last = lane_sum(jnp.sum(kt3, axis=0, keepdims=True) + jnp.exp(g_last) * dots[i])
        dgs.append(dg + jnp.where(row[:, :1] == SUB - 1, d_last, 0.0))
        dks.append(t3 - t1)
        dkk = beta * y
        syms.append(dkk + turned(dkk.astype(BF16), eye))
        nm = from_u[i][SUB:] * reads[i]
        hm = nm * prods[i][SUB:]
        t2 = ecs[i] * from_s[i][SUB:]
        nms.append((nm.astype(BF16), t2))
        dcs.append(lane_sum(hm + q * t2))
        minus.append(jnp.sum(hh, axis=0, keepdims=True) + jnp.sum(hm, axis=0, keepdims=True))
    tops = [
        nn(jnp.concatenate([s.astype(BF16), nm], axis=0), k) for s, (nm, _), k in zip(syms, nms, ks)
    ]
    turns = [nn(turned(nm, eye).astype(BF16), q) for (nm, _), q in zip(nms, qs)]
    for i, (b, h) in enumerate(items):
        d_r[h][tok[i], :HD] = (tops[i][SUB:] + nms[i][1]).astype(BF16)
        mixed[i] = dks[i] + tops[i][:SUB] + turns[i]
        d_r[h][tok[i], HD : 2 * HD] = mixed[i, pl.ds(0, SPAN, 2), :].astype(BF16)
        d_r[h][tok[i], 2 * HD : 3 * HD] = mixed[i, pl.ds(1, SPAN, 2), :].astype(BF16)
        cums[i] = jnp.where(col == 0, dbs[i], jnp.where(col == 1, dgs[i], 0.0))
        odd = pl.ds(1, SPAN, 2)
        cums[i, odd, :] = cums[i, odd, :] + jnp.where(col[:SPAN] == 1, dcs[i], 0.0)
        rows = jnp.transpose(cums[i])[:8]
        first = iota((8, SUB), 0)
        summed = exact_nn(rows - jnp.where(first == 1, minus[i], 0.0), later)
        drows_r[h][b] = jnp.where(first == 0, rows, summed)


def recur_back(gain, start, dz, q, k, v, gate, rows, o, u, s, t, first, steps, done=()):
    heads = len(q)
    tok, sub, row, wide, mat, one, state = recur_specs(heads, lambda i: first + steps - 1 - i)
    o_tok, o_sub, _, _, o_mat, _, _ = recur_specs(heads, lambda i: steps - 1 - i)
    n = steps * PER_STEP
    seq = q[0].shape[0]
    d_spec = pl.BlockSpec((PER_STEP * SPAN, 6 * HD), lambda i: (first + steps - 1 - i, 0))

    def shape(s, d):
        return jax.ShapeDtypeStruct(s, d)

    res = pl.pallas_call(
        functools.partial(recur_back_kernel, heads, len(done)),
        out_shape=[shape((seq, 6 * HD), BF16)] * heads
        + [shape((seq // SPAN, 8, SUB), F32)] * heads
        + [shape((1, HD), F32), shape((heads, HD, HD), F32)],
        grid=(steps,),
        in_specs=[one, state, wide]
        + [tok] * heads
        + [sub] * (2 * heads)
        + [tok] * heads
        + [row] * heads
        + [o_tok] * heads
        + [o_sub] * heads
        + [o_mat] * 2
        + [pl.BlockSpec(memory_space=pl.ANY)] * len(done),
        out_specs=[d_spec] * heads + [row] * heads + [one, state],
        scratch_shapes=[pltpu.VMEM((PER_STEP * heads, SUB, SUB), F32)] * 2,
        compiler_params=params(),
        input_output_aliases={5 + 7 * heads + i: i for i in range(len(done))},
        cost_estimate=cost(heads * n * 30 * 4.2e6, 1e6),
        name="recur_back",
    )(gain, start, dz, *q, *k, *v, *gate, *rows, *o, *u, s, t, *done)
    return res[:heads], res[heads : 2 * heads], res[2 * heads], res[2 * heads + 1]


def project_back_kernel(pieces, bit, h, scal_ref, a_ref, cw_ref, raw_ref, rows_ref, d_ref, drow_ref, *refs):
    outer, refs = refs[:pieces], refs[pieces:]
    dp_ref, dcw_ref, dsm_ref = refs[:3]
    stacked = refs[3:5]
    raw_s, ds_s, acc, aux_s = refs[5:]
    tile = a_ref.shape[0]
    depth = outer[0].shape[1]
    chunk = 64
    step, steps = pl.program_id(0), pl.num_programs(0)
    base = pl.multiple_of((steps - 1 - step) * tile, tile)

    @pl.when(step == 0)
    def _():
        ds_s[tile : tile + 8, :] = jnp.zeros_like(ds_s[tile : tile + 8, :])
        dcw_ref[...] = jnp.zeros_like(dcw_ref)
        dsm_ref[...] = jnp.zeros_like(dsm_ref)

    @pl.when(step > 0)
    def _():
        ds_s[tile : tile + 8, :] = ds_s[0:8, :]

    @pl.when(step == steps - 1)
    def _():
        raw_s[0:8, :] = jnp.zeros_like(raw_s[0:8, :])

    @pl.when(step < steps - 1)
    def _():
        before = raw_ref[pl.ds(pl.multiple_of(base - 16, 16), 16), :].astype(F32)
        raw_s[0:8, :] = before[8:]

    raw_s[8 : tile + 8, :] = raw_ref[pl.ds(base, tile), :].astype(F32)
    for g in range(5):
        lanes = slice(g * HD, (g + 1) * HD)
        taps = cw_ref[0, :, lanes]
        sums = [jnp.zeros((8, HD), F32)] * TAPS
        for i in range(tile // chunk):
            start = i * chunk
            shifted = conv_shifts(raw_s, start, chunk, lanes)
            pre = shifted[0] * taps[0:1]
            for j in range(1, TAPS):
                pre = pre + shifted[j] * taps[j : j + 1]
            sg = sigmoid(pre)
            act = pre * sg
            d = d_ref[start : start + chunk, lanes].astype(F32)
            if g < 3:
                inv = lax.rsqrt(lane_sum(act * act) + EPS_UNIT)
                unit = act * inv
                d = inv * (d - unit * lane_sum(d * unit))
            d = d * (sg + act * (1.0 - sg))
            ds_s[start : start + chunk, lanes] = d
            sums = [s + jnp.sum((d * x).reshape(chunk // 8, 8, HD), axis=0) for s, x in zip(sums, shifted)]
        for j in range(TAPS):
            dcw_ref[j : j + 1, lanes] += jnp.sum(sums[j], axis=0, keepdims=True)
        for i in range(tile // chunk):
            start = i * chunk
            views = conv_shifts_back(ds_s, start, chunk, lanes)
            total = views[0] * taps[0:1]
            for j in range(1, TAPS):
                total = total + views[j] * taps[j : j + 1]
            dp_ref[start : start + chunk, lanes] = total.astype(BF16)

    rate = scal_ref[h, 0]
    lane = iota((SPAN, HD), 1)
    total = jnp.zeros((8, HD), F32)
    for b in range(tile // SPAN):
        both = jnp.concatenate([rows_ref[b], drow_ref[b]] + [jnp.zeros((8, SUB), F32)] * (SUB // 8 - 2), axis=0)
        aux_s[b] = jnp.transpose(both)
        even, odd = aux_s[b, pl.ds(0, SPAN, 2), :], aux_s[b, pl.ds(1, SPAN, 2), :]
        b1, b2, dg = even[:, 0:1], odd[:, 0:1], even[:, 9:10]
        darg = -rate * dg * sigmoid(even[:, 2:3])
        d1 = even[:, 8:9] * b1 * (1.0 - b1)
        d2 = odd[:, 8:9] * b2 * (1.0 - b2)
        vals = jnp.where(lane == 0, d1, jnp.where(lane == 1, d2, jnp.where(lane == 2, darg, 0.0)))
        here = pl.ds(b * SPAN, SPAN)
        dp_ref[here, 6 * HD :] = vals[:, :SMALL].astype(BF16)
        dp_ref[here, 5 * HD : 6 * HD] = d_ref[here, 5 * HD :]
        extra = jnp.where(lane == 0, dg * even[:, 1:2], jnp.where(lane == 1, darg, 0.0))
        total += jnp.sum(extra.reshape(SPAN // 8, 8, HD), axis=0)
    dsm_ref[...] += total

    term = tn(dp_ref[...], a_ref[...])

    @pl.when(step == 0)
    def _():
        acc[...] = term

    @pl.when(step > 0)
    def _():
        acc[...] += term

    @pl.when(step == steps - 1)
    def _():
        for stack, group in zip(stacked, sides(pieces, bit)):
            for i, p in enumerate(group):
                stack[i, :HD] = outer[p][...]
                stack[i, HD:] = acc[:, p * depth : (p + 1) * depth].astype(BF16)


def project_back(h, normed, conv_t, scal, raw, rows, d, drows, outer, bit):
    seq, dim = normed.shape
    pieces = len(outer)
    depth = outer[0].shape[1]
    tile = min(512, seq)
    end = seq // tile - 1
    along = lambda i: (end - i, 0)
    deep = pl.BlockSpec((tile // SPAN, 8, SUB), lambda i: (end - i, 0, 0))
    fix = lambda i: (0, 0)
    outs = [((seq, UNITS), BF16), ((8, 5 * HD), F32), ((8, HD), F32)]
    shapes = [jax.ShapeDtypeStruct(s, t) for s, t in outs] + stacks(pieces, (HD + UNITS, depth))
    res = pl.pallas_call(
        functools.partial(project_back_kernel, pieces, bit, h),
        out_shape=shapes,
        grid=(seq // tile,),
        in_specs=[
            pl.BlockSpec(memory_space=pltpu.SMEM),
            pl.BlockSpec((tile, dim), along),
            pl.BlockSpec((1,) + conv_t.shape[1:], lambda i: (h, 0, 0)),
            pl.BlockSpec(raw.shape, fix),
            deep,
            pl.BlockSpec((tile, 6 * HD), along),
            deep,
        ]
        + [pl.BlockSpec(g.shape, fix) for g in outer],
        out_specs=[pl.BlockSpec((tile, UNITS), along)]
        + [pl.BlockSpec(s, fix) for s, _ in outs[1:]]
        + [pl.BlockSpec(v.shape, lambda i: (0, 0, 0)) for v in shapes[3:]],
        scratch_shapes=[
            pltpu.VMEM((tile + 8, 5 * HD), F32),
            pltpu.VMEM((tile + 8, 5 * HD), F32),
            pltpu.VMEM((UNITS, dim), F32),
            pltpu.VMEM((tile // SPAN, SUB, SUB), F32),
        ],
        compiler_params=params(),
        cost_estimate=cost(2 * seq * dim * UNITS, 1e6),
        name="project_back",
    )(scal, normed, conv_t, raw, rows, d, drows, *outer)
    return res[0], res[1], res[2], res[3:]


def input_back_kernel(heads, pieces, *refs):
    dps, parts = refs[:heads], refs[heads : heads + heads * pieces]
    x_ref, da_ref, dgain_ref = refs[heads + heads * pieces :]
    depth = parts[0].shape[1]
    x = x_ref[...].astype(F32)
    unit = x * lax.rsqrt(jnp.mean(x * x, axis=-1, keepdims=True) + EPS_NORM)
    shares = []
    for p in range(pieces):
        total = nn(
            jnp.concatenate([d[:, 6 * HD :] for d in dps], axis=1),
            jnp.concatenate([parts[h * pieces + p][7 * HD :] for h in range(heads)], axis=0),
        )
        for h in range(heads):
            total += nn(dps[h][:, : 6 * HD], parts[h * pieces + p][HD : 7 * HD])
        low = total.astype(BF16)
        lanes = slice(p * depth, (p + 1) * depth)
        da_ref[:, lanes] = low
        shares.append(jnp.sum(low.astype(F32) * unit[:, lanes], axis=0, keepdims=True))
    share = jnp.concatenate(shares, axis=1)

    @pl.when(pl.program_id(0) == 0)
    def _():
        dgain_ref[...] = share

    @pl.when(pl.program_id(0) > 0)
    def _():
        dgain_ref[...] += share


def input_back(dps, parts, x):
    seq = dps[0].shape[0]
    heads, pieces = len(parts), len(parts[0])
    flat = [w for head in parts for w in head]
    dim = pieces * flat[0].shape[1]
    tile = min(256, seq)
    along = lambda i: (i, 0)
    return pl.pallas_call(
        functools.partial(input_back_kernel, heads, pieces),
        out_shape=[jax.ShapeDtypeStruct((seq, dim), BF16), jax.ShapeDtypeStruct((1, dim), F32)],
        grid=(seq // tile,),
        in_specs=[pl.BlockSpec((tile, UNITS), along)] * heads
        + [pl.BlockSpec(w.shape, lambda i: (0, 0)) for w in flat]
        + [pl.BlockSpec((tile, dim), along)],
        out_specs=[pl.BlockSpec((tile, dim), along), pl.BlockSpec((1, dim), lambda i: (0, 0))],
        compiler_params=params(),
        cost_estimate=cost(2 * seq * dim * UNITS * heads, 1e6),
        name="input_back",
    )(*dps, *flat, x)


def mix_kernel(heads, pieces, z_ref, *refs):
    parts, out_ref = refs[:-1], refs[-1]
    depth = parts[0].shape[1]
    for p in range(pieces):
        right = jnp.concatenate([parts[h * pieces + p][...] for h in range(heads)], axis=0)
        out_ref[:, p * depth : (p + 1) * depth] = nn(z_ref[...], right).astype(BF16)


def outer_specs(parts):
    return [pl.BlockSpec((HD, w.shape[1]), lambda i: (0, 0)) for head in parts for w in head]


def mix_out(z, parts):
    seq = z.shape[0]
    heads, pieces = len(parts), len(parts[0])
    dim = pieces * parts[0][0].shape[1]
    tile = min(256, seq)
    along = lambda i: (i, 0)
    return pl.pallas_call(
        functools.partial(mix_kernel, heads, pieces),
        out_shape=jax.ShapeDtypeStruct((seq, dim), BF16),
        grid=(seq // tile,),
        in_specs=[pl.BlockSpec((tile, z.shape[1]), along)] + outer_specs(parts),
        out_specs=pl.BlockSpec((tile, dim), along),
        compiler_params=params(),
        cost_estimate=cost(2 * seq * dim * z.shape[1], 1e6),
        name="mix_out",
    )(z, *[w for head in parts for w in head])


def mix_back_kernel(heads, pieces, gain_ref, own_ref, other_ref, mid_ref, dy_ref, z_ref, *refs):
    parts, refs = refs[: heads * pieces], refs[heads * pieces :]
    dmix_ref, dz_ref, dgain_ref = refs[:3]
    grads, acc = refs[3:-1], refs[-1]
    depth = parts[0].shape[1]
    step, steps = pl.program_id(0), pl.num_programs(0)
    mid = mid_ref[...]
    dn = own_ref[...].astype(F32) + other_ref[...].astype(F32)
    inv = lax.rsqrt(jnp.mean(mid * mid, axis=-1, keepdims=True) + EPS_NORM)
    unit = mid * inv
    prod = dn * unit
    share = jnp.sum(prod, axis=0, keepdims=True)
    scaled = dn * gain_ref[...]
    back = inv * (scaled - unit * jnp.mean(prod * gain_ref[...], axis=-1, keepdims=True))
    dmix_ref[...] = (dy_ref[...].astype(F32) + back).astype(BF16)

    @pl.when(step == 0)
    def _():
        dgain_ref[...] = share
        acc[...] = jnp.zeros_like(acc)

    @pl.when(step > 0)
    def _():
        dgain_ref[...] += share

    dz = jnp.zeros((z_ref.shape[0], heads * HD), F32)
    for p in range(pieces):
        lanes = slice(p * depth, (p + 1) * depth)
        right = jnp.concatenate([parts[h * pieces + p][...] for h in range(heads)], axis=0)
        dz += nt(dmix_ref[:, lanes], right)
    acc[...] += tn(z_ref[...], dmix_ref[...])
    dz_ref[...] = dz.astype(BF16)

    @pl.when(step == steps - 1)
    def _():
        for h in range(heads):
            for p in range(pieces):
                grads[h * pieces + p][...] = acc[h * HD : (h + 1) * HD, p * depth : (p + 1) * depth].astype(BF16)


def mix_back(gain, own, other, mid, dy, z, parts):
    seq, dim = mid.shape
    heads, pieces = len(parts), len(parts[0])
    wide = z.shape[1]
    tile = min(256, seq)
    row = pl.BlockSpec((tile, dim), lambda i: (i, 0))
    one = pl.BlockSpec((1, dim), lambda i: (0, 0))
    zs = pl.BlockSpec((tile, wide), lambda i: (i, 0))
    res = pl.pallas_call(
        functools.partial(mix_back_kernel, heads, pieces),
        out_shape=[
            jax.ShapeDtypeStruct((seq, dim), BF16),
            jax.ShapeDtypeStruct((seq, wide), BF16),
            jax.ShapeDtypeStruct((1, dim), F32),
        ]
        + [jax.ShapeDtypeStruct((HD, dim // pieces), BF16)] * (heads * pieces),
        grid=(seq // tile,),
        in_specs=[one, row, row, row, row, zs] + outer_specs(parts),
        out_specs=[row, zs, one] + outer_specs(parts),
        scratch_shapes=[pltpu.VMEM((wide, dim), F32)],
        compiler_params=params(),
        cost_estimate=cost(4 * seq * dim * wide, 1e6),
        name="mix_back",
    )(gain, own, other, mid, dy, z, *[w for head in parts for w in head])
    return res[0], res[1], res[2], [res[3 + h * pieces : 3 + (h + 1) * pieces] for h in range(heads)]


def select_kernel(counts, apart, table_ref, *refs):
    j = pl.program_id(0)
    first = 0
    for g, n in enumerate(counts):
        width = refs[first].shape[2]
        value = refs[first][...]
        for i in range(1, n):
            value = jnp.where(table_ref[2 * g, j] == i, refs[first + i][...], value)
        if apart:
            refs[sum(counts) + g][...] = value
        else:
            refs[-1][:, :, g * width : (g + 1) * width] = value
        first += n


def select_blocks(groups, table, count, apart=False):
    specs, flat = [], []
    for g, sources in enumerate(groups):
        for i, value in enumerate(sources):

            def where(j, t, g=g, i=i):
                return (jnp.where(t[2 * g, j] == i, t[2 * g + 1, j], 0), 0, 0)

            specs.append(pl.BlockSpec((1,) + value.shape[1:], where))
            flat.append(value)
    piece, width = flat[0].shape[1:]
    total = width if apart else width * len(groups)
    outs = len(groups) if apart else 1
    res = pl.pallas_call(
        functools.partial(select_kernel, [len(g) for g in groups], apart),
        out_shape=[jax.ShapeDtypeStruct((count, piece, total), flat[0].dtype)] * outs,
        grid_spec=pltpu.PrefetchScalarGridSpec(
            num_scalar_prefetch=1,
            grid=(count,),
            in_specs=specs,
            out_specs=[pl.BlockSpec((1, piece, total), lambda j, t: (j, 0, 0))] * outs,
        ),
        compiler_params=params(),
        cost_estimate=cost(1e6, 1e6),
        name="select_blocks",
    )(table, *flat)
    return res if apart else res[0]


def ffn_kernel(pieces, chunks, bits, more, b_ref, dy_ref, *refs):
    weights = refs[: pieces * chunks]
    refs = refs[pieces * chunks :]
    sums_in, refs = (refs[:2], refs[2:]) if more else (None, refs)
    out_ref, db_ref = refs[:2]
    stacked = refs[2 : 2 + 2 * chunks]
    b_s, dy_s, hid_s, dg_s, du_s = refs[2 + 2 * chunks :]
    depth = weights[0].shape[1]
    units = weights[0].shape[0] // 3
    tile = b_ref.shape[0]
    step, steps = pl.program_id(0), pl.num_programs(0)

    def weight(p, i):
        return jnp.concatenate(
            [weights[c * pieces + p][i * units : (i + 1) * units] for c in range(chunks)], axis=0
        )

    rows = pl.ds(pl.multiple_of(step * tile, tile), tile)
    b_s[rows, :] = b_ref[...]
    dy_s[rows, :] = dy_ref[...]
    gate = jnp.zeros((tile, units * chunks), F32)
    up = jnp.zeros((tile, units * chunks), F32)
    dh = jnp.zeros((tile, units * chunks), F32)
    for p in range(pieces):
        lanes = slice(p * depth, (p + 1) * depth)
        block, dblock = b_ref[:, lanes], dy_ref[:, lanes]
        gate += nt(block, weight(p, 0))
        up += nt(block, weight(p, 1))
        dh += nt(dblock, weight(p, 2))
    sg = sigmoid(gate)
    act = gate * sg
    hid = (act * up).astype(BF16)
    du = (dh * act).astype(BF16)
    dg = (dh * up * (sg + act * (1.0 - sg))).astype(BF16)
    hid_s[rows, :] = hid
    dg_s[rows, :] = dg
    du_s[rows, :] = du
    for p in range(pieces):
        lanes = slice(p * depth, (p + 1) * depth)
        o = nn(hid, weight(p, 2))
        d = nn(dg, weight(p, 0)) + nn(du, weight(p, 1))
        if more:
            o += sums_in[0][:, lanes].astype(F32)
            d += sums_in[1][:, lanes].astype(F32)
        out_ref[:, lanes] = o.astype(out_ref.dtype)
        db_ref[:, lanes] = d.astype(db_ref.dtype)

    @pl.when(step == steps - 1)
    def _():
        for i, (left, right) in enumerate([(dg_s, b_s), (du_s, b_s), (hid_s, dy_s)]):
            g = tn(left[...], right[...]).astype(BF16)
            for c in range(chunks):
                for stack, group in zip(stacked[2 * c : 2 * c + 2], sides(pieces, bits[c])):
                    for n, p in enumerate(group):
                        stack[n, i * units : (i + 1) * units] = g[
                            c * units : (c + 1) * units, p * depth : (p + 1) * depth
                        ]


def ffn(normed, dy, parts, bits, sums=None, last=True):
    seq, dim = normed.shape
    chunks, pieces = len(parts), len(parts[0])
    flat = [w for chunk in parts for w in chunk]
    units = flat[0].shape[0] // 3
    tile = min(256, seq)
    row = pl.BlockSpec((tile, dim), lambda i: (i, 0))
    more = () if sums is None else tuple(sums)
    grads = stacks(pieces, flat[0].shape) * chunks
    res = pl.pallas_call(
        functools.partial(ffn_kernel, pieces, chunks, bits, bool(more)),
        out_shape=[jax.ShapeDtypeStruct((seq, dim), BF16 if last else F32)] * 2 + grads,
        grid=(seq // tile,),
        in_specs=[row, row] + [pl.BlockSpec(w.shape, lambda i: (0, 0)) for w in flat] + [row] * len(more),
        out_specs=[row, row] + [pl.BlockSpec(g.shape, lambda i: (0, 0, 0)) for g in grads],
        scratch_shapes=[pltpu.VMEM((seq, dim), BF16)] * 2 + [pltpu.VMEM((seq, units * chunks), BF16)] * 3,
        compiler_params=params(),
        cost_estimate=cost(18 * seq * dim * units * chunks, 1e6),
        name="ffn",
    )(normed, dy, *flat, *more)
    return res[0], res[1], [res[2 + 2 * c : 4 + 2 * c] for c in range(chunks)]


def sync(*trees):
    leaves, tree = jax.tree.flatten(trees)
    return jax.tree.unflatten(tree, lax.optimization_barrier(leaves))


def bits_of(n):
    return [1 << i for i in range(n.bit_length() - 1)]


class Place:
    def __init__(self):
        self.n_f = lax.axis_size("fsdp")
        self.n_t = lax.axis_size("tp")
        self.chips = self.n_f // 2
        f = lax.axis_index("fsdp")
        self.f = f
        self.core = f % 2
        self.k = f // 2
        self.t = lax.axis_index("tp")

    def swap(self, value):
        return lax.ppermute(value, "fsdp", [(i, i ^ 1) for i in range(self.n_f)])

    def move(self, value, bit):
        return lax.ppermute(value, "fsdp", [(i, i ^ (2 * bit)) for i in range(self.n_f)])

    def turn(self, value, r):
        return lax.ppermute(value, "tp", [(i, (i + r) % self.n_t) for i in range(self.n_t)])

    def in_order(self, mine, other, axis):
        first = jnp.where(self.core == 0, mine, other)
        second = jnp.where(self.core == 0, other, mine)
        return jnp.concatenate([first, second], axis=axis)

    def halves(self, value, axis):
        size = value.shape[axis] // 2
        return (
            lax.dynamic_slice_in_dim(value, self.core * size, size, axis),
            lax.dynamic_slice_in_dim(value, (1 - self.core) * size, size, axis),
        )

    def relative(self, value):
        width = value.shape[-1] // self.chips
        blocks = [
            lax.dynamic_slice_in_dim(value, (self.k ^ p) * width, width, value.ndim - 1) for p in range(self.chips)
        ]
        return jnp.concatenate(blocks, axis=-1)

    def spread_out(self, value):
        if value.shape[0] < self.n_t:
            value = jnp.pad(value, ((0, self.n_t - value.shape[0]),) + ((0, 0),) * (value.ndim - 1))
        return lax.all_to_all(value, "tp", split_axis=0, concat_axis=0, tiled=True)

    def all_sum(self, value):
        return self.chip_sum(self.line_sum(value))

    def chip_sum(self, value):
        for bit in [1] + [2 * b for b in bits_of(self.chips)]:
            value = value + lax.ppermute(value, "fsdp", [(i, i ^ bit) for i in range(self.n_f)])
        return value

    def line_sum(self, value):
        total = value
        for r in range(1, self.n_t):
            total = total + self.turn(value, r)
        return total

def rms_terms(value):
    return lax.rsqrt(jnp.mean(value * value, axis=-1, keepdims=True) + EPS_NORM)


def rms_back(value, gain, d_normed):
    inv = rms_terms(value)
    unit = value * inv
    dn = d_normed * gain
    return inv * (dn - unit * jnp.mean(dn * unit, axis=-1, keepdims=True))


class Gather:
    def __init__(self, at, shard):
        self.at = at
        self.parts = {(0, 0): shard}

    def turn(self, r, by=None):
        by = by or r
        self.parts[r, 0] = self.at.turn(self.parts[r - by, 0], by)

    def move(self, r, to, via):
        self.parts[r, to] = self.at.move(self.parts[r, to ^ via], via)

    def full(self, r):
        return [self.parts[r, p] for p in range(self.at.chips)]

    def rest(self):
        for r in range(1, self.at.n_t):
            self.turn(r)
        for r in range(self.at.n_t):
            for p in range(1, self.at.chips):
                self.move(r, p, p & -p)
        return [self.full(r) for r in range(self.at.n_t)]


def first_bit(at, r, late=False):
    return at.chips // 2 if r == 3 or r == (2 if late else 0) else 1


class Scatter:
    def __init__(self, at, late=False):
        self.at = at
        self.bit = lambda r: first_bit(at, r, late)
        self.near, self.far, self.two, self.one, self.end = {}, {}, {}, {}, {}

    def put(self, r, stacked):
        self.near[r], self.far[r] = stacked

    def cross(self, *turns):
        for r in turns:
            self.far[r] = self.at.move(self.far[r], self.bit(r))

    def add(self, *turns):
        sums = add_stacks([(self.near.pop(r), self.far.pop(r)) for r in turns])
        return dict(zip(turns, sums))

    def pass_on(self, sums):
        for r, (keep, give) in sums.items():
            self.two[r] = keep, self.at.move(give, 3 - self.bit(r))

    def fold(self, *turns):
        self.pass_on(self.add(*turns))

    def close(self, *turns):
        for r in turns:
            keep, came = self.two.pop(r)
            self.one[r] = (keep.astype(F32) + came.astype(F32)).astype(BF16)

    def home(self, r):
        self.end[r] = self.at.turn(self.one.pop(r), self.at.n_t - r)

    def merge(self, r):
        self.end[r] = self.at.turn(self.one.pop(r), self.at.n_t - 1)

    def join(self, r):
        self.one[r - 1] = (self.one[r - 1].astype(F32) + self.end.pop(r).astype(F32)).astype(BF16)

    def total(self):
        return sum(v.astype(F32) for v in list(self.one.values()) + list(self.end.values()))

    def state(self):
        return self.near, self.far, self.two, self.one, self.end

    def take(self, state):
        self.near, self.far, self.two, self.one, self.end = state

    def rest(self):
        for r in range(self.at.n_t):
            have = {}
            for stack, group in zip((self.near.pop(r), self.far.pop(r)), sides(self.at.chips, self.bit(r))):
                have.update({p: stack[i] for i, p in enumerate(group)})
            for bit in bits_of(self.at.chips):
                for p in [p for p in have if p & bit]:
                    came = self.at.move(have.pop(p), bit)
                    have[p ^ bit] = (have[p ^ bit].astype(F32) + came.astype(F32)).astype(BF16)
            self.one[r] = have[0]
            if r:
                self.home(r)


class Routing:
    def __init__(self, at, value, order, source):
        self.at, self.order = at, order
        self.per_chip = value.shape[0]
        self.have, self.where = [value], [0]
        reach = [0]
        for bit in order[:-1]:
            reach += [w | bit for w in reach]
        tables = []
        for chip in (at.k ^ order[-1], at.k):
            ask = lax.dynamic_slice_in_dim(source, chip * self.per_chip, self.per_chip, 0)
            distance = (ask // self.per_chip) ^ at.k
            src = sum(jnp.where(distance == w, i, 0) for i, w in enumerate(reach))
            near = (distance & order[-1]) == 0
            slot = ask % self.per_chip
            if chip is not at.k:
                tables.append((src, slot))
            else:
                tables.append(
                    (
                        jnp.where(near, src, len(reach)),
                        jnp.where(near, slot, jnp.arange(self.per_chip, dtype=jnp.int32)),
                    )
                )
        self.ask, self.keep = (jnp.stack(t) for t in tables)

    def step(self):
        bit = self.order[len(self.where).bit_length() - 1]
        self.have = self.have + [self.at.move(v, bit) for v in self.have]
        self.where = self.where + [w | bit for w in self.where]

    def last(self, give):
        self.have = self.have + [self.at.move(give, self.order[-1])]


def local(
    tokens, lengths, perm, cotangent, norm1_gain, input_weight, conv_w, decay_log, decay_bias, out_gain, w_out,
    norm2_gain, gate_up_weight, down_weight
):
    at = Place()
    slots, piece, dim = tokens.shape
    n_f, n_t, chips = at.n_f, at.n_t, at.chips
    heads_all = conv_w.shape[0]
    heads = heads_all // 2
    local_heads = input_weight.shape[1]
    cols = input_weight.shape[2]
    by_turn = local_heads == 2
    laps = list(range(n_t))
    bits = bits_of(chips)
    fast = by_turn and chips == 4 and n_t == 4
    per_chip = 2 * slots
    seq = n_t * piece
    steps = seq // SPAN // PER_STEP // 2

    pad = SMALL - (cols - 6 * HD)
    if by_turn:
        packed = jnp.transpose(input_weight, (1, 2, 0))
        zeros = jnp.zeros((local_heads, pad, packed.shape[2]), BF16)
        packed = jnp.concatenate([w_out.reshape(local_heads, HD, -1), packed, zeros], axis=1)
        mine, give = at.halves(packed, 0)
        m_own = at.in_order(mine[0], at.swap(give[0]), 1)
        head_ids = ((at.t - jnp.arange(n_t, dtype=jnp.int32)) % n_t) * 2 + at.core
    else:
        m_own = None
        head_ids = at.core * heads + jnp.arange(heads, dtype=jnp.int32)
    mine, give = at.halves(tokens, 2)
    both = at.in_order(mine, at.swap(give), 0)
    both, m_own, gate_up_weight, down_weight, cotangent = sync(both, m_own, gate_up_weight, down_weight, cotangent)
    packed = jnp.concatenate([jnp.transpose(gate_up_weight, (1, 2, 0)), down_weight[None]], axis=0)
    mine, give = at.halves(packed, 1)
    f_own = at.in_order(mine, at.swap(give), 2)
    f_own = f_own.reshape(-1, f_own.shape[2])
    mine, give = at.halves(cotangent, 2)
    cot_both = at.in_order(mine, at.swap(give), 0)

    own = head_ids[:, None] == jnp.arange(heads_all, dtype=jnp.int32)[None, :]
    taps = jnp.pad(jnp.transpose(conv_w, (0, 2, 1)), ((0, 0), (0, 8 - TAPS), (0, 0)))
    conv_t = jnp.sum(jnp.where(own[:, :, None, None], taps[None], 0.0), axis=1)
    scal = jnp.stack(
        [
            jnp.sum(jnp.where(own, jnp.exp(decay_log)[None], 0.0), axis=1),
            jnp.sum(jnp.where(own, decay_bias[None], 0.0), axis=1),
        ],
        axis=1,
    )
    gain1 = at.relative(norm1_gain)
    gain2 = at.relative(norm2_gain)
    gain_o = out_gain[None]
    start_state = jnp.zeros((heads, HD, HD), F32)

    seq_id = jnp.minimum(at.k * per_chip + at.t, lengths.shape[0] - 1)
    length = jnp.where(at.t < per_chip, lax.dynamic_index_in_dim(lengths, seq_id, 0, keepdims=False), 0)
    live = (jnp.arange(seq, dtype=jnp.int32) < length).astype(BF16)[:, None]
    slot_ids = jnp.arange(perm.shape[0], dtype=jnp.int32)
    source = jnp.sum(jnp.where(perm[None, :] == slot_ids[:, None], slot_ids[None, :], 0), axis=1)
    quarter = dim // 4
    routes = [
        Routing(at, cot_both[:, :, :quarter], bits, source),
        Routing(at, cot_both[:, :, quarter:], bits[::-1], source),
    ]

    def route_state():
        return [r.have for r in routes]

    def set_routes(state):
        for r, v in zip(routes, state):
            r.have = v

    def routed():
        groups = [r.have for r in routes]
        return select_blocks(groups, jnp.concatenate([r.keep for r in routes], axis=0), per_chip)

    def sequence(half):
        half = half.reshape(seq, -1)
        return at.relative(at.in_order(half, at.swap(half), 1))

    def norm_first(x):
        return (x * rms_terms(x) * gain1).astype(BF16)

    f = Gather(at, f_own)
    proj = {}

    def asked():
        return select_blocks([r.have for r in routes], jnp.concatenate([r.ask for r in routes], axis=0), per_chip, True)

    if fast:
        m = Gather(at, m_own)

        def run(r):
            proj[r] = project(r, normed_one, m.full(r), conv_t, scal)

        def without(parts, *keys):
            return {k: v for k, v in parts.items() if k not in keys}

        came = at.spread_out(both)
        for p in range(1, chips):
            m.move(0, p, p)
        m.parts, f.parts, came, cot_both, conv_t, scal, gain1, gain2, live, extra = sync(
            m.parts, f.parts, came, cot_both, conv_t, scal, gain1, gain2, live, [(r.ask, r.keep) for r in routes]
        )
        for r, (ask, keep), part in zip(routes, extra, (cot_both[:, :, :quarter], cot_both[:, :, quarter:])):
            r.ask, r.keep, r.have = ask, keep, [part]
        m.turn(1)
        for r in routes:
            r.step()
        x = sequence(came)
        normed_one = norm_first(x.astype(F32))
        run(0)
        state = route_state()
        m.parts, f.parts, state, proj[0], normed_one, x = sync(m.parts, f.parts, state, proj[0], normed_one, x)
        set_routes(state)
        m.turn(3)
        m.move(1, 1, 1)
        m.move(1, 2, 2)
        give = asked()
        m.parts, f.parts, give = sync(m.parts, f.parts, give)
        m.turn(2, 1)
        m.move(3, 1, 1)
        m.move(3, 2, 2)
        early = without(m.parts, (2, 0))
        early, f.parts, give = sync(early, f.parts, give)
        m.parts.update(early)
        m.move(1, 3, 1)
        m.move(3, 3, 2)
        f.turn(1)
        m.parts, f.parts, give = sync(m.parts, f.parts, give)
        m.move(2, 1, 1)
        m.move(2, 2, 2)
        for r, part in zip(routes, give):
            r.last(part)
        f.turn(3)
        run(1)
        run(3)
        state = route_state()
        m.parts, proj, normed_one, f.parts, state = sync(m.parts, proj, normed_one, f.parts, state)
        set_routes(state)
        m.move(2, 3, 1)
        f.turn(2, 1)
        f.move(0, 1, 1)
        f.move(0, 2, 2)
        cot_home = routed()
        early = without(f.parts, (0, 1), (0, 2))
        m.parts, early, cot_home, normed_one = sync(m.parts, early, cot_home, normed_one)
        f.parts.update(early)
        cot_came = at.spread_out(cot_home)
        f.move(1, 1, 1)
        f.move(1, 2, 2)
        run(2)
        early = without(f.parts, (1, 1), (1, 2))
        proj, early = sync(proj, early)
        f.parts.update(early)
        m_parts = [m.full(r) for r in laps]
    else:
        x = sequence(at.spread_out(both))
        normed_one = norm_first(x.astype(F32))
        if by_turn:
            m_parts = Gather(at, m_own).rest()
        else:
            full = lax.all_gather(lax.all_gather(input_weight, "tp", axis=1, tiled=True), "fsdp", axis=0, tiled=True)
            full = at.relative(jnp.transpose(full, (1, 2, 0)))
            full_out = lax.all_gather(lax.all_gather(w_out, "tp", axis=0, tiled=True), "fsdp", axis=1, tiled=True)
            full_out = at.relative(full_out).reshape(heads_all, HD, dim)
            zeros = jnp.zeros((heads_all, pad, dim), BF16)
            full = at.halves(jnp.concatenate([full_out, full, zeros], axis=1), 0)[0]
            m_parts = [jnp.split(full[h], chips, axis=1) for h in range(heads)]
        for h in range(heads):
            proj[h] = project(h, normed_one, m_parts[h], conv_t, scal)
        for r in routes:
            for _ in bits[1:]:
                r.step()
        for r, part in zip(routes, asked()):
            r.last(part)
        cot_came = at.spread_out(routed())
        f_parts = f.rest()

    raw, gate, q, k, v, rows = (list(group) for group in zip(*[proj[h] for h in range(heads)]))
    if fast:
        f.move(0, 3, 2)
    first = recur(gain_o, start_state, q, k, v, gate, rows, 0, steps)
    if fast:
        first, f.parts, cot_came = sync(first, f.parts, cot_came)
        f.move(1, 3, 1)
        for r in (3, 2):
            f.move(r, 1, 1)
            f.move(r, 2, 2)
    second = recur(gain_o, first[1], q, k, v, gate, rows, steps, steps, first[0])
    if fast:
        early = without(f.parts, (2, 1), (2, 2))
        second, early = sync(second, early)
        f.parts.update(early)
    z = second[0]
    mix = mix_out(z, m_parts)
    mid = x.astype(F32) + (mix.astype(F32) + at.swap(mix).astype(F32))
    normed_two = (mid * rms_terms(mid) * gain2).astype(BF16)
    dy = live * sequence(cot_came)

    f_rs = Scatter(at)
    half = n_t // 2
    group_a, group_b = laps[:half], laps[half:][::-1]
    bits_a, bits_b = [first_bit(at, r) for r in group_a], [first_bit(at, r) for r in group_b]
    if fast:
        normed_two, dy, f.parts = sync(normed_two, dy, f.parts)
        f.move(2, 3, 1)
        f.move(3, 3, 2)
        f_parts = {r: f.full(r) for r in group_a}
    net, db, grads = ffn(normed_two, dy, [f_parts[r] for r in group_a], bits_a, last=False)
    if fast:
        net, db, grads, f.parts = sync(net, db, grads, f.parts)
        f_parts = {r: f.full(r) for r in group_b}
    for r, g in zip(group_a, grads):
        f_rs.put(r, g)
    if fast:
        f_rs.cross(0, 1)
    net, db, grads = ffn(normed_two, dy, [f_parts[r] for r in group_b], bits_b, (net, db))
    if fast:
        net, db, grads, state = sync(net, db, grads, f_rs.state())
        f_rs.take(state)
    for r, g in zip(group_b, grads):
        f_rs.put(r, g)

    db_other = at.swap(db)
    if fast:
        f_rs.fold(0, 1)
        f_rs.cross(3, 2)
    d_mix, dz, g_gain2, g_out = mix_back(gain2[None], db, db_other, mid, dy, z, m_parts)
    if fast:
        dz, d_mix, g_out, f_rs.two, net = sync(dz, d_mix, g_out, f_rs.two, net)
    net_other = at.swap(net)
    back = recur_back(gain_o, start_state, dz, q, k, v, gate, rows, *second[2:], steps, steps)
    if fast:
        back, state, net_other, dz = sync(back, f_rs.state(), net_other, dz)
        f_rs.take(state)
        f_rs.close(0, 1)
        f_rs.fold(3, 2)

    def give_back(value):
        mine = at.halves(at.relative(value.astype(BF16)), 1)[0]
        return mine.reshape(n_t, piece, dim // 2)

    def settle(came):
        mine, give = at.halves(came[:per_chip], 0)
        return at.in_order(mine, at.swap(give), 2)

    g_gain_o = back[2]
    out_home = give_back(live.astype(F32) * (mid + (net.astype(F32) + net_other.astype(F32))))
    out_came = lax.all_to_all(out_home, "tp", split_axis=0, concat_axis=0, tiled=True)
    back = recur_back(
        gain_o, back[3], dz, q, k, v, gate, rows, *first[2:], 0, steps, tuple(back[0]) + tuple(back[1])
    )
    g_gain_o = g_gain_o + back[2]
    ds, drows = back[:2]
    if fast:
        ds, drows, out_came, state = sync(ds, drows, out_came, f_rs.state())
        f_rs.take(state)
        f_rs.close(3, 2)
        f_rs.merge(2)
        f_rs.home(3)

    dps, g_conv, g_small = {}, {}, {}
    m_rs = Scatter(at, late=True)

    def run_back(h):
        dps[h], g_conv[h], g_small[h], grads = project_back(
            h, normed_one, conv_t, scal, raw[h], rows[h], ds[h], drows[h], g_out[h], m_rs.bit(h)
        )
        m_rs.put(h, grads)

    def moved(group, key):
        return {r: v for r, v in group.items() if r == key}

    if fast:
        run_back(2)
        dps, m_rs.near, m_rs.far, ds = sync(dps, m_rs.near, m_rs.far, ds)
        m_rs.cross(2)
        run_back(1)
        dps, m_rs.near, far, ds, f_state = sync(dps, m_rs.near, moved(m_rs.far, 1), ds, f_rs.state())
        m_rs.far.update(far)
        f_rs.take(f_state)
        f_rs.join(2)
        f_rs.home(1)
        m_rs.cross(1)
        run_back(3)
        dps, m_rs.near, m_rs.far, ds = sync(dps, m_rs.near, m_rs.far, ds)
        m_rs.fold(1, 2)
        m_rs.cross(3)
        run_back(0)
        far = {0: m_rs.far[0]}
        dps, m_rs.near, far, m_rs.two, f_rs.end = sync(dps, m_rs.near, far, m_rs.two, f_rs.end)
        m_rs.far.update(far)
        m_rs.close(1, 2)
        dps, m_rs.one = sync(dps, m_rs.one)
        m_rs.merge(2)
        m_rs.cross(0)
    else:
        for h in range(heads):
            run_back(h)
    output = settle(out_came)
    da, g_gain1 = input_back([dps[h] for h in range(heads)], m_parts, x)
    if fast:
        far = {3: m_rs.far[3]}
        da, g_gain1, far, m_rs.end = sync(da, g_gain1, far, m_rs.end)
        m_rs.far.update(far)
        m_rs.join(2)
        m_rs.home(1)
    da_other = at.swap(da)
    d_x_norm = rms_back(x.astype(F32), gain1, da.astype(F32) + da_other.astype(F32))
    dx_home = give_back(d_mix.astype(F32) + d_x_norm)

    small = [jnp.sum(g_small[h], axis=0) for h in range(heads)]
    conv_all = sum(jnp.where(own[h][:, None, None], g_conv[h][None, :TAPS], 0.0) for h in range(heads)).reshape(-1, HD)
    decay_all = sum(jnp.where(own[h][:, None], small[h][None], 0.0) for h in range(heads))
    gains = jnp.concatenate([at.relative(g_gain1[0]), 0.5 * at.relative(g_gain2[0])]).reshape(-1, HD)
    sums = jnp.concatenate([conv_all, decay_all, gains, g_gain_o], axis=0)
    if fast:
        dx_home, sums, m_rs.near, m_rs.end = sync(dx_home, sums, m_rs.near, m_rs.end)
        m_rs.fold(3)
        m_rs.close(3)
        m_rs.home(3)
        m_rs.fold(0)
        sums = at.chip_sum(at.line_sum(sums))
    else:
        sums = at.all_sum(sums)
    dx_came = lax.all_to_all(dx_home, "tp", split_axis=0, concat_axis=0, tiled=True)
    if fast:
        dx_came, m_rs.two, m_rs.end = sync(dx_came, m_rs.two, m_rs.end)
        m_rs.close(0)
    input_grad = settle(dx_came)
    n_conv = conv_all.shape[0]
    g_conv_all = jnp.transpose(sums[:n_conv].reshape(heads_all, TAPS, -1), (0, 2, 1))
    decay_sum = sums[n_conv : n_conv + heads_all]
    gain_sum = sums[n_conv + heads_all : -1].reshape(2, dim)

    def to_core(value, joined):
        mine, give = at.halves(value.astype(BF16), value.ndim - 1)
        return at.in_order(mine, at.swap(give), joined).astype(F32)

    if not fast:
        f_rs.rest()
    f_total = f_rs.total()
    g_ffn = to_core(f_total.reshape(3, -1, f_total.shape[1]), 1)
    grad_gate_up = jnp.transpose(g_ffn[:2], (2, 0, 1))
    grad_down = g_ffn[2]
    if by_turn:
        if not fast:
            m_rs.rest()
        joined = to_core(m_rs.total()[None], 0)
    else:
        joined = []
        for h in range(heads):
            have = {}
            for stack, group in zip((m_rs.near[h], m_rs.far[h]), sides(chips, m_rs.bit(h))):
                have.update({p: stack[i] for i, p in enumerate(group)})
            joined.append(jnp.concatenate([have[p] for p in range(chips)], axis=1))
        joined = jnp.stack(joined)
        spread = jnp.zeros((heads_all,) + joined.shape[1:], BF16)
        spread = lax.dynamic_update_slice_in_dim(spread, at.relative(joined), at.core * heads, 0)
        spread = lax.psum_scatter(spread, "tp", scatter_dimension=0, tiled=True)
        joined = lax.psum_scatter(spread, "fsdp", scatter_dimension=2, tiled=True).astype(F32)
    grad_in = jnp.transpose(joined[:, HD : HD + cols], (2, 0, 1))
    grad_out = joined[:, :HD].reshape(local_heads * HD, -1)
    return (
        output, input_grad, gain_sum[0], grad_in, g_conv_all, decay_sum[:, 0], decay_sum[:, 1], sums[-1], grad_out,
        gain_sum[1], grad_gate_up, grad_down
    )


def solution(mesh):
    tokens = P("fsdp", "tp", None)
    rows = P("tp", "fsdp")
    split = P("fsdp", None, "tp")
    return jax.shard_map(
        local,
        mesh=mesh,
        in_specs=(tokens, P(), P(), tokens, P(), tokens, P(), P(), P(), P(), rows, P(), split, rows),
        out_specs=(tokens, tokens, P(), tokens, P(), P(), P(), P(), rows, P(), split, rows),
        check_vma=False,
    )
```
